256 devices in a mesh: ang: 32 (over x, y, z_lo), slab: 8 (over z_hi, core).
Axes of the slice: x: 4, y: 4, z: 8 (z_hi: 4, z_lo: 2; z = z_hi * 2 + z_lo), core: 2. Of those that a mesh axis runs over, the one named last changes fastest.
Arguments:
- start_volume: float32 [48, 24, 2048], P('slab'), may hold values from -6 to 6
- measured: float32 [64, 48, 2048], P('ang', 'slab'), may hold values from -6 to 6
- row_shift: int32 [64, 48], P('ang'), may hold values from 0 to 24, as said below
- col_shift: int32 [64, 48], P('ang'), may hold values from -16 to 16, as said below
- col_frac: float32 [64, 48], P('ang'), may hold values from 0 to 1
Outputs:
- new_volume: float32 [48, 24, 2048], P('slab')
- new_residual: float32 [64, 48, 2048], P('ang', 'slab')
- new_direction: float32 [48, 24, 2048], P('slab')
The draws below stay inside these ranges and needn't reach their ends.
Inputs may be any that keep to these rules, and one draw needn't show every extreme that they name: For each angle, row_shift is monotone over the slices, starts or ends at 0, and some angle spans the whole range. For each angle, col_shift is monotone over the slices; some angle reaches both ends.
All inputs are finite; a program needn't handle non-finite values.
Results may differ from the reference program's by a relative error of at most 0.003.
Values sent between devices are 32-bit elements; how exact they have to be, the bound alone decides.
A program may use at most 192 MiB of HBM per device.

```python
import jax
import jax.numpy as jnp
from jax import lax

X = 2048
Y = 24
CMAX = 16
Z = 48
A = 64
R = 48


def draw_row_shift(key, part):
    key = jax.random.fold_in(key, 11)
    key_slope, key_sign, key_pick = jax.random.split(key, 3)
    spread = R - Y
    slope = jax.random.randint(key_slope, (A,), 0, spread + 1)
    chosen = jax.random.randint(key_pick, (), 0, A)
    slope = jnp.where(jnp.arange(A) == chosen, spread, slope)
    rising = jax.random.randint(key_sign, (A,), 0, 2)
    depth = jnp.arange(Z)[None, :]
    climb = depth * slope[:, None] // (Z - 1)
    return jnp.where(rising[:, None] == 1, climb, slope[:, None] - climb).astype(jnp.int32)


def draw_col_shift(key, part):
    key = jax.random.fold_in(key, 23)
    key_slope, key_pick = jax.random.split(key, 2)
    slope = jax.random.randint(key_slope, (A,), -CMAX, CMAX + 1)
    chosen = jax.random.randint(key_pick, (), 0, A)
    slope = jnp.where(jnp.arange(A) == chosen, CMAX, slope)
    depth = jnp.arange(Z)[None, :]
    return (slope[:, None] * (2 * depth - (Z - 1)) // (Z - 1)).astype(jnp.int32)


def block_levels(stream_key, extent, cuts, least, high):
    loudness = 1.0
    for dim, shards_of in cuts:
        steps = jax.random.uniform(jax.random.fold_in(jax.random.fold_in(stream_key, 6), dim), (shards_of,), jnp.float32, least / len(cuts), high / len(cuts))
        loudness = loudness * jnp.repeat(jnp.exp(steps), extent[dim] // shards_of).reshape((-1,) + (1,) * (len(extent) - 1 - dim))
    return loudness


def noise(rng, extent, scale, reach, cuts=(), dtype=jnp.bfloat16):
    drawn = scale * jax.random.normal(rng, extent, jnp.float32)
    if cuts:
        drawn = drawn * block_levels(rng, extent, cuts, -0.22, 0.18)
    return jnp.clip(drawn, -reach, reach).astype(dtype)


def setup_inputs(seed: int = 0) -> dict:
    key_list = jax.random.split(jax.random.key(seed), 6)
    start_volume = noise(key_list[0], (Z, Y, X), 1.0, 6.0, ((0, 8),), jnp.float32)
    measured = noise(key_list[1], (A, R, X), 1.0, 6.0, ((0, 32), (1, 8)), jnp.float32)
    row_shift = draw_row_shift(jax.random.fold_in(key_list[5], 71), 0)
    col_shift = draw_col_shift(jax.random.fold_in(key_list[5], 71), 0)
    col_frac = jnp.clip(1.0 * jax.random.uniform(key_list[4], (A, Z), jnp.float32) ** block_levels(key_list[4], (A, Z), ((0, 32),), -0.2, 0.2), 0.0, 1.0)
    return {"start_volume": start_volume, "measured": measured, "row_shift": row_shift, "col_shift": col_shift, "col_frac": col_frac}


def project(volume, shifts, columns, fracs, row0, nrows, margin):
    count, lines, width = volume.shape
    pcols = CMAX + 1
    padded = jnp.pad(volume, ((0, 0), (margin, margin), (pcols, pcols)))

    def step(total, item):
        plane, drow, dcol, dfrac = item

        def single(shift, colv, fracv):
            left = lax.dynamic_slice(plane, (margin + row0 - shift, pcols - colv - 1), (nrows, width + 1))
            return (1.0 - fracv) * left[:, 1:] + fracv * left[:, :-1]

        return total + jax.vmap(single)(drow, dcol, dfrac), None

    init = jnp.zeros((shifts.shape[0], nrows, width), jnp.float32)
    total, unused = lax.scan(step, init, (padded, shifts.T, columns.T, fracs.T))
    return total


def backproject(rows, shifts, columns, fracs, row0, lines, margin):
    angles, nrows, width = rows.shape
    pcols = CMAX + 1
    padded = jnp.pad(rows, ((0, 0), (margin, margin), (pcols, pcols)))

    def step(total, item):
        plane, drow, dcol, dfrac = item

        def single(shift, colv, fracv):
            right = lax.dynamic_slice(plane, (margin + shift - row0, pcols + colv), (lines, width + 1))
            return (1.0 - fracv) * right[:, :-1] + fracv * right[:, 1:]

        return total + jax.vmap(single)(drow, dcol, dfrac), None

    init = jnp.zeros((shifts.shape[1], lines, width), jnp.float32)
    total, unused = lax.scan(step, init, (padded, shifts, columns, fracs))
    return total


def reference(start_volume, measured, row_shift, col_shift, col_frac):
    nrows = measured.shape[1]
    lines = start_volume.shape[1]
    residual = measured - project(start_volume, row_shift, col_shift, col_frac, 0, nrows, nrows)
    gradient = backproject(residual, row_shift, col_shift, col_frac, 0, lines, nrows)
    gamma = jnp.sum(gradient * gradient)
    direction = gradient
    image = project(direction, row_shift, col_shift, col_frac, 0, nrows, nrows)
    alpha = gamma / jnp.sum(image * image)
    new_volume = start_volume + alpha * direction
    new_residual = residual - alpha * image
    new_gradient = backproject(new_residual, row_shift, col_shift, col_frac, 0, lines, nrows)
    new_gamma = jnp.sum(new_gradient * new_gradient)
    new_direction = new_gradient + (new_gamma / gamma) * direction
    return new_volume, new_residual, new_direction
```

```python
import jax
import jax.numpy as jnp
from jax import lax
from jax.experimental import pallas as pl
from jax.experimental.pallas import tpu as pltpu
from jax.sharding import PartitionSpec as P

MESH = pl.DeviceIdType.MESH
F32 = jnp.float32
PIECES = 16
SLICES = 3
LINES = 24
ROWS = 48
ANGLES = 4
LANES = 128
X = 2048


def rcopy(src, dst, send, recv, dev):
    return pltpu.make_async_remote_copy(
        src_ref=src, dst_ref=dst, send_sem=send, recv_sem=recv, device_id=dev, device_id_type=MESH
    )


def lanes_of(shape):
    return lax.broadcasted_iota(jnp.int32, shape, len(shape) - 1)


def kernel(
    x_hbm, m_hbm, rt_ref, ct_ref, ft_ref,
    vol_out, res_out, dir_out,
    xv, dirv, gslab, qslab, m_ref, msh, mbuf, rtv, ctv, ftv, rts, cts, fts,
    xbuf, xhalo, gbuf, ghalo, packed, pad, img, wide, diff,
    part, rs1, sum1, rs2, own, qpart, qrs1, qsum1, qland,
    rblk, iblk, rres, ires, tiles, sc1, sc2, sc3,
    loc_sem, tab_send, tab_recv, m_send, m_recv, x_send,
    ag_send, ag_recv, hl_send, hl_recv,
    rs_send, rs_recv, rt_send, rt_recv, own_send, own_recv,
    sl_send, sl_recv, blk_send, blk_recv, sc_send, sc_recv, out_sem,
):
    ang = lax.axis_index("ang")
    slab = lax.axis_index("slab")
    p = lax.div(ang, 2)
    zlo = lax.rem(ang, 2)
    px = lax.div(p, 4)
    py = lax.rem(p, 4)
    zhi = lax.div(slab, 2)
    core = lax.rem(slab, 2)
    z = 2 * zhi + zlo
    c = 2 * z + core
    even = core == 0
    u = jnp.where(even, px, py)
    w = jnp.where(even, py, px)

    def pid(a, b):
        return jnp.where(even, 4 * a + b, 4 * b + a)

    def plane_dev(q):
        return (2 * q + zlo, slab)

    def col_dev(k):
        zz = lax.div(k, 2)
        return (2 * p + lax.rem(zz, 2), 2 * lax.div(zz, 2) + lax.rem(k, 2))

    def turn(v, d, n):
        return lax.rem(v + d, n)

    lane = lanes_of((LINES, LANES))
    lane_r = lanes_of((ROWS, LANES))
    me_dev = (ang, slab)

    def xy(a, b):
        return jnp.where(even, a, b), jnp.where(even, b, a)

    def is_me(dev):
        return jnp.logical_and(dev[0] == ang, dev[1] == slab)

    def apart(dev, then, here):
        pl.when(jnp.logical_not(is_me(dev)))(then)
        pl.when(is_me(dev))(here)

    def owner_dev(xx, yy):
        return (2 * (4 * zhi + 2 * core + lax.rem(yy, 2)) + zlo, 2 * xx + lax.div(yy, 2))

    partner = (2 * p + (1 - zlo), slab)
    yhi = lax.div(py, 2)
    ylo = lax.rem(py, 2)

    mload = pltpu.make_async_copy(m_hbm, m_ref, loc_sem.at[0])
    mload.start()
    tables = ((rt_ref, rtv, rts), (ct_ref, ctv, cts), (ft_ref, ftv, fts))

    def table_copy(n):
        return pltpu.make_async_copy(tables[n][0], tables[n][1].at[zlo], loc_sem.at[4 + n])

    for n in range(3):
        table_copy(n).start()
    xload = pltpu.make_async_copy(x_hbm, xv, loc_sem.at[1])
    xload.start()

    barrier = pltpu.get_barrier_semaphore()

    def greet(dev):
        pl.semaphore_signal(barrier, inc=1, device_id=dev, device_id_type=MESH)

    @pl.loop(1, PIECES)
    def _(d):
        greet(col_dev(turn(c, d, PIECES)))

    for d in range(1, 4):
        greet(plane_dev(pid(turn(u, d, 4), w)))
        greet(plane_dev(pid(u, turn(w, d, 4))))
    for a in range(4):
        greet((2 * pid(a, w) + 1 - zlo, slab))
    mine = 0
    for a in range(4):
        to = owner_dev(*xy(a, w))
        pl.when(jnp.logical_not(is_me(to)))(lambda to=to: greet(to))
        mine = mine + jnp.where(is_me(to), 1, 0)
        at_x, at_y = zhi, 2 * core + ylo
        come = (2 * jnp.where(yhi == 0, 4 * a + at_y, 4 * at_x + a) + zlo, 2 * px + yhi)
        pl.when(jnp.logical_not(is_me(come)))(lambda come=come: greet(come))

    lane6 = lanes_of((6, LANES))
    mload.wait()
    for a in range(2):
        prev = jnp.zeros((6, LANES), F32)
        for t in range(17):
            cur = jnp.zeros((6, LANES), F32)
            if t < 16:
                cur = pltpu.roll(m_ref[:, a, pl.ds(LANES * t, LANES)], 64, 1)
            msh[a, :, pl.ds(LANES * t, LANES)] = jnp.where(lane6 < 64, prev, cur)
            prev = cur

    pad[...] = jnp.zeros_like(pad)
    img[...] = jnp.zeros_like(img)
    pl.semaphore_wait(barrier, 15 + 6 + 4 + 8 - 2 * mine)

    def x_each(act_far, act_here):
        for to in range(4):
            for h in range(3):
                cc = 4 * to + 2 * zlo + (1 if h < 2 else 0)
                half = h if h < 2 else ylo
                k = 4 * zhi + 2 * core + half
                src = x_hbm.at[pl.ds(3 * half, SLICES), :, pl.ds(pl.multiple_of(LANES * cc, LANES), LANES)]
                copy = rcopy(src, xbuf.at[k], x_send.at[to, h], ag_recv.at[0, k], col_dev(cc))
                local = pltpu.make_async_copy(src, xbuf.at[k], ag_recv.at[0, k])

                def act(copy=copy, local=local, cc=cc):
                    apart(col_dev(cc), lambda: act_far(copy), lambda: act_here(local))

                if h < 2:
                    pl.when(lax.rem(zhi, 2) == lax.rem(px, 2))(act)
                else:
                    act()

    x_each(lambda copy: copy.start(), lambda copy: copy.start())

    tabs = []
    for n, (src, dst, _) in enumerate(tables):
        t = rcopy(src, dst.at[zlo], tab_send.at[n], tab_recv.at[n], partner)
        t.start()
        tabs.append(t)

    def m_window(k):
        return msh.at[:, :, pl.ds(pl.multiple_of(LANES * k, LANES), 2 * LANES)]

    def m_copy(d):
        k = turn(c, d, PIECES)
        return rcopy(m_window(k), mbuf.at[c], m_send.at[d], m_recv.at[c], col_dev(k))

    @pl.loop(1, PIECES)
    def _(d):
        m_copy(d).start()

    mbuf[c] = msh[:, :, pl.ds(pl.multiple_of(LANES * c, LANES), 2 * LANES)]

    def step(q):
        return jnp.where(q < 2, q, 5 - q)

    def piece_order(t):
        late = t - 9
        dx = jnp.where(t < 9, step(lax.rem(t, 3)), jnp.where(late < 4, 2, step(late - 4)))
        dy = jnp.where(t < 9, step(lax.div(t, 3)), jnp.where(late < 4, step(late), 2))
        return 4 * turn(px, 4 - dx, 4) + turn(py, 4 - dy, 4)

    def gather_send1(buf, n):
        for d in range(1, 4):
            rcopy(buf.at[p], buf.at[p], ag_send.at[n, d - 1], ag_recv.at[n, p],
                  plane_dev(pid(turn(u, d, 4), w))).start()

    def gather_copy2(buf, n, da, d):
        k = pid(turn(u, 4 - da, 4), w)
        return rcopy(buf.at[k], buf.at[k], ag_send.at[n, 3 + 3 * da + d - 1], ag_recv.at[n, k],
                     plane_dev(pid(u, turn(w, d, 4))))

    def halo_copy(halo, n, k, side):
        to = turn(c, 1 if side == 0 else PIECES - 1, PIECES)
        return rcopy(packed.at[n, k, side], halo.at[k, side], hl_send.at[n, side, k], hl_recv.at[n, side, k], col_dev(to))

    def halo_start(buf, halo, n, k):
        for side in range(2):
            shift = 42 if side == 0 else 0
            v = [pltpu.roll(buf[k, i], shift + 42 * i, 1) if shift + i else buf[k, i] for i in range(SLICES)]
            packed[n, k, side] = jnp.where(lane < 42, v[0], jnp.where(lane < 84, v[1], v[2]))
            halo_copy(halo, n, k, side).start()

    def gather_wait(buf, n, k):
        rcopy(buf.at[k], buf.at[k], ag_send.at[n, 0], ag_recv.at[n, k], partner).wait_recv()

    def project_piece(buf, halo, k):
        for s in range(SLICES):
            mid = pltpu.roll(buf[k, s], 64, 1)
            left = jnp.where(c > 0, pltpu.roll(halo[k, 0], (150 - 42 * s) % LANES, 1), 0.0)
            right = jnp.where(c < PIECES - 1, pltpu.roll(halo[k, 1], (192 - 42 * s) % LANES, 1), 0.0)
            w0 = jnp.where(lane < 64, left, mid)
            w1 = jnp.where(lane < 64, mid, right)
            s0 = pltpu.roll(w0, 1, 1)
            s1 = pltpu.roll(w1, 1, 1)
            d0 = jnp.where(lane < 1, s1, s0) - w0
            d1 = jnp.where(lane < 1, s0, s1) - w1
            at = SLICES * k + s
            for a in range(ANGLES):
                f = fts[a // 2, a % 2, at]
                cs = cts[a // 2, a % 2, at]
                v0 = w0 + f * d0
                v1 = w1 + f * d1
                other = jnp.logical_or(lane >= LANES - cs, lane < -cs)
                sh = lax.rem(cs + LANES, LANES)
                pad[SLICES * a + s, 0, pl.ds(LINES, LINES), :] = pltpu.roll(jnp.where(other, v1, v0), sh, 1)
                pad[SLICES * a + s, 1, pl.ds(LINES, LINES), :] = pltpu.roll(jnp.where(other, v0, v1), sh, 1)
        for a in range(ANGLES):
            for t in range(2):
                acc = img[a, t]
                for s in range(SLICES):
                    rs = rts[a // 2, a % 2, SLICES * k + s]
                    acc = acc + pad[SLICES * a + s, t, pl.ds(LINES - rs, ROWS), :]
                img[a, t] = acc

    def gather_project(buf, halo, n):
        for da in (0, 1, 3, 2):
            k = pid(turn(u, 4 - da, 4), w)
            if n == 0 or da:
                gather_wait(buf, n, k)
            for d in (2, 1, 3) if n else (1, 3):
                gather_copy2(buf, n, da, d).start()
            halo_start(buf, halo, n, k)

        @pl.loop(0, 8)
        def _(t):
            k = pid(turn(u, 4 - step(lax.div(t, 2)), 4), turn(w, 3 - 2 * lax.rem(t, 2), 4))
            gather_wait(buf, n, k)
            halo_start(buf, halo, n, k)

        @pl.loop(0, PIECES)
        def _(t):
            @pl.when(jnp.logical_and(t >= 4, t < 8))
            def _():
                k = pid(turn(u, 4 - step(t - 4), 4), turn(w, 2, 4))
                gather_wait(buf, n, k)
                halo_start(buf, halo, n, k)

            k = piece_order(t)
            for side in range(2):
                halo_copy(halo, n, k, side).wait_recv()
            project_piece(buf, halo, k)

    def col_mask(t, ln):
        if t == 0:
            return jnp.logical_or(ln >= 64, c > 0)
        return jnp.logical_or(ln < 64, c < PIECES - 1)

    def own_tile(v0, v1, ln):
        return pltpu.roll(jnp.where(ln >= 64, v0, v1), 64, 1)

    def make_diff():
        for a in range(ANGLES):
            v0 = wide[a, 0]
            v1 = wide[a, 1]
            s0 = pltpu.roll(v0, LANES - 1, 1)
            s1 = pltpu.roll(v1, LANES - 1, 1)
            diff[a, 0] = jnp.where(lane_r == LANES - 1, s1, s0) - v0
            diff[a, 1] = jnp.where(lane_r == LANES - 1, s0, s1) - v1

    def back_piece(dst, k):
        for s in range(SLICES):
            at = SLICES * k + s
            acc = None
            for a in range(ANGLES):
                rs = rts[a // 2, a % 2, at]
                cs = cts[a // 2, a % 2, at]
                f = fts[a // 2, a % 2, at]
                first = lane >= 64 + cs
                v = jnp.where(first, wide[a, 0, pl.ds(rs, LINES), :], wide[a, 1, pl.ds(rs, LINES), :])
                e = jnp.where(first, diff[a, 0, pl.ds(rs, LINES), :], diff[a, 1, pl.ds(rs, LINES), :])
                term = pltpu.roll(v + f * e, 64 - cs, 1)
                acc = term if acc is None else acc + term
            dst[k, s] = acc

    def scatter_copy1(src, land, n, d, a):
        return rcopy(src.at[pid(a, turn(w, d, 4))], land.at[d - 1, a], rs_send.at[n, 4 * (d - 1) + a],
                     rs_recv.at[n, 4 * (d - 1) + a], plane_dev(pid(u, turn(w, d, 4))))

    def scatter_copy2(src, dst, n, d):
        a = turn(u, d, 4)
        return rcopy(src.at[a], dst.at[d - 1], rt_send.at[n, d - 1], rt_recv.at[n, d - 1], plane_dev(pid(a, w)))

    def back_scatter(dst, land, n, first):
        @pl.loop(0, PIECES)
        def _(t):
            i = lax.rem(t, 3)
            d = jnp.where(t >= 12, 0, jnp.where(i == 0, 2, 2 * i - 1))
            a = turn(first, jnp.where(t >= 12, t - 12, lax.div(t, 3)), 4)
            back_piece(dst, pid(a, turn(w, d, 4)))

            @pl.when(t < 12)
            def _():
                scatter_copy1(dst, land, n, d, a).start()

    def line_sum(dst, land, n, a):
        total = dst[pid(a, w)]
        for d in (1, 3, 2):
            scatter_copy1(dst, land, n, d, a).wait_recv()
            total = total + land[d - 1, a]
        return total

    def plane_sum(dst, land, total1, land2, n):
        for da in (1, 2, 3, 0):
            a = turn(u, da, 4)
            total1[a] = line_sum(dst, land, n, a)
            if da:
                scatter_copy2(total1, land2, n, da).start()
        total = total1[u]
        for d in (1, 3, 2):
            scatter_copy2(total1, land2, n, d).wait_recv()
            total = total + land2[d - 1]
        return total

    def owner_copy(a, total1, land):
        return rcopy(total1.at[a], land.at[u], own_send.at[a], own_recv.at[u], owner_dev(*xy(a, w)))

    def owner_start(dst, land1, total1, land, n):
        for a in range(4):
            total1[a] = line_sum(dst, land1, n, a)
            copy = owner_copy(a, total1, land)
            local = pltpu.make_async_copy(total1.at[a], land.at[u], own_recv.at[u])
            apart(owner_dev(*xy(a, w)), lambda: copy.start(), lambda: local.start())

    def owner_sum(total1, land):
        total = None
        for a in range(4):
            rcopy(total1.at[0], land.at[a], own_send.at[0], own_recv.at[a], partner).wait_recv()
            total = land[a] if total is None else total + land[a]
        return total

    def owner_finish(total1, land):
        for a in range(4):
            copy = owner_copy(a, total1, land)
            pl.when(jnp.logical_not(is_me(owner_dev(*xy(a, w)))))(lambda: copy.wait_send())

    def slab_at(buf, h, block):
        return buf.at[pl.ds(3 * h, SLICES), :, pl.ds(pl.multiple_of(LANES * block, LANES), LANES)]

    def slab_piece(buf, xx, yy, lo):
        return slab_at(buf, lax.rem(yy, 2), 4 * xx + 2 * lo + lax.div(yy, 2))

    def slab_copy(buf, n, a, b, lo, slot, dev):
        xx, yy = xy(a, b)
        ref = slab_piece(buf, xx, yy, lo)
        return rcopy(ref, ref, sl_send.at[n, slot], sl_recv.at[n, 2 * (4 * xx + yy) + lo], dev)

    def second_dev(d):
        return plane_dev(pid(u, turn(w, d, 4)))

    def slab_wait(buf, n, a, b, lo):
        slab_copy(buf, n, a, b, lo, 0, partner).wait_recv()

    def swap_copy(src, buf, n):
        return rcopy(src, slab_at(buf, ylo, c), sl_send.at[n, 31],
                     sl_recv.at[n, 2 * (4 * zhi + 2 * core + ylo) + zlo], owner_dev(px, py))

    def swap_start(src, buf, n):
        local = pltpu.make_async_copy(src, slab_at(buf, ylo, c), sl_recv.at[n, 2 * (4 * zhi + 2 * core + ylo) + zlo])
        apart(owner_dev(px, py), lambda: swap_copy(src, buf, n).start(), lambda: local.start())

    def slab_near(buf, n, a, lo, slot):
        slab_copy(buf, n, a, w, lo, slot, second_dev(1)).start()
        slab_copy(buf, n, a, w, lo, slot + 1, second_dev(3)).start()

    def slab_first(buf, n):
        for i, d in enumerate((2, 1, 3)):
            slab_copy(buf, n, u, w, zlo, i, plane_dev(pid(turn(u, d, 4), w))).start()
        slab_near(buf, n, u, zlo, 7)
        for i, d in enumerate((2, 1, 3, 0)):
            slab_copy(buf, n, u, w, zlo, 3 + i, (2 * pid(turn(u, d, 4), w) + 1 - zlo, slab)).start()

    def slab_second(buf, n):
        for i, d in enumerate((1, 3, 2)):
            a = turn(u, d, 4)
            slab_wait(buf, n, a, w, zlo)
            slab_near(buf, n, a, zlo, 9 + 2 * i)
        for i, d in enumerate((0, 1, 3, 2)):
            a = turn(u, d, 4)
            slab_wait(buf, n, a, w, 1 - zlo)
            slab_near(buf, n, a, 1 - zlo, 15 + 2 * i)

    def slab_third(buf, n):
        for i, d in enumerate((0, 1, 3, 2)):
            a = turn(u, d, 4)
            slab_wait(buf, n, a, turn(w, 3, 4), 0)
            slab_copy(buf, n, a, turn(w, 3, 4), 0, 23 + 2 * i, second_dev(1)).start()
            slab_wait(buf, n, a, turn(w, 1, 4), 1)
            slab_copy(buf, n, a, turn(w, 1, 4), 1, 24 + 2 * i, second_dev(3)).start()

    def slab_rest(buf, n):
        for lo in range(2):
            for d in (3 if lo else 1, 2):
                @pl.loop(0, 4)
                def _(a):
                    slab_wait(buf, n, a, turn(w, d, 4), lo)

    def slab_finish(buf, n):
        @pl.loop(0, 31)
        def _(t):
            slab_copy(buf, n, u, w, zlo, t, partner).wait_send()

    def blk_copy(src, dst, n, d):
        k = turn(c, d, PIECES)
        return rcopy(src.at[k], dst.at[:, :, pl.ds(pl.multiple_of(LANES * c, LANES), LANES)], blk_send.at[n, d],
                     blk_recv.at[n, c], col_dev(k))

    def blk_send_all(src, dst, n):
        @pl.loop(1, PIECES)
        def _(d):
            blk_copy(src, dst, n, d).start()

        dst[:, :, pl.ds(pl.multiple_of(LANES * c, LANES), LANES)] = src[c]

    def blk_finish(src, dst, n):
        @pl.loop(1, PIECES)
        def _(d):
            k = turn(c, d, PIECES)
            rcopy(src.at[0], dst.at[:, :, pl.ds(pl.multiple_of(LANES * k, LANES), LANES)], blk_send.at[n, d],
                  blk_recv.at[n, k], partner).wait_recv()
            blk_copy(src, dst, n, d).wait_send()

    def gather_finish(buf, halo, n):
        if n:
            for d in range(1, 4):
                rcopy(buf.at[0], buf.at[0], ag_send.at[n, d - 1], ag_recv.at[n, 0], partner).wait_send()
        for da in range(4):
            for d in (1, 2, 3) if n else (1, 3):
                gather_copy2(buf, n, da, d).wait_send()

        @pl.loop(0, PIECES)
        def _(t):
            for side in range(2):
                halo_copy(halo, n, t, side).wait_send()

    def scatter_finish(src, land1, n):
        @pl.loop(0, 12)
        def _(t):
            rcopy(src.at[0], land1.at[0, 0], rs_send.at[n, t], rs_recv.at[n, 0], partner).wait_send()

    def smem_copy(n):
        return pltpu.make_async_copy(tables[n][1], tables[n][2], loc_sem.at[4 + n])

    for n in range(3):
        table_copy(n).wait()
        tabs[n].wait()
        smem_copy(n).start()
    for n in range(3):
        smem_copy(n).wait()

    gather_project(xbuf, xhalo, 0)

    @pl.loop(1, PIECES)
    def _(d):
        k = turn(c, d, PIECES)
        rcopy(m_window(0), mbuf.at[k], m_send.at[d], m_recv.at[k], partner).wait_recv()

    for k in range(PIECES):
        rows = pl.ds(6 * (2 * (k // 4) + k % 2), 6)
        for e in range(2):
            a = 2 * ((k // 2) % 2) + e
            v0 = jnp.where(col_mask(0, lane6), mbuf[k, e, :, :LANES] - img[a, 0, rows, :], 0.0)
            v1 = jnp.where(col_mask(1, lane6), mbuf[k, e, :, LANES:] - img[a, 1, rows, :], 0.0)
            wide[a, 0, rows, :] = v0
            wide[a, 1, rows, :] = v1
            rblk[k, e] = own_tile(v0, v1, lane6)
    make_diff()

    back_scatter(part, rs1, 0, turn(u, 1, 4))
    blk_send_all(rblk, rres, 0)
    own[...] = plane_sum(part, rs1, sum1, rs2, 0)
    gbuf[p] = own[...]
    gather_send1(gbuf, 1)
    swap_start(own, gslab, 0)
    img[...] = jnp.zeros_like(img)
    gather_project(gbuf, ghalo, 1)
    slab_wait(gslab, 0, u, w, zlo)
    slab_first(gslab, 0)

    norm = jnp.zeros((ROWS, LANES), F32)
    for a in range(ANGLES):
        v0 = jnp.where(col_mask(0, lane_r), img[a, 0], 0.0)
        v1 = jnp.where(col_mask(1, lane_r), img[a, 1], 0.0)
        wide[a, 0] = v0
        wide[a, 1] = v1
        mine = jnp.where(lane_r >= 64, v0, v1)
        norm = norm + mine * mine
    make_diff()
    back_scatter(qpart, qrs1, 1, 0)
    slab_second(gslab, 0)
    owner_start(qpart, qrs1, qsum1, qland, 1)
    for k in range(PIECES):
        rows = pl.ds(6 * (2 * (k // 4) + k % 2), 6)
        for e in range(2):
            a = 2 * ((k // 2) % 2) + e
            iblk[k, e] = own_tile(wide[a, 0, rows, :], wide[a, 1, rows, :], lane6)
    q = owner_sum(qsum1, qland)
    qslab[pl.ds(3 * ylo, SLICES), :, pl.ds(pl.multiple_of(LANES * (4 * px + 2 * zlo + yhi), LANES), LANES)] = q
    slab_first(qslab, 1)

    tiles[...] = jnp.zeros_like(tiles)

    def down(v):
        return jnp.sum(v, axis=0, keepdims=True)

    g = own[...]
    tiles[0, 0:1, :] = down(jnp.sum(g * g, axis=0))
    tiles[0, 1:2, :] = down(norm)
    tiles[0, 2:3, :] = down(jnp.sum(q * q, axis=0))

    def sum_copy(land, n, d):
        at, dev = (
            (c, col_dev(turn(c, d, PIECES))),
            (px, plane_dev(4 * turn(px, d, 4) + py)),
            (py, plane_dev(4 * px + turn(py, d, 4))),
        )[n]
        return rcopy(tiles.at[n], land.at[at], sc_send.at[n, d], sc_recv.at[n, at], dev)

    def sum_start(land, n):
        @pl.loop(1, PIECES if n == 0 else 4)
        def _(d):
            sum_copy(land, n, d).start()

        land[(c, px, py)[n]] = tiles[n]

    def sum_finish(land, n):
        count = PIECES if n == 0 else 4

        @pl.loop(1, count)
        def _(d):
            k = turn((c, px, py)[n], d, count)
            rcopy(tiles.at[n], land.at[k], sc_send.at[n, d], sc_recv.at[n, k], partner).wait_recv()
            sum_copy(land, n, d).wait_send()

        total = land[0]
        for k in range(1, count):
            total = total + land[k]
        return total

    sum_start(sc1, 0)
    blk_send_all(iblk, ires, 1)
    slab_third(gslab, 0)
    slab_second(qslab, 1)
    tiles[1] = sum_finish(sc1, 0)
    sum_start(sc2, 1)
    slab_third(qslab, 1)
    tiles[2] = sum_finish(sc2, 1)
    sum_start(sc3, 2)
    slab_rest(gslab, 0)
    sums = jnp.sum(sum_finish(sc3, 2), axis=1, keepdims=True)
    gamma = sums[0:1]
    alpha = gamma / sums[1:2]
    scale = alpha * alpha * (sums[2:3] / gamma)

    blk_finish(rblk, rres, 0)
    blk_finish(iblk, ires, 1)
    for e in range(2):
        res_out[:, e, :] = rres[e] - alpha * ires[e]
    xload.wait()

    def out_copy(src, dst, n, i):
        return pltpu.make_async_copy(src.at[i], dst.at[i], out_sem.at[n, i])

    for i in range(6):
        xv[i] = xv[i] + alpha * gslab[i]
        out_copy(xv, vol_out, 0, i).start()
    slab_rest(qslab, 1)
    for i in range(6):
        dirv[i] = scale * gslab[i] - alpha * qslab[i]
        out_copy(dirv, dir_out, 1, i).start()

    @pl.loop(1, PIECES)
    def _(d):
        m_copy(d).wait_send()

    gather_finish(xbuf, xhalo, 0)
    gather_finish(gbuf, ghalo, 1)
    scatter_finish(part, rs1, 0)
    scatter_finish(qpart, qrs1, 1)
    for d in range(1, 4):
        scatter_copy2(sum1, rs2, 0, d).wait_send()
    owner_finish(qsum1, qland)
    slab_finish(gslab, 0)
    slab_finish(qslab, 1)
    pl.when(jnp.logical_not(is_me(owner_dev(px, py))))(lambda: swap_copy(own, gslab, 0).wait_send())
    x_each(lambda copy: copy.wait_send(), lambda copy: None)
    for i in range(6):
        out_copy(xv, vol_out, 0, i).wait()
        out_copy(dirv, dir_out, 1, i).wait()


def per_device(start_volume, measured, row_shift, col_shift, col_frac):
    piece = (SLICES, LINES, LANES)
    vmem = pltpu.VMEM
    dma = pltpu.SemaphoreType.DMA
    scratch = [
        vmem(start_volume.shape, F32), vmem(start_volume.shape, F32), vmem(start_volume.shape, F32), vmem(start_volume.shape, F32),
        vmem((6, 2, X), F32),
        vmem((2, 6, 17 * LANES), F32),
        vmem((PIECES, 2, 6, 2 * LANES), F32),
        vmem((2, 2, 48), jnp.int32), vmem((2, 2, 48), jnp.int32), vmem((2, 2, 48), F32),
        pltpu.SMEM((2, 2, 48), jnp.int32), pltpu.SMEM((2, 2, 48), jnp.int32), pltpu.SMEM((2, 2, 48), F32),
        vmem((PIECES,) + piece, F32), vmem((PIECES, 2, LINES, LANES), F32),
        vmem((PIECES,) + piece, F32), vmem((PIECES, 2, LINES, LANES), F32),
        vmem((2, PIECES, 2, LINES, LANES), F32),
        vmem((ANGLES * SLICES, 2, 3 * LINES, LANES), F32),
        vmem((ANGLES, 2, ROWS, LANES), F32),
        vmem((ANGLES, 2, ROWS, LANES), F32),
        vmem((ANGLES, 2, ROWS, LANES), F32),
        vmem((PIECES,) + piece, F32), vmem((3, 4) + piece, F32), vmem((4,) + piece, F32), vmem((3,) + piece, F32), vmem(piece, F32),
        vmem((PIECES,) + piece, F32), vmem((3, 4) + piece, F32), vmem((4,) + piece, F32), vmem((4,) + piece, F32),
        vmem((PIECES, 2, 6, LANES), F32), vmem((PIECES, 2, 6, LANES), F32),
        vmem(measured.shape, F32), vmem(measured.shape, F32),
        vmem((3, 8, LANES), F32), vmem((PIECES, 8, LANES), F32), vmem((4, 8, LANES), F32), vmem((4, 8, LANES), F32),
        dma((8,)), dma((3,)), dma((3,)), dma((PIECES,)), dma((PIECES,)), dma((4, 3)),
        dma((2, 15)), dma((2, PIECES)), dma((2, 2, PIECES)), dma((2, 2, PIECES)),
        dma((2, 12)), dma((2, 12)), dma((1, 3)), dma((1, 3)), dma((4,)), dma((4,)),
        dma((2, 32)), dma((2, 32)), dma((2, PIECES)), dma((2, PIECES)), dma((3, PIECES)), dma((3, PIECES)), dma((2, 6)),
    ]
    whole = pl.BlockSpec(memory_space=pltpu.VMEM)
    far = pl.BlockSpec(memory_space=pltpu.HBM)
    rows = jnp.transpose(measured, (1, 0, 2))
    volume, residual, direction = pl.pallas_call(
        kernel,
        out_shape=(
            jax.ShapeDtypeStruct(start_volume.shape, F32),
            jax.ShapeDtypeStruct(rows.shape, F32),
            jax.ShapeDtypeStruct(start_volume.shape, F32),
        ),
        in_specs=[far] * 5,
        out_specs=(far, whole, far),
        scratch_shapes=scratch,
        compiler_params=pltpu.CompilerParams(
            collective_id=0, has_side_effects=True, vmem_limit_bytes=60 * 2**20
        ),
    )(start_volume, rows, row_shift, col_shift, col_frac)
    return volume, jnp.transpose(residual, (1, 0, 2)), direction


def solution(mesh):
    return jax.shard_map(
        per_device,
        mesh=mesh,
        in_specs=(
            P("slab", None, None),
            P("ang", "slab", None),
            P("ang", None),
            P("ang", None),
            P("ang", None),
        ),
        out_specs=(P("slab", None, None), P("ang", "slab", None), P("slab", None, None)),
        check_vma=False,
    )
```

```python
import jax
import jax.numpy as jnp
from jax import lax
from jax.experimental import pallas as pl
from jax.experimental.pallas import tpu as pltpu
from jax.sharding import PartitionSpec as P

MESH = pl.DeviceIdType.MESH
F32 = jnp.float32
PIECES = 16
SLICES = 3
LINES = 24
ROWS = 48
ANGLES = 4
LANES = 128
X = 2048


def rcopy(src, dst, send, recv, dev):
    return pltpu.make_async_remote_copy(
        src_ref=src, dst_ref=dst, send_sem=send, recv_sem=recv, device_id=dev, device_id_type=MESH
    )


def lanes_of(shape):
    return lax.broadcasted_iota(jnp.int32, shape, len(shape) - 1)


def kernel(
    x_hbm, m_hbm, rt_ref, ct_ref, ft_ref,
    vol_out, res_out, dir_out,
    xv, volv, dirv, gslab, qslab, m_ref, msh, mbuf, rtv, ctv, ftv, rts, cts, fts,
    xbuf, xhalo, gbuf, ghalo, packed, pad, img, wide, diff,
    part, rs1, sum1, rs2, own, qpart, qrs1, qsum1, qland,
    rblk, iblk, rres, ires, tiles, sc1, sc2, sc3,
    loc_sem, tab_send, tab_recv, m_send, m_recv, x_send,
    ag_send, ag_recv, hl_send, hl_recv,
    rs_send, rs_recv, rt_send, rt_recv, own_send, own_recv,
    sl_send, sl_recv, blk_send, blk_recv, sc_send, sc_recv, out_sem,
):
    ang = lax.axis_index("ang")
    slab = lax.axis_index("slab")
    p = lax.div(ang, 2)
    zlo = lax.rem(ang, 2)
    px = lax.div(p, 4)
    py = lax.rem(p, 4)
    zhi = lax.div(slab, 2)
    core = lax.rem(slab, 2)
    z = 2 * zhi + zlo
    c = 2 * z + core
    even = core == 0
    u = jnp.where(even, px, py)
    w = jnp.where(even, py, px)

    def pid(a, b):
        return jnp.where(even, 4 * a + b, 4 * b + a)

    def plane_dev(q):
        return (2 * q + zlo, slab)

    def col_dev(k):
        zz = lax.div(k, 2)
        return (2 * p + lax.rem(zz, 2), 2 * lax.div(zz, 2) + lax.rem(k, 2))

    def turn(v, d, n):
        return lax.rem(v + d, n)

    lane = lanes_of((LINES, LANES))
    lane_r = lanes_of((ROWS, LANES))
    me_dev = (ang, slab)

    def xy(a, b):
        return jnp.where(even, a, b), jnp.where(even, b, a)

    def is_me(dev):
        return jnp.logical_and(dev[0] == ang, dev[1] == slab)

    def apart(dev, then, here):
        pl.when(jnp.logical_not(is_me(dev)))(then)
        pl.when(is_me(dev))(here)

    def owner_dev(xx, yy):
        return (2 * (4 * zhi + 2 * core + lax.rem(yy, 2)) + zlo, 2 * xx + lax.div(yy, 2))

    partner = (2 * p + (1 - zlo), slab)
    yhi = lax.div(py, 2)
    ylo = lax.rem(py, 2)

    mload = pltpu.make_async_copy(m_hbm, m_ref, loc_sem.at[0])
    mload.start()
    tables = ((rt_ref, rtv, rts), (ct_ref, ctv, cts), (ft_ref, ftv, fts))

    def table_copy(n):
        return pltpu.make_async_copy(tables[n][0], tables[n][1].at[zlo], loc_sem.at[4 + n])

    for n in range(3):
        table_copy(n).start()
    xload = pltpu.make_async_copy(x_hbm, xv, loc_sem.at[1])
    xload.start()

    barrier = pltpu.get_barrier_semaphore()

    def greet(dev):
        pl.semaphore_signal(barrier, inc=1, device_id=dev, device_id_type=MESH)

    @pl.loop(1, PIECES)
    def _(d):
        greet(col_dev(turn(c, d, PIECES)))

    for d in range(1, 4):
        greet(plane_dev(pid(turn(u, d, 4), w)))
        greet(plane_dev(pid(u, turn(w, d, 4))))
    for a in range(4):
        greet((2 * pid(a, w) + 1 - zlo, slab))
    mine = 0
    for a in range(4):
        to = owner_dev(*xy(a, w))
        pl.when(jnp.logical_not(is_me(to)))(lambda to=to: greet(to))
        mine = mine + jnp.where(is_me(to), 1, 0)
        at_x, at_y = zhi, 2 * core + ylo
        come = (2 * jnp.where(yhi == 0, 4 * a + at_y, 4 * at_x + a) + zlo, 2 * px + yhi)
        pl.when(jnp.logical_not(is_me(come)))(lambda come=come: greet(come))

    lane6 = lanes_of((6, LANES))
    mload.wait()
    for a in range(2):
        prev = jnp.zeros((6, LANES), F32)
        for t in range(17):
            cur = jnp.zeros((6, LANES), F32)
            if t < 16:
                cur = pltpu.roll(m_ref[:, a, pl.ds(LANES * t, LANES)], 64, 1)
            msh[a, :, pl.ds(LANES * t, LANES)] = jnp.where(lane6 < 64, prev, cur)
            prev = cur

    pad[...] = jnp.zeros_like(pad)
    img[...] = jnp.zeros_like(img)
    xload.wait()
    pl.semaphore_wait(barrier, 15 + 6 + 4 + 8 - 2 * mine)

    def x_each(act_far, act_here):
        for to in range(4):
            for h in range(3):
                cc = 4 * to + 2 * zlo + (1 if h < 2 else 0)
                half = h if h < 2 else ylo
                k = 4 * zhi + 2 * core + half
                src = xv.at[pl.ds(3 * half, SLICES), :, pl.ds(pl.multiple_of(LANES * cc, LANES), LANES)]
                copy = rcopy(src, xbuf.at[k], x_send.at[to, h], ag_recv.at[0, k], col_dev(cc))
                local = pltpu.make_async_copy(src, xbuf.at[k], ag_recv.at[0, k])

                def act(copy=copy, local=local, cc=cc):
                    apart(col_dev(cc), lambda: act_far(copy), lambda: act_here(local))

                if h < 2:
                    pl.when(lax.rem(zhi, 2) == lax.rem(px, 2))(act)
                else:
                    act()

    x_each(lambda copy: copy.start(), lambda copy: copy.start())

    tabs = []
    for n, (src, dst, _) in enumerate(tables):
        t = rcopy(src, dst.at[zlo], tab_send.at[n], tab_recv.at[n], partner)
        t.start()
        tabs.append(t)

    def m_window(k):
        return msh.at[:, :, pl.ds(pl.multiple_of(LANES * k, LANES), 2 * LANES)]

    def m_copy(d):
        k = turn(c, d, PIECES)
        return rcopy(m_window(k), mbuf.at[c], m_send.at[d], m_recv.at[c], col_dev(k))

    @pl.loop(1, PIECES)
    def _(d):
        m_copy(d).start()

    mbuf[c] = msh[:, :, pl.ds(pl.multiple_of(LANES * c, LANES), 2 * LANES)]

    def step(q):
        return jnp.where(q < 2, q, 5 - q)

    def piece_order(t):
        late = t - 9
        dx = jnp.where(t < 9, step(lax.rem(t, 3)), jnp.where(late < 4, 2, step(late - 4)))
        dy = jnp.where(t < 9, step(lax.div(t, 3)), jnp.where(late < 4, step(late), 2))
        return 4 * turn(px, 4 - dx, 4) + turn(py, 4 - dy, 4)

    def gather_send1(buf, n):
        for d in range(1, 4):
            rcopy(buf.at[p], buf.at[p], ag_send.at[n, d - 1], ag_recv.at[n, p],
                  plane_dev(pid(turn(u, d, 4), w))).start()

    def gather_copy2(buf, n, da, d):
        k = pid(turn(u, 4 - da, 4), w)
        return rcopy(buf.at[k], buf.at[k], ag_send.at[n, 3 + 3 * da + d - 1], ag_recv.at[n, k],
                     plane_dev(pid(u, turn(w, d, 4))))

    def halo_copy(halo, n, k, side):
        to = turn(c, 1 if side == 0 else PIECES - 1, PIECES)
        return rcopy(packed.at[n, k, side], halo.at[k, side], hl_send.at[n, side, k], hl_recv.at[n, side, k], col_dev(to))

    def halo_start(buf, halo, n, k):
        for side in range(2):
            shift = 42 if side == 0 else 0
            v = [pltpu.roll(buf[k, i], shift + 42 * i, 1) if shift + i else buf[k, i] for i in range(SLICES)]
            packed[n, k, side] = jnp.where(lane < 42, v[0], jnp.where(lane < 84, v[1], v[2]))
            halo_copy(halo, n, k, side).start()

    def gather_wait(buf, n, k):
        rcopy(buf.at[k], buf.at[k], ag_send.at[n, 0], ag_recv.at[n, k], partner).wait_recv()

    def project_piece(buf, halo, k):
        for s in range(SLICES):
            mid = pltpu.roll(buf[k, s], 64, 1)
            left = jnp.where(c > 0, pltpu.roll(halo[k, 0], (150 - 42 * s) % LANES, 1), 0.0)
            right = jnp.where(c < PIECES - 1, pltpu.roll(halo[k, 1], (192 - 42 * s) % LANES, 1), 0.0)
            w0 = jnp.where(lane < 64, left, mid)
            w1 = jnp.where(lane < 64, mid, right)
            s0 = pltpu.roll(w0, 1, 1)
            s1 = pltpu.roll(w1, 1, 1)
            d0 = jnp.where(lane < 1, s1, s0) - w0
            d1 = jnp.where(lane < 1, s0, s1) - w1
            at = SLICES * k + s
            for a in range(ANGLES):
                f = fts[a // 2, a % 2, at]
                cs = cts[a // 2, a % 2, at]
                v0 = w0 + f * d0
                v1 = w1 + f * d1
                other = jnp.logical_or(lane >= LANES - cs, lane < -cs)
                sh = lax.rem(cs + LANES, LANES)
                pad[SLICES * a + s, 0, pl.ds(LINES, LINES), :] = pltpu.roll(jnp.where(other, v1, v0), sh, 1)
                pad[SLICES * a + s, 1, pl.ds(LINES, LINES), :] = pltpu.roll(jnp.where(other, v0, v1), sh, 1)
        for a in range(ANGLES):
            for t in range(2):
                acc = img[a, t]
                for s in range(SLICES):
                    rs = rts[a // 2, a % 2, SLICES * k + s]
                    acc = acc + pad[SLICES * a + s, t, pl.ds(LINES - rs, ROWS), :]
                img[a, t] = acc

    def gather_project(buf, halo, n):
        for da in (0, 1, 3, 2):
            k = pid(turn(u, 4 - da, 4), w)
            if n == 0 or da:
                gather_wait(buf, n, k)
            for d in (2, 1, 3) if n else (1, 3):
                gather_copy2(buf, n, da, d).start()
            halo_start(buf, halo, n, k)

        @pl.loop(0, 8)
        def _(t):
            k = pid(turn(u, 4 - step(lax.div(t, 2)), 4), turn(w, 3 - 2 * lax.rem(t, 2), 4))
            gather_wait(buf, n, k)
            halo_start(buf, halo, n, k)

        @pl.loop(0, PIECES)
        def _(t):
            @pl.when(jnp.logical_and(t >= 4, t < 8))
            def _():
                k = pid(turn(u, 4 - step(t - 4), 4), turn(w, 2, 4))
                gather_wait(buf, n, k)
                halo_start(buf, halo, n, k)

            k = piece_order(t)
            for side in range(2):
                halo_copy(halo, n, k, side).wait_recv()
            project_piece(buf, halo, k)

    def col_mask(t, ln):
        if t == 0:
            return jnp.logical_or(ln >= 64, c > 0)
        return jnp.logical_or(ln < 64, c < PIECES - 1)

    def own_tile(v0, v1, ln):
        return pltpu.roll(jnp.where(ln >= 64, v0, v1), 64, 1)

    def make_diff():
        for a in range(ANGLES):
            v0 = wide[a, 0]
            v1 = wide[a, 1]
            s0 = pltpu.roll(v0, LANES - 1, 1)
            s1 = pltpu.roll(v1, LANES - 1, 1)
            diff[a, 0] = jnp.where(lane_r == LANES - 1, s1, s0) - v0
            diff[a, 1] = jnp.where(lane_r == LANES - 1, s0, s1) - v1

    def back_piece(dst, k):
        for s in range(SLICES):
            at = SLICES * k + s
            acc = None
            for a in range(ANGLES):
                rs = rts[a // 2, a % 2, at]
                cs = cts[a // 2, a % 2, at]
                f = fts[a // 2, a % 2, at]
                first = lane >= 64 + cs
                v = jnp.where(first, wide[a, 0, pl.ds(rs, LINES), :], wide[a, 1, pl.ds(rs, LINES), :])
                e = jnp.where(first, diff[a, 0, pl.ds(rs, LINES), :], diff[a, 1, pl.ds(rs, LINES), :])
                term = pltpu.roll(v + f * e, 64 - cs, 1)
                acc = term if acc is None else acc + term
            dst[k, s] = acc

    def scatter_copy1(src, land, n, d, a):
        return rcopy(src.at[pid(a, turn(w, d, 4))], land.at[d - 1, a], rs_send.at[n, 4 * (d - 1) + a],
                     rs_recv.at[n, 4 * (d - 1) + a], plane_dev(pid(u, turn(w, d, 4))))

    def scatter_copy2(src, dst, n, d):
        a = turn(u, d, 4)
        return rcopy(src.at[a], dst.at[d - 1], rt_send.at[n, d - 1], rt_recv.at[n, d - 1], plane_dev(pid(a, w)))

    def back_scatter(dst, land, n, first):
        @pl.loop(0, PIECES)
        def _(t):
            i = lax.rem(t, 3)
            d = jnp.where(t >= 12, 0, jnp.where(i == 0, 2, 2 * i - 1))
            a = turn(first, jnp.where(t >= 12, t - 12, lax.div(t, 3)), 4)
            back_piece(dst, pid(a, turn(w, d, 4)))

            @pl.when(t < 12)
            def _():
                scatter_copy1(dst, land, n, d, a).start()

    def line_sum(dst, land, n, a):
        total = dst[pid(a, w)]
        for d in (1, 3, 2):
            scatter_copy1(dst, land, n, d, a).wait_recv()
            total = total + land[d - 1, a]
        return total

    def plane_sum(dst, land, total1, land2, n):
        for da in (1, 2, 3, 0):
            a = turn(u, da, 4)
            total1[a] = line_sum(dst, land, n, a)
            if da:
                scatter_copy2(total1, land2, n, da).start()
        total = total1[u]
        for d in (1, 3, 2):
            scatter_copy2(total1, land2, n, d).wait_recv()
            total = total + land2[d - 1]
        return total

    def owner_copy(a, total1, land):
        return rcopy(total1.at[a], land.at[u], own_send.at[a], own_recv.at[u], owner_dev(*xy(a, w)))

    def owner_start(dst, land1, total1, land, n):
        for a in range(4):
            total1[a] = line_sum(dst, land1, n, a)
            copy = owner_copy(a, total1, land)
            local = pltpu.make_async_copy(total1.at[a], land.at[u], own_recv.at[u])
            apart(owner_dev(*xy(a, w)), lambda: copy.start(), lambda: local.start())

    def owner_sum(total1, land):
        total = None
        for a in range(4):
            rcopy(total1.at[0], land.at[a], own_send.at[0], own_recv.at[a], partner).wait_recv()
            total = land[a] if total is None else total + land[a]
        return total

    def owner_finish(total1, land):
        for a in range(4):
            copy = owner_copy(a, total1, land)
            pl.when(jnp.logical_not(is_me(owner_dev(*xy(a, w)))))(lambda: copy.wait_send())

    def slab_at(buf, h, block):
        return buf.at[pl.ds(3 * h, SLICES), :, pl.ds(pl.multiple_of(LANES * block, LANES), LANES)]

    def slab_piece(buf, xx, yy, lo):
        return slab_at(buf, lax.rem(yy, 2), 4 * xx + 2 * lo + lax.div(yy, 2))

    def slab_copy(buf, n, a, b, lo, slot, dev):
        xx, yy = xy(a, b)
        ref = slab_piece(buf, xx, yy, lo)
        return rcopy(ref, ref, sl_send.at[n, slot], sl_recv.at[n, 2 * (4 * xx + yy) + lo], dev)

    def second_dev(d):
        return plane_dev(pid(u, turn(w, d, 4)))

    def slab_wait(buf, n, a, b, lo):
        slab_copy(buf, n, a, b, lo, 0, partner).wait_recv()

    def swap_copy(src, buf, n):
        return rcopy(src, slab_at(buf, ylo, c), sl_send.at[n, 31],
                     sl_recv.at[n, 2 * (4 * zhi + 2 * core + ylo) + zlo], owner_dev(px, py))

    def swap_start(src, buf, n):
        local = pltpu.make_async_copy(src, slab_at(buf, ylo, c), sl_recv.at[n, 2 * (4 * zhi + 2 * core + ylo) + zlo])
        apart(owner_dev(px, py), lambda: swap_copy(src, buf, n).start(), lambda: local.start())

    def slab_near(buf, n, a, lo, slot):
        slab_copy(buf, n, a, w, lo, slot, second_dev(1)).start()
        slab_copy(buf, n, a, w, lo, slot + 1, second_dev(3)).start()

    def slab_first(buf, n):
        for i, d in enumerate((2, 1, 3)):
            slab_copy(buf, n, u, w, zlo, i, plane_dev(pid(turn(u, d, 4), w))).start()
        slab_near(buf, n, u, zlo, 7)
        for i, d in enumerate((2, 1, 3, 0)):
            slab_copy(buf, n, u, w, zlo, 3 + i, (2 * pid(turn(u, d, 4), w) + 1 - zlo, slab)).start()

    def slab_second(buf, n):
        for i, d in enumerate((1, 3, 2)):
            a = turn(u, d, 4)
            slab_wait(buf, n, a, w, zlo)
            slab_near(buf, n, a, zlo, 9 + 2 * i)
        for i, d in enumerate((0, 1, 3, 2)):
            a = turn(u, d, 4)
            slab_wait(buf, n, a, w, 1 - zlo)
            slab_near(buf, n, a, 1 - zlo, 15 + 2 * i)

    def slab_third(buf, n):
        for i, d in enumerate((0, 1, 3, 2)):
            a = turn(u, d, 4)
            slab_wait(buf, n, a, turn(w, 3, 4), 0)
            slab_copy(buf, n, a, turn(w, 3, 4), 0, 23 + 2 * i, second_dev(1)).start()
            slab_wait(buf, n, a, turn(w, 1, 4), 1)
            slab_copy(buf, n, a, turn(w, 1, 4), 1, 24 + 2 * i, second_dev(3)).start()

    def slab_rest(buf, n):
        for lo in range(2):
            for d in (3 if lo else 1, 2):
                @pl.loop(0, 4)
                def _(a):
                    slab_wait(buf, n, a, turn(w, d, 4), lo)

    def slab_finish(buf, n):
        @pl.loop(0, 31)
        def _(t):
            slab_copy(buf, n, u, w, zlo, t, partner).wait_send()

    def blk_copy(src, dst, n, d):
        k = turn(c, d, PIECES)
        return rcopy(src.at[k], dst.at[:, :, pl.ds(pl.multiple_of(LANES * c, LANES), LANES)], blk_send.at[n, d],
                     blk_recv.at[n, c], col_dev(k))

    def blk_send_all(src, dst, n):
        @pl.loop(1, PIECES)
        def _(d):
            blk_copy(src, dst, n, d).start()

        dst[:, :, pl.ds(pl.multiple_of(LANES * c, LANES), LANES)] = src[c]

    def blk_finish(src, dst, n):
        @pl.loop(1, PIECES)
        def _(d):
            k = turn(c, d, PIECES)
            rcopy(src.at[0], dst.at[:, :, pl.ds(pl.multiple_of(LANES * k, LANES), LANES)], blk_send.at[n, d],
                  blk_recv.at[n, k], partner).wait_recv()
            blk_copy(src, dst, n, d).wait_send()

    def gather_finish(buf, halo, n):
        if n:
            for d in range(1, 4):
                rcopy(buf.at[0], buf.at[0], ag_send.at[n, d - 1], ag_recv.at[n, 0], partner).wait_send()
        for da in range(4):
            for d in (1, 2, 3) if n else (1, 3):
                gather_copy2(buf, n, da, d).wait_send()

        @pl.loop(0, PIECES)
        def _(t):
            for side in range(2):
                halo_copy(halo, n, t, side).wait_send()

    def scatter_finish(src, land1, n):
        @pl.loop(0, 12)
        def _(t):
            rcopy(src.at[0], land1.at[0, 0], rs_send.at[n, t], rs_recv.at[n, 0], partner).wait_send()

    def smem_copy(n):
        return pltpu.make_async_copy(tables[n][1], tables[n][2], loc_sem.at[4 + n])

    for n in range(3):
        table_copy(n).wait()
        tabs[n].wait()
        smem_copy(n).start()
    for n in range(3):
        smem_copy(n).wait()

    gather_project(xbuf, xhalo, 0)

    @pl.loop(1, PIECES)
    def _(d):
        k = turn(c, d, PIECES)
        rcopy(m_window(0), mbuf.at[k], m_send.at[d], m_recv.at[k], partner).wait_recv()

    for k in range(PIECES):
        rows = pl.ds(6 * (2 * (k // 4) + k % 2), 6)
        for e in range(2):
            a = 2 * ((k // 2) % 2) + e
            v0 = jnp.where(col_mask(0, lane6), mbuf[k, e, :, :LANES] - img[a, 0, rows, :], 0.0)
            v1 = jnp.where(col_mask(1, lane6), mbuf[k, e, :, LANES:] - img[a, 1, rows, :], 0.0)
            wide[a, 0, rows, :] = v0
            wide[a, 1, rows, :] = v1
            rblk[k, e] = own_tile(v0, v1, lane6)
    make_diff()

    back_scatter(part, rs1, 0, turn(u, 1, 4))
    blk_send_all(rblk, rres, 0)
    own[...] = plane_sum(part, rs1, sum1, rs2, 0)
    gbuf[p] = own[...]
    gather_send1(gbuf, 1)
    swap_start(own, gslab, 0)
    img[...] = jnp.zeros_like(img)
    gather_project(gbuf, ghalo, 1)
    slab_wait(gslab, 0, u, w, zlo)
    slab_first(gslab, 0)

    norm = jnp.zeros((ROWS, LANES), F32)
    for a in range(ANGLES):
        v0 = jnp.where(col_mask(0, lane_r), img[a, 0], 0.0)
        v1 = jnp.where(col_mask(1, lane_r), img[a, 1], 0.0)
        wide[a, 0] = v0
        wide[a, 1] = v1
        mine = jnp.where(lane_r >= 64, v0, v1)
        norm = norm + mine * mine
    make_diff()
    back_scatter(qpart, qrs1, 1, 0)
    slab_second(gslab, 0)
    owner_start(qpart, qrs1, qsum1, qland, 1)
    for k in range(PIECES):
        rows = pl.ds(6 * (2 * (k // 4) + k % 2), 6)
        for e in range(2):
            a = 2 * ((k // 2) % 2) + e
            iblk[k, e] = own_tile(wide[a, 0, rows, :], wide[a, 1, rows, :], lane6)
    q = owner_sum(qsum1, qland)
    qslab[pl.ds(3 * ylo, SLICES), :, pl.ds(pl.multiple_of(LANES * (4 * px + 2 * zlo + yhi), LANES), LANES)] = q
    slab_first(qslab, 1)

    tiles[...] = jnp.zeros_like(tiles)

    def down(v):
        return jnp.sum(v, axis=0, keepdims=True)

    g = own[...]
    tiles[0, 0:1, :] = down(jnp.sum(g * g, axis=0))
    tiles[0, 1:2, :] = down(norm)
    tiles[0, 2:3, :] = down(jnp.sum(q * q, axis=0))

    def sum_copy(land, n, d):
        at, dev = (
            (c, col_dev(turn(c, d, PIECES))),
            (px, plane_dev(4 * turn(px, d, 4) + py)),
            (py, plane_dev(4 * px + turn(py, d, 4))),
        )[n]
        return rcopy(tiles.at[n], land.at[at], sc_send.at[n, d], sc_recv.at[n, at], dev)

    def sum_start(land, n):
        @pl.loop(1, PIECES if n == 0 else 4)
        def _(d):
            sum_copy(land, n, d).start()

        land[(c, px, py)[n]] = tiles[n]

    def sum_finish(land, n):
        count = PIECES if n == 0 else 4

        @pl.loop(1, count)
        def _(d):
            k = turn((c, px, py)[n], d, count)
            rcopy(tiles.at[n], land.at[k], sc_send.at[n, d], sc_recv.at[n, k], partner).wait_recv()
            sum_copy(land, n, d).wait_send()

        total = land[0]
        for k in range(1, count):
            total = total + land[k]
        return total

    sum_start(sc1, 0)
    blk_send_all(iblk, ires, 1)
    slab_third(gslab, 0)
    slab_second(qslab, 1)
    tiles[1] = sum_finish(sc1, 0)
    sum_start(sc2, 1)
    slab_third(qslab, 1)
    tiles[2] = sum_finish(sc2, 1)
    sum_start(sc3, 2)
    slab_rest(gslab, 0)
    sums = jnp.sum(sum_finish(sc3, 2), axis=1, keepdims=True)
    gamma = sums[0:1]
    alpha = gamma / sums[1:2]
    scale = alpha * alpha * (sums[2:3] / gamma)

    blk_finish(rblk, rres, 0)
    blk_finish(iblk, ires, 1)
    for e in range(2):
        res_out[:, e, :] = rres[e] - alpha * ires[e]

    def out_copy(src, dst, n, i):
        return pltpu.make_async_copy(src.at[i], dst.at[i], out_sem.at[n, i])

    for i in range(6):
        volv[i] = xv[i] + alpha * gslab[i]
        out_copy(volv, vol_out, 0, i).start()
    slab_rest(qslab, 1)
    for i in range(6):
        dirv[i] = scale * gslab[i] - alpha * qslab[i]
        out_copy(dirv, dir_out, 1, i).start()

    @pl.loop(1, PIECES)
    def _(d):
        m_copy(d).wait_send()

    gather_finish(xbuf, xhalo, 0)
    gather_finish(gbuf, ghalo, 1)
    scatter_finish(part, rs1, 0)
    scatter_finish(qpart, qrs1, 1)
    for d in range(1, 4):
        scatter_copy2(sum1, rs2, 0, d).wait_send()
    owner_finish(qsum1, qland)
    slab_finish(gslab, 0)
    slab_finish(qslab, 1)
    pl.when(jnp.logical_not(is_me(owner_dev(px, py))))(lambda: swap_copy(own, gslab, 0).wait_send())
    x_each(lambda copy: copy.wait_send(), lambda copy: None)
    for i in range(6):
        out_copy(volv, vol_out, 0, i).wait()
        out_copy(dirv, dir_out, 1, i).wait()


def per_device(start_volume, measured, row_shift, col_shift, col_frac):
    piece = (SLICES, LINES, LANES)
    vmem = pltpu.VMEM
    dma = pltpu.SemaphoreType.DMA
    scratch = [
        vmem(start_volume.shape, F32), vmem(start_volume.shape, F32), vmem(start_volume.shape, F32),
        vmem(start_volume.shape, F32), vmem(start_volume.shape, F32),
        vmem((6, 2, X), F32),
        vmem((2, 6, 17 * LANES), F32),
        vmem((PIECES, 2, 6, 2 * LANES), F32),
        vmem((2, 2, 48), jnp.int32), vmem((2, 2, 48), jnp.int32), vmem((2, 2, 48), F32),
        pltpu.SMEM((2, 2, 48), jnp.int32), pltpu.SMEM((2, 2, 48), jnp.int32), pltpu.SMEM((2, 2, 48), F32),
        vmem((PIECES,) + piece, F32), vmem((PIECES, 2, LINES, LANES), F32),
        vmem((PIECES,) + piece, F32), vmem((PIECES, 2, LINES, LANES), F32),
        vmem((2, PIECES, 2, LINES, LANES), F32),
        vmem((ANGLES * SLICES, 2, 3 * LINES, LANES), F32),
        vmem((ANGLES, 2, ROWS, LANES), F32),
        vmem((ANGLES, 2, ROWS, LANES), F32),
        vmem((ANGLES, 2, ROWS, LANES), F32),
        vmem((PIECES,) + piece, F32), vmem((3, 4) + piece, F32), vmem((4,) + piece, F32), vmem((3,) + piece, F32), vmem(piece, F32),
        vmem((PIECES,) + piece, F32), vmem((3, 4) + piece, F32), vmem((4,) + piece, F32), vmem((4,) + piece, F32),
        vmem((PIECES, 2, 6, LANES), F32), vmem((PIECES, 2, 6, LANES), F32),
        vmem(measured.shape, F32), vmem(measured.shape, F32),
        vmem((3, 8, LANES), F32), vmem((PIECES, 8, LANES), F32), vmem((4, 8, LANES), F32), vmem((4, 8, LANES), F32),
        dma((8,)), dma((3,)), dma((3,)), dma((PIECES,)), dma((PIECES,)), dma((4, 3)),
        dma((2, 15)), dma((2, PIECES)), dma((2, 2, PIECES)), dma((2, 2, PIECES)),
        dma((2, 12)), dma((2, 12)), dma((1, 3)), dma((1, 3)), dma((4,)), dma((4,)),
        dma((2, 32)), dma((2, 32)), dma((2, PIECES)), dma((2, PIECES)), dma((3, PIECES)), dma((3, PIECES)), dma((2, 6)),
    ]
    whole = pl.BlockSpec(memory_space=pltpu.VMEM)
    far = pl.BlockSpec(memory_space=pltpu.HBM)
    rows = jnp.transpose(measured, (1, 0, 2))
    volume, residual, direction = pl.pallas_call(
        kernel,
        out_shape=(
            jax.ShapeDtypeStruct(start_volume.shape, F32),
            jax.ShapeDtypeStruct(rows.shape, F32),
            jax.ShapeDtypeStruct(start_volume.shape, F32),
        ),
        in_specs=[far] * 5,
        out_specs=(far, whole, far),
        scratch_shapes=scratch,
        compiler_params=pltpu.CompilerParams(
            collective_id=0, has_side_effects=True, vmem_limit_bytes=60 * 2**20
        ),
    )(start_volume, rows, row_shift, col_shift, col_frac)
    return volume, jnp.transpose(residual, (1, 0, 2)), direction


def solution(mesh):
    return jax.shard_map(
        per_device,
        mesh=mesh,
        in_specs=(
            P("slab", None, None),
            P("ang", "slab", None),
            P("ang", None),
            P("ang", None),
            P("ang", None),
        ),
        out_specs=(P("slab", None, None), P("ang", "slab", None), P("slab", None, None)),
        check_vma=False,
    )
```

```python
import jax
import jax.numpy as jnp
from jax import lax
from jax.experimental import pallas as pl
from jax.experimental.pallas import tpu as pltpu
from jax.sharding import PartitionSpec as P

MESH = pl.DeviceIdType.MESH
F32 = jnp.float32
PIECES = 16
SLICES = 3
LINES = 24
ROWS = 48
ANGLES = 4
LANES = 128
X = 2048


def rcopy(src, dst, send, recv, dev):
    return pltpu.make_async_remote_copy(
        src_ref=src, dst_ref=dst, send_sem=send, recv_sem=recv, device_id=dev, device_id_type=MESH
    )


class Piece:
    def __init__(self, *args):
        self.args = args

    def start(self):
        src, dst, *rest = self.args
        for i in range(SLICES):
            rcopy(src.at[i], dst.at[i], *rest).start()

    def wait_send(self):
        rcopy(*self.args).wait_send()

    def wait_recv(self):
        rcopy(*self.args).wait_recv()


def lanes_of(shape):
    return lax.broadcasted_iota(jnp.int32, shape, len(shape) - 1)


def kernel(
    x_hbm, m_hbm, rt_ref, ct_ref, ft_ref,
    vol_out, res_out, dir_out,
    xv, volv, dirv, gslab, qslab, m_ref, msh, mbuf, rtv, ctv, ftv, rts, cts, fts,
    xbuf, xhalo, gbuf, ghalo, packed, pad, img, wide, diff,
    part, rs1, sum1, rs2, own, qpart, qrs1, qsum1, qland,
    rblk, iblk, rres, ires, tiles, sc1, sc2, sc3,
    loc_sem, tab_send, tab_recv, m_send, m_recv, x_send,
    ag_send, ag_recv, hl_send, hl_recv,
    rs_send, rs_recv, rt_send, rt_recv, own_send, own_recv,
    sl_send, sl_recv, blk_send, blk_recv, sc_send, sc_recv, out_sem,
):
    ang = lax.axis_index("ang")
    slab = lax.axis_index("slab")
    p = lax.div(ang, 2)
    zlo = lax.rem(ang, 2)
    px = lax.div(p, 4)
    py = lax.rem(p, 4)
    zhi = lax.div(slab, 2)
    core = lax.rem(slab, 2)
    z = 2 * zhi + zlo
    c = 2 * z + core
    even = core == 0
    u = jnp.where(even, px, py)
    w = jnp.where(even, py, px)

    def pid(a, b):
        return jnp.where(even, 4 * a + b, 4 * b + a)

    def plane_dev(q):
        return (2 * q + zlo, slab)

    def col_dev(k):
        zz = lax.div(k, 2)
        return (2 * p + lax.rem(zz, 2), 2 * lax.div(zz, 2) + lax.rem(k, 2))

    def turn(v, d, n):
        return lax.rem(v + d, n)

    lane = lanes_of((LINES, LANES))
    lane_r = lanes_of((ROWS, LANES))
    me_dev = (ang, slab)

    def xy(a, b):
        return jnp.where(even, a, b), jnp.where(even, b, a)

    def is_me(dev):
        return jnp.logical_and(dev[0] == ang, dev[1] == slab)

    def apart(dev, then, here):
        pl.when(jnp.logical_not(is_me(dev)))(then)
        pl.when(is_me(dev))(here)

    def owner_dev(xx, yy):
        return (2 * (4 * zhi + 2 * core + lax.rem(yy, 2)) + zlo, 2 * xx + lax.div(yy, 2))

    partner = (2 * p + (1 - zlo), slab)
    yhi = lax.div(py, 2)
    ylo = lax.rem(py, 2)

    mload = pltpu.make_async_copy(m_hbm, m_ref, loc_sem.at[0])
    mload.start()
    tables = ((rt_ref, rtv, rts), (ct_ref, ctv, cts), (ft_ref, ftv, fts))

    def table_copy(n):
        return pltpu.make_async_copy(tables[n][0], tables[n][1].at[zlo], loc_sem.at[4 + n])

    for n in range(3):
        table_copy(n).start()
    xload = pltpu.make_async_copy(x_hbm, xv, loc_sem.at[1])
    xload.start()

    barrier = pltpu.get_barrier_semaphore()

    def greet(dev):
        pl.semaphore_signal(barrier, inc=1, device_id=dev, device_id_type=MESH)

    @pl.loop(1, PIECES)
    def _(d):
        greet(col_dev(turn(c, d, PIECES)))

    for d in range(1, 4):
        greet(plane_dev(pid(turn(u, d, 4), w)))
        greet(plane_dev(pid(u, turn(w, d, 4))))
    for a in range(4):
        greet((2 * pid(a, w) + 1 - zlo, slab))
    mine = 0
    for a in range(4):
        to = owner_dev(*xy(a, w))
        pl.when(jnp.logical_not(is_me(to)))(lambda to=to: greet(to))
        mine = mine + jnp.where(is_me(to), 1, 0)
        at_x, at_y = zhi, 2 * core + ylo
        come = (2 * jnp.where(yhi == 0, 4 * a + at_y, 4 * at_x + a) + zlo, 2 * px + yhi)
        pl.when(jnp.logical_not(is_me(come)))(lambda come=come: greet(come))

    lane6 = lanes_of((6, LANES))
    mload.wait()
    for a in range(2):
        prev = jnp.zeros((6, LANES), F32)
        for t in range(17):
            cur = jnp.zeros((6, LANES), F32)
            if t < 16:
                cur = pltpu.roll(m_ref[:, a, pl.ds(LANES * t, LANES)], 64, 1)
            msh[a, :, pl.ds(LANES * t, LANES)] = jnp.where(lane6 < 64, prev, cur)
            prev = cur

    pad[...] = jnp.zeros_like(pad)
    img[...] = jnp.zeros_like(img)
    xload.wait()
    pl.semaphore_wait(barrier, 15 + 6 + 4 + 8 - 2 * mine)

    def x_each(act_far, act_here):
        for to in range(4):
            for h in range(3):
                cc = 4 * to + 2 * zlo + (1 if h < 2 else 0)
                half = h if h < 2 else ylo
                k = 4 * zhi + 2 * core + half
                src = xv.at[pl.ds(3 * half, SLICES), :, pl.ds(pl.multiple_of(LANES * cc, LANES), LANES)]
                copy = Piece(src, xbuf.at[k], x_send.at[to, h], ag_recv.at[0, k], col_dev(cc))
                local = pltpu.make_async_copy(src, xbuf.at[k], ag_recv.at[0, k])

                def act(copy=copy, local=local, cc=cc):
                    apart(col_dev(cc), lambda: act_far(copy), lambda: act_here(local))

                if h < 2:
                    pl.when(lax.rem(zhi, 2) == lax.rem(px, 2))(act)
                else:
                    act()

    x_each(lambda copy: copy.start(), lambda copy: copy.start())

    tabs = []
    for n, (src, dst, _) in enumerate(tables):
        t = rcopy(src, dst.at[zlo], tab_send.at[n], tab_recv.at[n], partner)
        t.start()
        tabs.append(t)

    def m_window(k):
        return msh.at[:, :, pl.ds(pl.multiple_of(LANES * k, LANES), 2 * LANES)]

    def m_copy(d):
        k = turn(c, d, PIECES)
        return rcopy(m_window(k), mbuf.at[c], m_send.at[d], m_recv.at[c], col_dev(k))

    @pl.loop(1, PIECES)
    def _(d):
        m_copy(d).start()

    mbuf[c] = msh[:, :, pl.ds(pl.multiple_of(LANES * c, LANES), 2 * LANES)]

    def step(q):
        return jnp.where(q < 2, q, 5 - q)

    def piece_order(t):
        late = t - 9
        dx = jnp.where(t < 9, step(lax.rem(t, 3)), jnp.where(late < 4, 2, step(late - 4)))
        dy = jnp.where(t < 9, step(lax.div(t, 3)), jnp.where(late < 4, step(late), 2))
        return 4 * turn(px, 4 - dx, 4) + turn(py, 4 - dy, 4)

    def gather_send1(buf, n):
        for d in range(1, 4):
            Piece(buf.at[p], buf.at[p], ag_send.at[n, d - 1], ag_recv.at[n, p],
                  plane_dev(pid(turn(u, d, 4), w))).start()

    def gather_copy2(buf, n, da, d):
        k = pid(turn(u, 4 - da, 4), w)
        return rcopy(buf.at[k], buf.at[k], ag_send.at[n, 3 + 3 * da + d - 1], ag_recv.at[n, k],
                     plane_dev(pid(u, turn(w, d, 4))))

    def halo_copy(halo, n, k, side):
        to = turn(c, 1 if side == 0 else PIECES - 1, PIECES)
        return rcopy(packed.at[n, k, side], halo.at[k, side], hl_send.at[n, side, k], hl_recv.at[n, side, k], col_dev(to))

    def halo_start(buf, halo, n, k):
        for side in range(2):
            shift = 42 if side == 0 else 0
            v = [pltpu.roll(buf[k, i], shift + 42 * i, 1) if shift + i else buf[k, i] for i in range(SLICES)]
            packed[n, k, side] = jnp.where(lane < 42, v[0], jnp.where(lane < 84, v[1], v[2]))
            halo_copy(halo, n, k, side).start()

    def gather_wait(buf, n, k):
        rcopy(buf.at[k], buf.at[k], ag_send.at[n, 0], ag_recv.at[n, k], partner).wait_recv()

    def project_piece(buf, halo, k):
        for s in range(SLICES):
            mid = pltpu.roll(buf[k, s], 64, 1)
            left = jnp.where(c > 0, pltpu.roll(halo[k, 0], (150 - 42 * s) % LANES, 1), 0.0)
            right = jnp.where(c < PIECES - 1, pltpu.roll(halo[k, 1], (192 - 42 * s) % LANES, 1), 0.0)
            w0 = jnp.where(lane < 64, left, mid)
            w1 = jnp.where(lane < 64, mid, right)
            s0 = pltpu.roll(w0, 1, 1)
            s1 = pltpu.roll(w1, 1, 1)
            d0 = jnp.where(lane < 1, s1, s0) - w0
            d1 = jnp.where(lane < 1, s0, s1) - w1
            at = SLICES * k + s
            for a in range(ANGLES):
                f = fts[a // 2, a % 2, at]
                cs = cts[a // 2, a % 2, at]
                v0 = w0 + f * d0
                v1 = w1 + f * d1
                other = jnp.logical_or(lane >= LANES - cs, lane < -cs)
                sh = lax.rem(cs + LANES, LANES)
                pad[SLICES * a + s, 0, pl.ds(LINES, LINES), :] = pltpu.roll(jnp.where(other, v1, v0), sh, 1)
                pad[SLICES * a + s, 1, pl.ds(LINES, LINES), :] = pltpu.roll(jnp.where(other, v0, v1), sh, 1)
        for a in range(ANGLES):
            for t in range(2):
                acc = img[a, t]
                for s in range(SLICES):
                    rs = rts[a // 2, a % 2, SLICES * k + s]
                    acc = acc + pad[SLICES * a + s, t, pl.ds(LINES - rs, ROWS), :]
                img[a, t] = acc

    def gather_project(buf, halo, n):
        for da in (0, 1, 3, 2):
            k = pid(turn(u, 4 - da, 4), w)
            if n == 0 or da:
                gather_wait(buf, n, k)
            for d in (2, 1, 3) if n else (1, 3):
                gather_copy2(buf, n, da, d).start()
            halo_start(buf, halo, n, k)

        @pl.loop(0, 8)
        def _(t):
            k = pid(turn(u, 4 - step(lax.div(t, 2)), 4), turn(w, 3 - 2 * lax.rem(t, 2), 4))
            gather_wait(buf, n, k)
            halo_start(buf, halo, n, k)

        @pl.loop(0, PIECES)
        def _(t):
            @pl.when(jnp.logical_and(t >= 4, t < 8))
            def _():
                k = pid(turn(u, 4 - step(t - 4), 4), turn(w, 2, 4))
                gather_wait(buf, n, k)
                halo_start(buf, halo, n, k)

            k = piece_order(t)
            for side in range(2):
                halo_copy(halo, n, k, side).wait_recv()
            project_piece(buf, halo, k)

    def col_mask(t, ln):
        if t == 0:
            return jnp.logical_or(ln >= 64, c > 0)
        return jnp.logical_or(ln < 64, c < PIECES - 1)

    def own_tile(v0, v1, ln):
        return pltpu.roll(jnp.where(ln >= 64, v0, v1), 64, 1)

    def make_diff():
        for a in range(ANGLES):
            v0 = wide[a, 0]
            v1 = wide[a, 1]
            s0 = pltpu.roll(v0, LANES - 1, 1)
            s1 = pltpu.roll(v1, LANES - 1, 1)
            diff[a, 0] = jnp.where(lane_r == LANES - 1, s1, s0) - v0
            diff[a, 1] = jnp.where(lane_r == LANES - 1, s0, s1) - v1

    def back_piece(dst, k):
        for s in range(SLICES):
            at = SLICES * k + s
            acc = None
            for a in range(ANGLES):
                rs = rts[a // 2, a % 2, at]
                cs = cts[a // 2, a % 2, at]
                f = fts[a // 2, a % 2, at]
                first = lane >= 64 + cs
                v = jnp.where(first, wide[a, 0, pl.ds(rs, LINES), :], wide[a, 1, pl.ds(rs, LINES), :])
                e = jnp.where(first, diff[a, 0, pl.ds(rs, LINES), :], diff[a, 1, pl.ds(rs, LINES), :])
                term = pltpu.roll(v + f * e, 64 - cs, 1)
                acc = term if acc is None else acc + term
            dst[k, s] = acc

    def scatter_copy1(src, land, n, d, a):
        return rcopy(src.at[pid(a, turn(w, d, 4))], land.at[d - 1, a], rs_send.at[n, 4 * (d - 1) + a],
                     rs_recv.at[n, 4 * (d - 1) + a], plane_dev(pid(u, turn(w, d, 4))))

    def scatter_copy2(src, dst, n, d):
        a = turn(u, d, 4)
        return Piece(src.at[a], dst.at[d - 1], rt_send.at[n, d - 1], rt_recv.at[n, d - 1], plane_dev(pid(a, w)))

    def back_scatter(dst, land, n, first):
        @pl.loop(0, PIECES)
        def _(t):
            i = lax.rem(t, 3)
            d = jnp.where(t >= 12, 0, jnp.where(i == 0, 2, 2 * i - 1))
            a = turn(first, jnp.where(t >= 12, t - 12, lax.div(t, 3)), 4)
            back_piece(dst, pid(a, turn(w, d, 4)))

            @pl.when(t < 12)
            def _():
                scatter_copy1(dst, land, n, d, a).start()

    def line_sum(dst, land, n, a):
        total = dst[pid(a, w)]
        for d in (1, 3, 2):
            scatter_copy1(dst, land, n, d, a).wait_recv()
            total = total + land[d - 1, a]
        return total

    def plane_sum(dst, land, total1, land2, n):
        for da in (1, 2, 3, 0):
            a = turn(u, da, 4)
            total1[a] = line_sum(dst, land, n, a)
            if da:
                scatter_copy2(total1, land2, n, da).start()
        total = total1[u]
        for d in (1, 3, 2):
            scatter_copy2(total1, land2, n, d).wait_recv()
            total = total + land2[d - 1]
        return total

    def owner_copy(a, total1, land):
        return Piece(total1.at[a], land.at[u], own_send.at[a], own_recv.at[u], owner_dev(*xy(a, w)))

    def owner_start(dst, land1, total1, land, n):
        for a in range(4):
            total1[a] = line_sum(dst, land1, n, a)
            copy = owner_copy(a, total1, land)
            local = pltpu.make_async_copy(total1.at[a], land.at[u], own_recv.at[u])
            apart(owner_dev(*xy(a, w)), lambda: copy.start(), lambda: local.start())

    def owner_sum(total1, land):
        total = None
        for a in range(4):
            rcopy(total1.at[0], land.at[a], own_send.at[0], own_recv.at[a], partner).wait_recv()
            total = land[a] if total is None else total + land[a]
        return total

    def owner_finish(total1, land):
        for a in range(4):
            copy = owner_copy(a, total1, land)
            pl.when(jnp.logical_not(is_me(owner_dev(*xy(a, w)))))(lambda: copy.wait_send())

    def slab_at(buf, h, block):
        return buf.at[pl.ds(3 * h, SLICES), :, pl.ds(pl.multiple_of(LANES * block, LANES), LANES)]

    def slab_piece(buf, xx, yy, lo):
        return slab_at(buf, lax.rem(yy, 2), 4 * xx + 2 * lo + lax.div(yy, 2))

    def slab_copy(buf, n, a, b, lo, slot, dev):
        xx, yy = xy(a, b)
        ref = slab_piece(buf, xx, yy, lo)
        return (Piece if slot < 7 else rcopy)(ref, ref, sl_send.at[n, slot], sl_recv.at[n, 2 * (4 * xx + yy) + lo], dev)

    def second_dev(d):
        return plane_dev(pid(u, turn(w, d, 4)))

    def slab_wait(buf, n, a, b, lo):
        slab_copy(buf, n, a, b, lo, 0, partner).wait_recv()

    def swap_copy(src, buf, n):
        return rcopy(src, slab_at(buf, ylo, c), sl_send.at[n, 31],
                     sl_recv.at[n, 2 * (4 * zhi + 2 * core + ylo) + zlo], owner_dev(px, py))

    def swap_start(src, buf, n):
        local = pltpu.make_async_copy(src, slab_at(buf, ylo, c), sl_recv.at[n, 2 * (4 * zhi + 2 * core + ylo) + zlo])
        apart(owner_dev(px, py), lambda: swap_copy(src, buf, n).start(), lambda: local.start())

    def slab_near(buf, n, a, lo, slot):
        slab_copy(buf, n, a, w, lo, slot, second_dev(1)).start()
        slab_copy(buf, n, a, w, lo, slot + 1, second_dev(3)).start()

    def slab_first(buf, n):
        for i, d in enumerate((2, 1, 3)):
            slab_copy(buf, n, u, w, zlo, i, plane_dev(pid(turn(u, d, 4), w))).start()
        slab_near(buf, n, u, zlo, 7)
        for i, d in enumerate((2, 1, 3, 0)):
            slab_copy(buf, n, u, w, zlo, 3 + i, (2 * pid(turn(u, d, 4), w) + 1 - zlo, slab)).start()

    def slab_second(buf, n):
        for i, d in enumerate((1, 3, 2)):
            a = turn(u, d, 4)
            slab_wait(buf, n, a, w, zlo)
            slab_near(buf, n, a, zlo, 9 + 2 * i)
        for i, d in enumerate((0, 1, 3, 2)):
            a = turn(u, d, 4)
            slab_wait(buf, n, a, w, 1 - zlo)
            slab_near(buf, n, a, 1 - zlo, 15 + 2 * i)

    def slab_third(buf, n):
        for i, d in enumerate((0, 1, 3, 2)):
            a = turn(u, d, 4)
            slab_wait(buf, n, a, turn(w, 3, 4), 0)
            slab_copy(buf, n, a, turn(w, 3, 4), 0, 23 + 2 * i, second_dev(1)).start()
            slab_wait(buf, n, a, turn(w, 1, 4), 1)
            slab_copy(buf, n, a, turn(w, 1, 4), 1, 24 + 2 * i, second_dev(3)).start()

    def slab_rest(buf, n):
        for lo in range(2):
            for d in (3 if lo else 1, 2):
                @pl.loop(0, 4)
                def _(a):
                    slab_wait(buf, n, a, turn(w, d, 4), lo)

    def slab_finish(buf, n):
        @pl.loop(0, 31)
        def _(t):
            rcopy(buf.at[0:3, :, 0:LANES], buf.at[0:3, :, 0:LANES], sl_send.at[n, t], sl_recv.at[n, 0], partner).wait_send()

    def blk_copy(src, dst, n, d):
        k = turn(c, d, PIECES)
        return rcopy(src.at[k], dst.at[:, :, pl.ds(pl.multiple_of(LANES * c, LANES), LANES)], blk_send.at[n, d],
                     blk_recv.at[n, c], col_dev(k))

    def blk_send_all(src, dst, n):
        @pl.loop(1, PIECES)
        def _(d):
            blk_copy(src, dst, n, d).start()

        dst[:, :, pl.ds(pl.multiple_of(LANES * c, LANES), LANES)] = src[c]

    def blk_finish(src, dst, n):
        @pl.loop(1, PIECES)
        def _(d):
            k = turn(c, d, PIECES)
            rcopy(src.at[0], dst.at[:, :, pl.ds(pl.multiple_of(LANES * k, LANES), LANES)], blk_send.at[n, d],
                  blk_recv.at[n, k], partner).wait_recv()
            blk_copy(src, dst, n, d).wait_send()

    def gather_finish(buf, halo, n):
        if n:
            for d in range(1, 4):
                rcopy(buf.at[0], buf.at[0], ag_send.at[n, d - 1], ag_recv.at[n, 0], partner).wait_send()
        for da in range(4):
            for d in (1, 2, 3) if n else (1, 3):
                gather_copy2(buf, n, da, d).wait_send()

        @pl.loop(0, PIECES)
        def _(t):
            for side in range(2):
                halo_copy(halo, n, t, side).wait_send()

    def scatter_finish(src, land1, n):
        @pl.loop(0, 12)
        def _(t):
            rcopy(src.at[0], land1.at[0, 0], rs_send.at[n, t], rs_recv.at[n, 0], partner).wait_send()

    def smem_copy(n):
        return pltpu.make_async_copy(tables[n][1], tables[n][2], loc_sem.at[4 + n])

    for n in range(3):
        table_copy(n).wait()
        tabs[n].wait()
        smem_copy(n).start()
    for n in range(3):
        smem_copy(n).wait()

    gather_project(xbuf, xhalo, 0)

    @pl.loop(1, PIECES)
    def _(d):
        k = turn(c, d, PIECES)
        rcopy(m_window(0), mbuf.at[k], m_send.at[d], m_recv.at[k], partner).wait_recv()

    for k in range(PIECES):
        rows = pl.ds(6 * (2 * (k // 4) + k % 2), 6)
        for e in range(2):
            a = 2 * ((k // 2) % 2) + e
            v0 = jnp.where(col_mask(0, lane6), mbuf[k, e, :, :LANES] - img[a, 0, rows, :], 0.0)
            v1 = jnp.where(col_mask(1, lane6), mbuf[k, e, :, LANES:] - img[a, 1, rows, :], 0.0)
            wide[a, 0, rows, :] = v0
            wide[a, 1, rows, :] = v1
            rblk[k, e] = own_tile(v0, v1, lane6)
    make_diff()

    back_scatter(part, rs1, 0, turn(u, 1, 4))
    blk_send_all(rblk, rres, 0)
    own[...] = plane_sum(part, rs1, sum1, rs2, 0)
    gbuf[p] = own[...]
    gather_send1(gbuf, 1)
    swap_start(own, gslab, 0)
    img[...] = jnp.zeros_like(img)
    gather_project(gbuf, ghalo, 1)
    slab_wait(gslab, 0, u, w, zlo)
    slab_first(gslab, 0)

    norm = jnp.zeros((ROWS, LANES), F32)
    for a in range(ANGLES):
        v0 = jnp.where(col_mask(0, lane_r), img[a, 0], 0.0)
        v1 = jnp.where(col_mask(1, lane_r), img[a, 1], 0.0)
        wide[a, 0] = v0
        wide[a, 1] = v1
        mine = jnp.where(lane_r >= 64, v0, v1)
        norm = norm + mine * mine
    make_diff()
    back_scatter(qpart, qrs1, 1, 0)
    slab_second(gslab, 0)
    owner_start(qpart, qrs1, qsum1, qland, 1)
    for k in range(PIECES):
        rows = pl.ds(6 * (2 * (k // 4) + k % 2), 6)
        for e in range(2):
            a = 2 * ((k // 2) % 2) + e
            iblk[k, e] = own_tile(wide[a, 0, rows, :], wide[a, 1, rows, :], lane6)
    q = owner_sum(qsum1, qland)
    qslab[pl.ds(3 * ylo, SLICES), :, pl.ds(pl.multiple_of(LANES * (4 * px + 2 * zlo + yhi), LANES), LANES)] = q
    slab_first(qslab, 1)

    tiles[...] = jnp.zeros_like(tiles)

    def down(v):
        return jnp.sum(v, axis=0, keepdims=True)

    g = own[...]
    tiles[0, 0:1, :] = down(jnp.sum(g * g, axis=0))
    tiles[0, 1:2, :] = down(norm)
    tiles[0, 2:3, :] = down(jnp.sum(q * q, axis=0))

    def sum_copy(land, n, d):
        at, dev = (
            (c, col_dev(turn(c, d, PIECES))),
            (px, plane_dev(4 * turn(px, d, 4) + py)),
            (py, plane_dev(4 * px + turn(py, d, 4))),
        )[n]
        return rcopy(tiles.at[n], land.at[at], sc_send.at[n, d], sc_recv.at[n, at], dev)

    def sum_start(land, n):
        @pl.loop(1, PIECES if n == 0 else 4)
        def _(d):
            sum_copy(land, n, d).start()

        land[(c, px, py)[n]] = tiles[n]

    def sum_finish(land, n):
        count = PIECES if n == 0 else 4

        @pl.loop(1, count)
        def _(d):
            k = turn((c, px, py)[n], d, count)
            rcopy(tiles.at[n], land.at[k], sc_send.at[n, d], sc_recv.at[n, k], partner).wait_recv()
            sum_copy(land, n, d).wait_send()

        total = land[0]
        for k in range(1, count):
            total = total + land[k]
        return total

    sum_start(sc1, 0)
    blk_send_all(iblk, ires, 1)
    slab_third(gslab, 0)
    slab_second(qslab, 1)
    tiles[1] = sum_finish(sc1, 0)
    sum_start(sc2, 1)
    slab_third(qslab, 1)
    tiles[2] = sum_finish(sc2, 1)
    sum_start(sc3, 2)
    slab_rest(gslab, 0)
    sums = jnp.sum(sum_finish(sc3, 2), axis=1, keepdims=True)
    gamma = sums[0:1]
    alpha = gamma / sums[1:2]
    scale = alpha * alpha * (sums[2:3] / gamma)

    blk_finish(rblk, rres, 0)
    blk_finish(iblk, ires, 1)
    for e in range(2):
        res_out[:, e, :] = rres[e] - alpha * ires[e]

    def out_copy(src, dst, n, i):
        return pltpu.make_async_copy(src.at[i], dst.at[i], out_sem.at[n, i])

    for i in range(6):
        volv[i] = xv[i] + alpha * gslab[i]
        out_copy(volv, vol_out, 0, i).start()
    slab_rest(qslab, 1)
    for i in range(6):
        dirv[i] = scale * gslab[i] - alpha * qslab[i]
        out_copy(dirv, dir_out, 1, i).start()

    @pl.loop(1, PIECES)
    def _(d):
        m_copy(d).wait_send()

    gather_finish(xbuf, xhalo, 0)
    gather_finish(gbuf, ghalo, 1)
    scatter_finish(part, rs1, 0)
    scatter_finish(qpart, qrs1, 1)
    for d in range(1, 4):
        scatter_copy2(sum1, rs2, 0, d).wait_send()
    owner_finish(qsum1, qland)
    slab_finish(gslab, 0)
    slab_finish(qslab, 1)
    pl.when(jnp.logical_not(is_me(owner_dev(px, py))))(lambda: swap_copy(own, gslab, 0).wait_send())
    x_each(lambda copy: copy.wait_send(), lambda copy: None)
    for i in range(6):
        out_copy(volv, vol_out, 0, i).wait()
        out_copy(dirv, dir_out, 1, i).wait()


def per_device(start_volume, measured, row_shift, col_shift, col_frac):
    piece = (SLICES, LINES, LANES)
    vmem = pltpu.VMEM
    dma = pltpu.SemaphoreType.DMA
    scratch = [
        vmem(start_volume.shape, F32), vmem(start_volume.shape, F32), vmem(start_volume.shape, F32),
        vmem(start_volume.shape, F32), vmem(start_volume.shape, F32),
        vmem((6, 2, X), F32),
        vmem((2, 6, 17 * LANES), F32),
        vmem((PIECES, 2, 6, 2 * LANES), F32),
        vmem((2, 2, 48), jnp.int32), vmem((2, 2, 48), jnp.int32), vmem((2, 2, 48), F32),
        pltpu.SMEM((2, 2, 48), jnp.int32), pltpu.SMEM((2, 2, 48), jnp.int32), pltpu.SMEM((2, 2, 48), F32),
        vmem((PIECES,) + piece, F32), vmem((PIECES, 2, LINES, LANES), F32),
        vmem((PIECES,) + piece, F32), vmem((PIECES, 2, LINES, LANES), F32),
        vmem((2, PIECES, 2, LINES, LANES), F32),
        vmem((ANGLES * SLICES, 2, 3 * LINES, LANES), F32),
        vmem((ANGLES, 2, ROWS, LANES), F32),
        vmem((ANGLES, 2, ROWS, LANES), F32),
        vmem((ANGLES, 2, ROWS, LANES), F32),
        vmem((PIECES,) + piece, F32), vmem((3, 4) + piece, F32), vmem((4,) + piece, F32), vmem((3,) + piece, F32), vmem(piece, F32),
        vmem((PIECES,) + piece, F32), vmem((3, 4) + piece, F32), vmem((4,) + piece, F32), vmem((4,) + piece, F32),
        vmem((PIECES, 2, 6, LANES), F32), vmem((PIECES, 2, 6, LANES), F32),
        vmem(measured.shape, F32), vmem(measured.shape, F32),
        vmem((3, 8, LANES), F32), vmem((PIECES, 8, LANES), F32), vmem((4, 8, LANES), F32), vmem((4, 8, LANES), F32),
        dma((8,)), dma((3,)), dma((3,)), dma((PIECES,)), dma((PIECES,)), dma((4, 3)),
        dma((2, 15)), dma((2, PIECES)), dma((2, 2, PIECES)), dma((2, 2, PIECES)),
        dma((2, 12)), dma((2, 12)), dma((1, 3)), dma((1, 3)), dma((4,)), dma((4,)),
        dma((2, 32)), dma((2, 32)), dma((2, PIECES)), dma((2, PIECES)), dma((3, PIECES)), dma((3, PIECES)), dma((2, 6)),
    ]
    whole = pl.BlockSpec(memory_space=pltpu.VMEM)
    far = pl.BlockSpec(memory_space=pltpu.HBM)
    rows = jnp.transpose(measured, (1, 0, 2))
    volume, residual, direction = pl.pallas_call(
        kernel,
        out_shape=(
            jax.ShapeDtypeStruct(start_volume.shape, F32),
            jax.ShapeDtypeStruct(rows.shape, F32),
            jax.ShapeDtypeStruct(start_volume.shape, F32),
        ),
        in_specs=[far] * 5,
        out_specs=(far, whole, far),
        scratch_shapes=scratch,
        compiler_params=pltpu.CompilerParams(
            collective_id=0, has_side_effects=True, vmem_limit_bytes=60 * 2**20
        ),
    )(start_volume, rows, row_shift, col_shift, col_frac)
    return volume, jnp.transpose(residual, (1, 0, 2)), direction


def solution(mesh):
    return jax.shard_map(
        per_device,
        mesh=mesh,
        in_specs=(
            P("slab", None, None),
            P("ang", "slab", None),
            P("ang", None),
            P("ang", None),
            P("ang", None),
        ),
        out_specs=(P("slab", None, None), P("ang", "slab", None), P("slab", None, None)),
        check_vma=False,
    )
```

```python
import jax
import jax.numpy as jnp
from jax import lax
from jax.experimental import pallas as pl
from jax.experimental.pallas import tpu as pltpu
from jax.sharding import PartitionSpec as P

MESH = pl.DeviceIdType.MESH
F32 = jnp.float32
PIECES = 16
SLICES = 3
LINES = 24
ROWS = 48
ANGLES = 4
LANES = 128
X = 2048


def rcopy(src, dst, send, recv, dev):
    return pltpu.make_async_remote_copy(
        src_ref=src, dst_ref=dst, send_sem=send, recv_sem=recv, device_id=dev, device_id_type=MESH
    )


def lanes_of(shape):
    return lax.broadcasted_iota(jnp.int32, shape, len(shape) - 1)


def kernel(
    x_hbm, m_hbm, rt_ref, ct_ref, ft_ref,
    vol_out, res_out, dir_out,
    xv, volv, dirv, gslab, qslab, m_ref, msh, mbuf, rtv, ctv, ftv, rts, cts, fts,
    xbuf, xhalo, gbuf, ghalo, pad, img, wide, diff,
    part, rs1, sum1, rs2, own, qpart, qrs1, qsum1, qland,
    rblk, iblk, rres, ires, tiles, sc1, sc2, sc3,
    loc_sem, tab_send, tab_recv, m_send, m_recv, x_send,
    ag_send, ag_recv, hl_send, hl_recv,
    rs_send, rs_recv, rt_send, rt_recv, own_send, own_recv,
    sl_send, sl_recv, blk_send, blk_recv, sc_send, sc_recv, out_sem,
):
    ang = lax.axis_index("ang")
    slab = lax.axis_index("slab")
    p = lax.div(ang, 2)
    zlo = lax.rem(ang, 2)
    px = lax.div(p, 4)
    py = lax.rem(p, 4)
    zhi = lax.div(slab, 2)
    core = lax.rem(slab, 2)
    z = 2 * zhi + zlo
    c = 2 * z + core
    even = core == 0
    u = jnp.where(even, px, py)
    w = jnp.where(even, py, px)

    def pid(a, b):
        return jnp.where(even, 4 * a + b, 4 * b + a)

    def plane_dev(q):
        return (2 * q + zlo, slab)

    def col_dev(k):
        zz = lax.div(k, 2)
        return (2 * p + lax.rem(zz, 2), 2 * lax.div(zz, 2) + lax.rem(k, 2))

    def turn(v, d, n):
        return lax.rem(v + d, n)

    lane = lanes_of((8, LANES))
    exist = jnp.where(lane < 64, jnp.where(c < PIECES - 1, 1, 0), jnp.where(c > 0, 1, 0)) > 0
    me_dev = (ang, slab)

    def xy(a, b):
        return jnp.where(even, a, b), jnp.where(even, b, a)

    def is_me(dev):
        return jnp.logical_and(dev[0] == ang, dev[1] == slab)

    def apart(dev, then, here):
        pl.when(jnp.logical_not(is_me(dev)))(then)
        pl.when(is_me(dev))(here)

    def owner_dev(xx, yy):
        return (2 * (4 * zhi + 2 * core + lax.rem(yy, 2)) + zlo, 2 * xx + lax.div(yy, 2))

    partner = (2 * p + (1 - zlo), slab)
    yhi = lax.div(py, 2)
    ylo = lax.rem(py, 2)

    mload = pltpu.make_async_copy(m_hbm, m_ref, loc_sem.at[0])
    mload.start()
    tables = ((rt_ref, rtv, rts), (ct_ref, ctv, cts), (ft_ref, ftv, fts))

    def table_copy(n):
        return pltpu.make_async_copy(tables[n][0], tables[n][1].at[zlo], loc_sem.at[4 + n])

    for n in range(3):
        table_copy(n).start()
    xload = pltpu.make_async_copy(x_hbm, xv, loc_sem.at[1])
    xload.start()

    barrier = pltpu.get_barrier_semaphore()

    def greet(dev):
        pl.semaphore_signal(barrier, inc=1, device_id=dev, device_id_type=MESH)

    @pl.loop(1, PIECES)
    def _(d):
        greet(col_dev(turn(c, d, PIECES)))

    for d in range(1, 4):
        greet(plane_dev(pid(turn(u, d, 4), w)))
        greet(plane_dev(pid(u, turn(w, d, 4))))
    for a in range(4):
        greet((2 * pid(a, w) + 1 - zlo, slab))
    mine = 0
    for a in range(4):
        to = owner_dev(*xy(a, w))
        pl.when(jnp.logical_not(is_me(to)))(lambda to=to: greet(to))
        mine = mine + jnp.where(is_me(to), 1, 0)
        at_x, at_y = zhi, 2 * core + ylo
        come = (2 * jnp.where(yhi == 0, 4 * a + at_y, 4 * at_x + a) + zlo, 2 * px + yhi)
        pl.when(jnp.logical_not(is_me(come)))(lambda come=come: greet(come))

    lane6 = lanes_of((6, LANES))
    mload.wait()
    for a in range(2):
        for t in range(PIECES):
            here = m_ref[:, a, pl.ds(LANES * t, LANES)]
            right = m_ref[:, a, pl.ds(LANES * min(t + 1, 15), LANES)]
            left = m_ref[:, a, pl.ds(LANES * max(t - 1, 0), LANES)]
            msh[t, a, :, :LANES] = here
            msh[t, a, :, LANES:] = jnp.where(lane6 < 64, right, left)

    pad[...] = jnp.zeros_like(pad)
    img[...] = jnp.zeros_like(img)
    xload.wait()
    pl.semaphore_wait(barrier, 15 + 6 + 4 + 8 - 2 * mine)

    def x_each(act_far, act_here):
        for to in range(4):
            for h in range(3):
                cc = 4 * to + 2 * zlo + (1 if h < 2 else 0)
                half = h if h < 2 else ylo
                k = 4 * zhi + 2 * core + half
                src = xv.at[pl.ds(3 * half, SLICES), :, pl.ds(pl.multiple_of(LANES * cc, LANES), LANES)]
                copy = rcopy(src, xbuf.at[k], x_send.at[to, h], ag_recv.at[0, k], col_dev(cc))
                local = pltpu.make_async_copy(src, xbuf.at[k], ag_recv.at[0, k])

                def act(copy=copy, local=local, cc=cc):
                    apart(col_dev(cc), lambda: act_far(copy), lambda: act_here(local))

                if h < 2:
                    pl.when(lax.rem(zhi, 2) == lax.rem(px, 2))(act)
                else:
                    act()

    x_each(lambda copy: copy.start(), lambda copy: copy.start())

    tabs = []
    for n, (src, dst, _) in enumerate(tables):
        t = rcopy(src, dst.at[zlo], tab_send.at[n], tab_recv.at[n], partner)
        t.start()
        tabs.append(t)

    def m_copy(d):
        k = turn(c, d, PIECES)
        return rcopy(msh.at[k], mbuf.at[c], m_send.at[d], m_recv.at[c], col_dev(k))

    @pl.loop(1, PIECES)
    def _(d):
        m_copy(d).start()

    mbuf[c] = msh[c]

    def step(q):
        return jnp.where(q < 2, q, 5 - q)

    def piece_order(t):
        late = t - 9
        dx = jnp.where(t < 9, step(lax.rem(t, 3)), jnp.where(late < 4, 2, step(late - 4)))
        dy = jnp.where(t < 9, step(lax.div(t, 3)), jnp.where(late < 4, step(late), 2))
        return 4 * turn(px, 4 - dx, 4) + turn(py, 4 - dy, 4)

    def gather_send1(buf, n):
        for d in range(1, 4):
            rcopy(buf.at[p], buf.at[p], ag_send.at[n, d - 1], ag_recv.at[n, p],
                  plane_dev(pid(turn(u, d, 4), w))).start()

    def gather_copy2(buf, n, da, d):
        k = pid(turn(u, 4 - da, 4), w)
        return rcopy(buf.at[k], buf.at[k], ag_send.at[n, 3 + 3 * da + d - 1], ag_recv.at[n, k],
                     plane_dev(pid(u, turn(w, d, 4))))

    def halo_copy(buf, halo, n, k, side):
        to = turn(c, 1 if side == 0 else PIECES - 1, PIECES)
        return rcopy(buf.at[k], halo.at[k, side], hl_send.at[n, side, k], hl_recv.at[n, side, k], col_dev(to))

    def halo_start(buf, halo, n, k):
        for side in range(2):
            halo_copy(buf, halo, n, k, side).start()

    def gather_wait(buf, n, k):
        rcopy(buf.at[k], buf.at[k], ag_send.at[n, 0], ag_recv.at[n, k], partner).wait_recv()

    tiles3 = (SLICES, 8, LANES)

    def project_piece(buf, halo, k):
        for s in range(SLICES):
            w0 = buf[k, s].reshape(tiles3)
            left = halo[k, 0, s].reshape(tiles3)
            right = halo[k, 1, s].reshape(tiles3)
            w1 = jnp.where(exist, jnp.where(lane < 64, right, left), 0.0)
            s0 = pltpu.roll(w0, 1, 2)
            s1 = pltpu.roll(w1, 1, 2)
            d0 = jnp.where(lane < 1, s1, s0) - w0
            d1 = jnp.where(lane < 1, s0, s1) - w1
            at = SLICES * k + s
            for a in range(ANGLES):
                f = fts[a // 2, a % 2, at]
                cs = cts[a // 2, a % 2, at]
                v0 = w0 + f * d0
                v1 = w1 + f * d1
                other = jnp.logical_or(lane >= LANES - cs, lane < -cs)
                sh = lax.rem(cs + LANES, LANES)
                full = (LINES, LANES)
                pad[SLICES * a + s, 0, pl.ds(LINES, LINES), :] = pltpu.roll(jnp.where(other, v1, v0), sh, 2).reshape(full)
                pad[SLICES * a + s, 1, pl.ds(LINES, LINES), :] = pltpu.roll(jnp.where(other, v0, v1), sh, 2).reshape(full)
        for a in range(ANGLES):
            for t in range(2):
                acc = img[a, t]
                for s in range(SLICES):
                    rs = rts[a // 2, a % 2, SLICES * k + s]
                    acc = acc + pad[SLICES * a + s, t, pl.ds(LINES - rs, ROWS), :]
                img[a, t] = acc

    def gather_project(buf, halo, n, during):
        for da in (0, 1, 3, 2):
            k = pid(turn(u, 4 - da, 4), w)
            if n == 0 or da:
                gather_wait(buf, n, k)
            for d in (2, 1, 3) if n else (1, 3):
                gather_copy2(buf, n, da, d).start()
            halo_start(buf, halo, n, k)

        @pl.loop(0, 8)
        def _(t):
            k = pid(turn(u, 4 - step(lax.div(t, 2)), 4), turn(w, 3 - 2 * lax.rem(t, 2), 4))
            gather_wait(buf, n, k)
            halo_start(buf, halo, n, k)

        @pl.loop(0, PIECES)
        def _(t):
            if during is not None:
                pl.when(t == 10)(during)

            @pl.when(jnp.logical_and(t >= 4, t < 8))
            def _():
                k = pid(turn(u, 4 - step(t - 4), 4), turn(w, 2, 4))
                gather_wait(buf, n, k)
                halo_start(buf, halo, n, k)

            k = piece_order(t)
            for side in range(2):
                halo_copy(buf, halo, n, k, side).wait_recv()
            project_piece(buf, halo, k)

    def halo_mask(v):
        return jnp.where(exist, v.reshape(ROWS // 8, 8, LANES), 0.0).reshape(ROWS, LANES)

    def make_diff():
        last = lanes_of((ROWS, LANES)) == LANES - 1
        for a in range(ANGLES):
            v0 = wide[a, 0]
            v1 = wide[a, 1]
            s0 = pltpu.roll(v0, LANES - 1, 1)
            s1 = pltpu.roll(v1, LANES - 1, 1)
            diff[a, 0] = jnp.where(last, s1, s0) - v0
            diff[a, 1] = jnp.where(last, s0, s1) - v1

    def back_piece(dst, k):
        for s in range(SLICES):
            at = SLICES * k + s
            acc = None
            for a in range(ANGLES):
                rs = rts[a // 2, a % 2, at]
                cs = cts[a // 2, a % 2, at]
                f = fts[a // 2, a % 2, at]
                other = jnp.logical_or(lane < cs, lane >= LANES + cs)

                def rows_at(ref, t):
                    return ref[a, t, pl.ds(rs, LINES), :].reshape(tiles3)

                v = jnp.where(other, rows_at(wide, 1), rows_at(wide, 0))
                e = jnp.where(other, rows_at(diff, 1), rows_at(diff, 0))
                term = pltpu.roll(v + f * e, lax.rem(LANES - cs, LANES), 2)
                acc = term if acc is None else acc + term
            dst[k, s] = acc.reshape(LINES, LANES)

    def scatter_copy1(src, land, n, d, a):
        return rcopy(src.at[pid(a, turn(w, d, 4))], land.at[d - 1, a], rs_send.at[n, 4 * (d - 1) + a],
                     rs_recv.at[n, 4 * (d - 1) + a], plane_dev(pid(u, turn(w, d, 4))))

    def scatter_copy2(src, dst, n, d):
        a = turn(u, d, 4)
        return rcopy(src.at[a], dst.at[d - 1], rt_send.at[n, d - 1], rt_recv.at[n, d - 1], plane_dev(pid(a, w)))

    def back_scatter(dst, land, n, first):
        @pl.loop(0, PIECES)
        def _(t):
            i = lax.rem(t, 3)
            d = jnp.where(t >= 12, 0, jnp.where(i == 0, 2, 2 * i - 1))
            a = turn(first, jnp.where(t >= 12, t - 12, lax.div(t, 3)), 4)
            back_piece(dst, pid(a, turn(w, d, 4)))

            @pl.when(t < 12)
            def _():
                scatter_copy1(dst, land, n, d, a).start()

    def line_sum(dst, land, n, a):
        total = dst[pid(a, w)]
        for d in (1, 3, 2):
            scatter_copy1(dst, land, n, d, a).wait_recv()
            total = total + land[d - 1, a]
        return total

    def plane_sum(dst, land, total1, land2, n):
        for da in (1, 2, 3, 0):
            a = turn(u, da, 4)
            total1[a] = line_sum(dst, land, n, a)
            if da:
                scatter_copy2(total1, land2, n, da).start()
        total = total1[u]
        for d in (1, 3, 2):
            scatter_copy2(total1, land2, n, d).wait_recv()
            total = total + land2[d - 1]
        return total

    def owner_copy(a, total1, land):
        return rcopy(total1.at[a], land.at[u], own_send.at[a], own_recv.at[u], owner_dev(*xy(a, w)))

    def owner_start(dst, land1, total1, land, n):
        for a in range(4):
            total1[a] = line_sum(dst, land1, n, a)
            copy = owner_copy(a, total1, land)
            local = pltpu.make_async_copy(total1.at[a], land.at[u], own_recv.at[u])
            apart(owner_dev(*xy(a, w)), lambda: copy.start(), lambda: local.start())

    def owner_sum(total1, land):
        total = None
        for a in range(4):
            rcopy(total1.at[0], land.at[a], own_send.at[0], own_recv.at[a], partner).wait_recv()
            total = land[a] if total is None else total + land[a]
        return total

    def owner_finish(total1, land):
        for a in range(4):
            copy = owner_copy(a, total1, land)
            pl.when(jnp.logical_not(is_me(owner_dev(*xy(a, w)))))(lambda: copy.wait_send())

    def slab_at(buf, h, block):
        return buf.at[pl.ds(3 * h, SLICES), :, pl.ds(pl.multiple_of(LANES * block, LANES), LANES)]

    def slab_piece(buf, xx, yy, lo):
        return slab_at(buf, lax.rem(yy, 2), 4 * xx + 2 * lo + lax.div(yy, 2))

    def slab_copy(buf, n, a, b, lo, slot, dev):
        xx, yy = xy(a, b)
        ref = slab_piece(buf, xx, yy, lo)
        return rcopy(ref, ref, sl_send.at[n, slot], sl_recv.at[n, 2 * (4 * xx + yy) + lo], dev)

    def second_dev(d):
        return plane_dev(pid(u, turn(w, d, 4)))

    def slab_wait(buf, n, a, b, lo):
        slab_copy(buf, n, a, b, lo, 0, partner).wait_recv()

    def swap_copy(src, buf, n):
        return rcopy(src, slab_at(buf, ylo, c), sl_send.at[n, 31],
                     sl_recv.at[n, 2 * (4 * zhi + 2 * core + ylo) + zlo], owner_dev(px, py))

    def swap_start(src, buf, n):
        local = pltpu.make_async_copy(src, slab_at(buf, ylo, c), sl_recv.at[n, 2 * (4 * zhi + 2 * core + ylo) + zlo])
        apart(owner_dev(px, py), lambda: swap_copy(src, buf, n).start(), lambda: local.start())

    def slab_near(buf, n, a, lo, slot):
        slab_copy(buf, n, a, w, lo, slot, second_dev(1)).start()
        slab_copy(buf, n, a, w, lo, slot + 1, second_dev(3)).start()

    def slab_first(buf, n):
        for i, d in enumerate((2, 1, 3)):
            slab_copy(buf, n, u, w, zlo, i, plane_dev(pid(turn(u, d, 4), w))).start()
        slab_near(buf, n, u, zlo, 7)
        for i, d in enumerate((2, 1, 3, 0)):
            slab_copy(buf, n, u, w, zlo, 3 + i, (2 * pid(turn(u, d, 4), w) + 1 - zlo, slab)).start()

    def slab_second(buf, n):
        for i, d in enumerate((1, 3, 2)):
            a = turn(u, d, 4)
            slab_wait(buf, n, a, w, zlo)
            slab_near(buf, n, a, zlo, 9 + 2 * i)
        for i, d in enumerate((0, 1, 3, 2)):
            a = turn(u, d, 4)
            slab_wait(buf, n, a, w, 1 - zlo)
            slab_near(buf, n, a, 1 - zlo, 15 + 2 * i)

    def slab_third(buf, n):
        for i, d in enumerate((0, 1, 3, 2)):
            a = turn(u, d, 4)
            slab_wait(buf, n, a, turn(w, 3, 4), 0)
            slab_copy(buf, n, a, turn(w, 3, 4), 0, 23 + 2 * i, second_dev(1)).start()
            slab_wait(buf, n, a, turn(w, 1, 4), 1)
            slab_copy(buf, n, a, turn(w, 1, 4), 1, 24 + 2 * i, second_dev(3)).start()

    def slab_rest(buf, n):
        for lo in range(2):
            for d in (3 if lo else 1, 2):
                @pl.loop(0, 4)
                def _(a):
                    slab_wait(buf, n, a, turn(w, d, 4), lo)

    def slab_finish(buf, n):
        @pl.loop(0, 31)
        def _(t):
            slab_copy(buf, n, u, w, zlo, t, partner).wait_send()

    def blk_copy(src, dst, n, d):
        k = turn(c, d, PIECES)
        return rcopy(src.at[k], dst.at[:, :, pl.ds(pl.multiple_of(LANES * c, LANES), LANES)], blk_send.at[n, d],
                     blk_recv.at[n, c], col_dev(k))

    def blk_send_all(src, dst, n):
        @pl.loop(1, PIECES)
        def _(d):
            blk_copy(src, dst, n, d).start()

        dst[:, :, pl.ds(pl.multiple_of(LANES * c, LANES), LANES)] = src[c]

    def blk_finish(src, dst, n):
        @pl.loop(1, PIECES)
        def _(d):
            k = turn(c, d, PIECES)
            rcopy(src.at[0], dst.at[:, :, pl.ds(pl.multiple_of(LANES * k, LANES), LANES)], blk_send.at[n, d],
                  blk_recv.at[n, k], partner).wait_recv()
            blk_copy(src, dst, n, d).wait_send()

    def gather_finish(buf, halo, n):
        if n:
            for d in range(1, 4):
                rcopy(buf.at[0], buf.at[0], ag_send.at[n, d - 1], ag_recv.at[n, 0], partner).wait_send()
        for da in range(4):
            for d in (1, 2, 3) if n else (1, 3):
                gather_copy2(buf, n, da, d).wait_send()

        @pl.loop(0, PIECES)
        def _(t):
            for side in range(2):
                halo_copy(buf, halo, n, t, side).wait_send()

    def scatter_finish(src, land1, n):
        @pl.loop(0, 12)
        def _(t):
            rcopy(src.at[0], land1.at[0, 0], rs_send.at[n, t], rs_recv.at[n, 0], partner).wait_send()

    def smem_copy(n):
        return pltpu.make_async_copy(tables[n][1], tables[n][2], loc_sem.at[4 + n])

    for n in range(3):
        table_copy(n).wait()
        tabs[n].wait()
        smem_copy(n).start()
    for n in range(3):
        smem_copy(n).wait()

    def place_measured():
        @pl.loop(1, PIECES)
        def _(d):
            k = turn(c, d, PIECES)
            rcopy(msh.at[0], mbuf.at[k], m_send.at[d], m_recv.at[k], partner).wait_recv()

        for k in range(PIECES):
            rows = pl.ds(6 * (2 * (k // 4) + k % 2), 6)
            for e in range(2):
                for t in range(2):
                    wide[2 * ((k // 2) % 2) + e, t, rows, :] = mbuf[k, e, :, LANES * t:LANES * (t + 1)]

    def rows_of(blk):
        for k in range(PIECES):
            rows = pl.ds(6 * (2 * (k // 4) + k % 2), 6)
            for e in range(2):
                blk[k, e] = wide[2 * ((k // 2) % 2) + e, 0, rows, :]

    gather_project(xbuf, xhalo, 0, place_measured)
    for a in range(ANGLES):
        wide[a, 0] = wide[a, 0] - img[a, 0]
        wide[a, 1] = halo_mask(wide[a, 1] - img[a, 1])
    make_diff()

    back_scatter(part, rs1, 0, turn(u, 1, 4))
    rows_of(rblk)
    blk_send_all(rblk, rres, 0)
    own[...] = plane_sum(part, rs1, sum1, rs2, 0)
    gbuf[p] = own[...]
    gather_send1(gbuf, 1)
    swap_start(own, gslab, 0)
    img[...] = jnp.zeros_like(img)
    gather_project(gbuf, ghalo, 1, None)
    slab_wait(gslab, 0, u, w, zlo)
    slab_first(gslab, 0)

    norm = jnp.zeros((ROWS, LANES), F32)
    for a in range(ANGLES):
        mine = img[a, 0]
        wide[a, 0] = mine
        wide[a, 1] = halo_mask(img[a, 1])
        norm = norm + mine * mine
    make_diff()
    back_scatter(qpart, qrs1, 1, 0)
    slab_second(gslab, 0)
    owner_start(qpart, qrs1, qsum1, qland, 1)
    rows_of(iblk)
    q = owner_sum(qsum1, qland)
    qslab[pl.ds(3 * ylo, SLICES), :, pl.ds(pl.multiple_of(LANES * (4 * px + 2 * zlo + yhi), LANES), LANES)] = q
    slab_first(qslab, 1)

    tiles[...] = jnp.zeros_like(tiles)

    def down(v):
        return jnp.sum(v, axis=0, keepdims=True)

    g = own[...]
    tiles[0, 0:1, :] = down(jnp.sum(g * g, axis=0))
    tiles[0, 1:2, :] = down(norm)
    tiles[0, 2:3, :] = down(jnp.sum(q * q, axis=0))

    def sum_copy(land, n, d):
        at, dev = (
            (c, col_dev(turn(c, d, PIECES))),
            (px, plane_dev(4 * turn(px, d, 4) + py)),
            (py, plane_dev(4 * px + turn(py, d, 4))),
        )[n]
        return rcopy(tiles.at[n], land.at[at], sc_send.at[n, d], sc_recv.at[n, at], dev)

    def sum_start(land, n):
        @pl.loop(1, PIECES if n == 0 else 4)
        def _(d):
            sum_copy(land, n, d).start()

        land[(c, px, py)[n]] = tiles[n]

    def sum_finish(land, n):
        count = PIECES if n == 0 else 4

        @pl.loop(1, count)
        def _(d):
            k = turn((c, px, py)[n], d, count)
            rcopy(tiles.at[n], land.at[k], sc_send.at[n, d], sc_recv.at[n, k], partner).wait_recv()
            sum_copy(land, n, d).wait_send()

        total = land[0]
        for k in range(1, count):
            total = total + land[k]
        return total

    sum_start(sc1, 0)
    blk_send_all(iblk, ires, 1)
    slab_third(gslab, 0)
    slab_second(qslab, 1)
    tiles[1] = sum_finish(sc1, 0)
    sum_start(sc2, 1)
    slab_third(qslab, 1)
    tiles[2] = sum_finish(sc2, 1)
    sum_start(sc3, 2)
    slab_rest(gslab, 0)
    sums = jnp.sum(sum_finish(sc3, 2), axis=1, keepdims=True)
    gamma = sums[0:1]
    alpha = gamma / sums[1:2]
    scale = alpha * alpha * (sums[2:3] / gamma)

    blk_finish(rblk, rres, 0)
    blk_finish(iblk, ires, 1)
    for e in range(2):
        res_out[:, e, :] = rres[e] - alpha * ires[e]

    def out_copy(src, dst, n, i):
        return pltpu.make_async_copy(src.at[i], dst.at[i], out_sem.at[n, i])

    for i in range(6):
        volv[i] = xv[i] + alpha * gslab[i]
        out_copy(volv, vol_out, 0, i).start()
    slab_rest(qslab, 1)
    for i in range(6):
        dirv[i] = scale * gslab[i] - alpha * qslab[i]
        out_copy(dirv, dir_out, 1, i).start()

    @pl.loop(1, PIECES)
    def _(d):
        m_copy(d).wait_send()

    gather_finish(xbuf, xhalo, 0)
    gather_finish(gbuf, ghalo, 1)
    scatter_finish(part, rs1, 0)
    scatter_finish(qpart, qrs1, 1)
    for d in range(1, 4):
        scatter_copy2(sum1, rs2, 0, d).wait_send()
    owner_finish(qsum1, qland)
    slab_finish(gslab, 0)
    slab_finish(qslab, 1)
    pl.when(jnp.logical_not(is_me(owner_dev(px, py))))(lambda: swap_copy(own, gslab, 0).wait_send())
    x_each(lambda copy: copy.wait_send(), lambda copy: None)
    for i in range(6):
        out_copy(volv, vol_out, 0, i).wait()
        out_copy(dirv, dir_out, 1, i).wait()


def per_device(start_volume, measured, row_shift, col_shift, col_frac):
    piece = (SLICES, LINES, LANES)
    vmem = pltpu.VMEM
    dma = pltpu.SemaphoreType.DMA
    scratch = [
        vmem(start_volume.shape, F32), vmem(start_volume.shape, F32), vmem(start_volume.shape, F32),
        vmem(start_volume.shape, F32), vmem(start_volume.shape, F32),
        vmem((6, 2, X), F32),
        vmem((PIECES, 2, 6, 2 * LANES), F32),
        vmem((PIECES, 2, 6, 2 * LANES), F32),
        vmem((2, 2, 48), jnp.int32), vmem((2, 2, 48), jnp.int32), vmem((2, 2, 48), F32),
        pltpu.SMEM((2, 2, 48), jnp.int32), pltpu.SMEM((2, 2, 48), jnp.int32), pltpu.SMEM((2, 2, 48), F32),
        vmem((PIECES,) + piece, F32), vmem((PIECES, 2) + piece, F32),
        vmem((PIECES,) + piece, F32), vmem((PIECES, 2) + piece, F32),
        vmem((ANGLES * SLICES, 2, 3 * LINES, LANES), F32),
        vmem((ANGLES, 2, ROWS, LANES), F32),
        vmem((ANGLES, 2, ROWS, LANES), F32),
        vmem((ANGLES, 2, ROWS, LANES), F32),
        vmem((PIECES,) + piece, F32), vmem((3, 4) + piece, F32), vmem((4,) + piece, F32), vmem((3,) + piece, F32), vmem(piece, F32),
        vmem((PIECES,) + piece, F32), vmem((3, 4) + piece, F32), vmem((4,) + piece, F32), vmem((4,) + piece, F32),
        vmem((PIECES, 2, 6, LANES), F32), vmem((PIECES, 2, 6, LANES), F32),
        vmem(measured.shape, F32), vmem(measured.shape, F32),
        vmem((3, 8, LANES), F32), vmem((PIECES, 8, LANES), F32), vmem((4, 8, LANES), F32), vmem((4, 8, LANES), F32),
        dma((8,)), dma((3,)), dma((3,)), dma((PIECES,)), dma((PIECES,)), dma((4, 3)),
        dma((2, 15)), dma((2, PIECES)), dma((2, 2, PIECES)), dma((2, 2, PIECES)),
        dma((2, 12)), dma((2, 12)), dma((1, 3)), dma((1, 3)), dma((4,)), dma((4,)),
        dma((2, 32)), dma((2, 32)), dma((2, PIECES)), dma((2, PIECES)), dma((3, PIECES)), dma((3, PIECES)), dma((2, 6)),
    ]
    whole = pl.BlockSpec(memory_space=pltpu.VMEM)
    far = pl.BlockSpec(memory_space=pltpu.HBM)
    rows = jnp.transpose(measured, (1, 0, 2))
    volume, residual, direction = pl.pallas_call(
        kernel,
        out_shape=(
            jax.ShapeDtypeStruct(start_volume.shape, F32),
            jax.ShapeDtypeStruct(rows.shape, F32),
            jax.ShapeDtypeStruct(start_volume.shape, F32),
        ),
        in_specs=[far] * 5,
        out_specs=(far, whole, far),
        scratch_shapes=scratch,
        compiler_params=pltpu.CompilerParams(
            collective_id=0, has_side_effects=True, vmem_limit_bytes=60 * 2**20
        ),
    )(start_volume, rows, row_shift, col_shift, col_frac)
    return volume, jnp.transpose(residual, (1, 0, 2)), direction


def solution(mesh):
    return jax.shard_map(
        per_device,
        mesh=mesh,
        in_specs=(
            P("slab", None, None),
            P("ang", "slab", None),
            P("ang", None),
            P("ang", None),
            P("ang", None),
        ),
        out_specs=(P("slab", None, None), P("ang", "slab", None), P("slab", None, None)),
        check_vma=False,
    )
```

```python
import jax
import jax.numpy as jnp
from jax import lax
from jax.experimental import pallas as pl
from jax.experimental.pallas import tpu as pltpu
from jax.sharding import PartitionSpec as P

MESH = pl.DeviceIdType.MESH
F32 = jnp.float32
PIECES = 16
SLICES = 3
LINES = 24
ROWS = 48
ANGLES = 4
LANES = 128
X = 2048


def rcopy(src, dst, send, recv, dev):
    return pltpu.make_async_remote_copy(
        src_ref=src, dst_ref=dst, send_sem=send, recv_sem=recv, device_id=dev, device_id_type=MESH
    )


def lanes_of(shape):
    return lax.broadcasted_iota(jnp.int32, shape, len(shape) - 1)


def kernel(
    x_hbm, m_hbm, rt_ref, ct_ref, ft_ref,
    vol_out, res_out, dir_out,
    xv, volv, dirv, gslab, qslab, m_ref, msh, mbuf, rtv, ctv, ftv, rts, cts, fts,
    xbuf, xhalo, gbuf, ghalo, pad, img, wide, diff,
    part, rs1, sum1, rs2, own, qpart, qrs1, qsum1, qland,
    rblk, iblk, rres, ires, tiles, sc1, sc2, sc3,
    loc_sem, tab_send, tab_recv, m_send, m_recv, x_send,
    ag_send, ag_recv, hl_send, hl_recv,
    rs_send, rs_recv, rt_send, rt_recv, own_send, own_recv,
    sl_send, sl_recv, blk_send, blk_recv, sc_send, sc_recv, out_sem,
):
    ang = lax.axis_index("ang")
    slab = lax.axis_index("slab")
    p = lax.div(ang, 2)
    zlo = lax.rem(ang, 2)
    px = lax.div(p, 4)
    py = lax.rem(p, 4)
    zhi = lax.div(slab, 2)
    core = lax.rem(slab, 2)
    z = 2 * zhi + zlo
    c = 2 * z + core
    even = core == 0
    u = jnp.where(even, px, py)
    w = jnp.where(even, py, px)

    def pid(a, b):
        return jnp.where(even, 4 * a + b, 4 * b + a)

    def plane_dev(q):
        return (2 * q + zlo, slab)

    def col_dev(k):
        zz = lax.div(k, 2)
        return (2 * p + lax.rem(zz, 2), 2 * lax.div(zz, 2) + lax.rem(k, 2))

    def turn(v, d, n):
        return lax.rem(v + d, n)

    lane = lanes_of((8, LANES))
    exist = jnp.where(lane < 64, jnp.where(c < PIECES - 1, 1, 0), jnp.where(c > 0, 1, 0)) > 0
    me_dev = (ang, slab)

    def xy(a, b):
        return jnp.where(even, a, b), jnp.where(even, b, a)

    def is_me(dev):
        return jnp.logical_and(dev[0] == ang, dev[1] == slab)

    def apart(dev, then, here):
        pl.when(jnp.logical_not(is_me(dev)))(then)
        pl.when(is_me(dev))(here)

    def owner_dev(xx, yy):
        return (2 * (4 * zhi + 2 * core + lax.rem(yy, 2)) + zlo, 2 * xx + lax.div(yy, 2))

    partner = (2 * p + (1 - zlo), slab)
    yhi = lax.div(py, 2)
    ylo = lax.rem(py, 2)

    mload = pltpu.make_async_copy(m_hbm, m_ref, loc_sem.at[0])
    mload.start()
    tables = ((rt_ref, rtv, rts), (ct_ref, ctv, cts), (ft_ref, ftv, fts))

    def table_copy(n):
        return pltpu.make_async_copy(tables[n][0], tables[n][1].at[zlo], loc_sem.at[4 + n])

    for n in range(3):
        table_copy(n).start()
    xload = pltpu.make_async_copy(x_hbm, xv, loc_sem.at[1])
    xload.start()

    barrier = pltpu.get_barrier_semaphore()

    def greet(dev):
        pl.semaphore_signal(barrier, inc=1, device_id=dev, device_id_type=MESH)

    @pl.loop(1, PIECES)
    def _(d):
        greet(col_dev(turn(c, d, PIECES)))

    for d in range(1, 4):
        greet(plane_dev(pid(turn(u, d, 4), w)))
        greet(plane_dev(pid(u, turn(w, d, 4))))
    for a in range(4):
        greet((2 * pid(a, w) + 1 - zlo, slab))
    mine = 0
    for a in range(4):
        to = owner_dev(*xy(a, w))
        pl.when(jnp.logical_not(is_me(to)))(lambda to=to: greet(to))
        mine = mine + jnp.where(is_me(to), 1, 0)
        at_x, at_y = zhi, 2 * core + ylo
        come = (2 * jnp.where(yhi == 0, 4 * a + at_y, 4 * at_x + a) + zlo, 2 * px + yhi)
        pl.when(jnp.logical_not(is_me(come)))(lambda come=come: greet(come))

    lane6 = lanes_of((6, LANES))
    mload.wait()
    for a in range(2):
        for t in range(PIECES):
            here = m_ref[:, a, pl.ds(LANES * t, LANES)]
            right = m_ref[:, a, pl.ds(LANES * min(t + 1, 15), LANES)]
            left = m_ref[:, a, pl.ds(LANES * max(t - 1, 0), LANES)]
            msh[t, a, :, :LANES] = here
            msh[t, a, :, LANES:] = jnp.where(lane6 < 64, right, left)

    pad[...] = jnp.zeros_like(pad)
    img[...] = jnp.zeros_like(img)
    xload.wait()
    pl.semaphore_wait(barrier, 15 + 6 + 4 + 8 - 2 * mine)

    near = turn(zhi, 3 + 2 * zlo, 4)
    served = ((zhi, zlo), (near, 0), (near, 1), (turn(zhi, 2, 4), 1 - zlo))

    def x_each(act_far, act_here):
        for to, (to_hi, to_lo) in enumerate(served):
            for h in range(3):
                cc = 4 * to_hi + 2 * to_lo + (1 if h < 2 else 0)
                half = h if h < 2 else ylo
                k = 4 * zhi + 2 * core + half
                src = xv.at[pl.ds(3 * half, SLICES), :, pl.ds(pl.multiple_of(LANES * cc, LANES), LANES)]
                copy = rcopy(src, xbuf.at[k], x_send.at[to, h], ag_recv.at[0, k], col_dev(cc))
                local = pltpu.make_async_copy(src, xbuf.at[k], ag_recv.at[0, k])

                def act(copy=copy, local=local, cc=cc):
                    apart(col_dev(cc), lambda: act_far(copy), lambda: act_here(local))

                pl.when(zhi == px if h < 2 else core == yhi)(act)

    x_each(lambda copy: copy.start(), lambda copy: copy.start())

    tabs = []
    for n, (src, dst, _) in enumerate(tables):
        t = rcopy(src, dst.at[zlo], tab_send.at[n], tab_recv.at[n], partner)
        t.start()
        tabs.append(t)

    def m_copy(d):
        k = turn(c, d, PIECES)
        return rcopy(msh.at[k], mbuf.at[c], m_send.at[d], m_recv.at[c], col_dev(k))

    def m_start():
        @pl.loop(1, PIECES)
        def _(d):
            m_copy(d).start()

    mbuf[c] = msh[c]

    def step(q):
        return jnp.where(q < 2, q, 5 - q)

    def piece_order(t):
        late = t - 9
        dx = jnp.where(t < 9, step(lax.rem(t, 3)), jnp.where(late < 4, 2, step(late - 4)))
        dy = jnp.where(t < 9, step(lax.div(t, 3)), jnp.where(late < 4, step(late), 2))
        return 4 * turn(px, 4 - dx, 4) + turn(py, 4 - dy, 4)

    def gather_send1(buf, n):
        for d in range(1, 4):
            rcopy(buf.at[p], buf.at[p], ag_send.at[n, d - 1], ag_recv.at[n, p],
                  plane_dev(pid(turn(u, d, 4), w))).start()

    def gather_copy2(buf, n, da, d):
        k = pid(turn(u, 4 - da, 4), w)
        return rcopy(buf.at[k], buf.at[k], ag_send.at[n, 3 + 3 * da + d - 1], ag_recv.at[n, k],
                     plane_dev(pid(u, turn(w, d, 4))))

    def halo_copy(buf, halo, n, k, side):
        to = turn(c, 1 if side == 0 else PIECES - 1, PIECES)
        return rcopy(buf.at[k], halo.at[k, side], hl_send.at[n, side, k], hl_recv.at[n, side, k], col_dev(to))

    def halo_start(buf, halo, n, k):
        for side in range(2):
            halo_copy(buf, halo, n, k, side).start()

    def gather_wait(buf, n, k):
        rcopy(buf.at[k], buf.at[k], ag_send.at[n, 0], ag_recv.at[n, k], partner).wait_recv()

    tiles3 = (SLICES, 8, LANES)

    def project_piece(buf, halo, k):
        for s in range(SLICES):
            w0 = buf[k, s].reshape(tiles3)
            left = halo[k, 0, s].reshape(tiles3)
            right = halo[k, 1, s].reshape(tiles3)
            w1 = jnp.where(exist, jnp.where(lane < 64, right, left), 0.0)
            s0 = pltpu.roll(w0, 1, 2)
            s1 = pltpu.roll(w1, 1, 2)
            d0 = jnp.where(lane < 1, s1, s0) - w0
            d1 = jnp.where(lane < 1, s0, s1) - w1
            at = SLICES * k + s
            for a in range(ANGLES):
                f = fts[a // 2, a % 2, at]
                cs = cts[a // 2, a % 2, at]
                v0 = w0 + f * d0
                v1 = w1 + f * d1
                other = jnp.logical_or(lane >= LANES - cs, lane < -cs)
                sh = lax.rem(cs + LANES, LANES)
                full = (LINES, LANES)
                pad[SLICES * a + s, 0, pl.ds(LINES, LINES), :] = pltpu.roll(jnp.where(other, v1, v0), sh, 2).reshape(full)
                pad[SLICES * a + s, 1, pl.ds(LINES, LINES), :] = pltpu.roll(jnp.where(other, v0, v1), sh, 2).reshape(full)
        for a in range(ANGLES):
            for t in range(2):
                acc = img[a, t]
                for s in range(SLICES):
                    rs = rts[a // 2, a % 2, SLICES * k + s]
                    acc = acc + pad[SLICES * a + s, t, pl.ds(LINES - rs, ROWS), :]
                img[a, t] = acc

    def gather_project(buf, halo, n, during):
        for da in (0, 1, 3, 2):
            k = pid(turn(u, 4 - da, 4), w)
            if n == 0 or da:
                gather_wait(buf, n, k)
            for d in (2, 1, 3):
                gather_copy2(buf, n, da, d).start()
            halo_start(buf, halo, n, k)

        @pl.loop(0, 8)
        def _(t):
            k = pid(turn(u, 4 - step(lax.div(t, 2)), 4), turn(w, 3 - 2 * lax.rem(t, 2), 4))
            gather_wait(buf, n, k)
            halo_start(buf, halo, n, k)

        if n == 0:
            m_start()

        @pl.loop(0, PIECES)
        def _(t):
            if during is not None:
                pl.when(t == 10)(during)

            @pl.when(jnp.logical_and(t >= 4, t < 8))
            def _():
                k = pid(turn(u, 4 - step(t - 4), 4), turn(w, 2, 4))
                gather_wait(buf, n, k)
                halo_start(buf, halo, n, k)

            k = piece_order(t)
            for side in range(2):
                halo_copy(buf, halo, n, k, side).wait_recv()
            project_piece(buf, halo, k)

    def halo_mask(v):
        return jnp.where(exist, v.reshape(ROWS // 8, 8, LANES), 0.0).reshape(ROWS, LANES)

    def make_diff():
        last = lanes_of((ROWS, LANES)) == LANES - 1
        for a in range(ANGLES):
            v0 = wide[a, 0]
            v1 = wide[a, 1]
            s0 = pltpu.roll(v0, LANES - 1, 1)
            s1 = pltpu.roll(v1, LANES - 1, 1)
            diff[a, 0] = jnp.where(last, s1, s0) - v0
            diff[a, 1] = jnp.where(last, s0, s1) - v1

    def back_piece(dst, k):
        for s in range(SLICES):
            at = SLICES * k + s
            acc = None
            for a in range(ANGLES):
                rs = rts[a // 2, a % 2, at]
                cs = cts[a // 2, a % 2, at]
                f = fts[a // 2, a % 2, at]
                other = jnp.logical_or(lane < cs, lane >= LANES + cs)

                def rows_at(ref, t):
                    return ref[a, t, pl.ds(rs, LINES), :].reshape(tiles3)

                v = jnp.where(other, rows_at(wide, 1), rows_at(wide, 0))
                e = jnp.where(other, rows_at(diff, 1), rows_at(diff, 0))
                term = pltpu.roll(v + f * e, lax.rem(LANES - cs, LANES), 2)
                acc = term if acc is None else acc + term
            dst[k, s] = acc.reshape(LINES, LANES)

    def scatter_copy1(src, land, n, d, a):
        return rcopy(src.at[pid(a, turn(w, d, 4))], land.at[d - 1, a], rs_send.at[n, 4 * (d - 1) + a],
                     rs_recv.at[n, 4 * (d - 1) + a], plane_dev(pid(u, turn(w, d, 4))))

    def scatter_copy2(src, dst, n, d):
        a = turn(u, d, 4)
        return rcopy(src.at[a], dst.at[d - 1], rt_send.at[n, d - 1], rt_recv.at[n, d - 1], plane_dev(pid(a, w)))

    def back_scatter(dst, land, n, first):
        @pl.loop(0, PIECES)
        def _(t):
            i = lax.rem(t, 3)
            d = jnp.where(t >= 12, 0, jnp.where(i == 0, 2, 2 * i - 1))
            a = turn(first, jnp.where(t >= 12, t - 12, lax.div(t, 3)), 4)
            back_piece(dst, pid(a, turn(w, d, 4)))

            @pl.when(t < 12)
            def _():
                scatter_copy1(dst, land, n, d, a).start()

    def line_sum(dst, land, n, a):
        total = dst[pid(a, w)]
        for d in (1, 3, 2):
            scatter_copy1(dst, land, n, d, a).wait_recv()
            total = total + land[d - 1, a]
        return total

    def plane_sum(dst, land, total1, land2, n):
        for da in (1, 2, 3, 0):
            a = turn(u, da, 4)
            total1[a] = line_sum(dst, land, n, a)
            if da:
                scatter_copy2(total1, land2, n, da).start()
        total = total1[u]
        for d in (1, 3, 2):
            scatter_copy2(total1, land2, n, d).wait_recv()
            total = total + land2[d - 1]
        return total

    def owner_copy(a, total1, land):
        return rcopy(total1.at[a], land.at[u], own_send.at[a], own_recv.at[u], owner_dev(*xy(a, w)))

    def owner_start(dst, land1, total1, land, n):
        for a in range(4):
            total1[a] = line_sum(dst, land1, n, a)
            copy = owner_copy(a, total1, land)
            local = pltpu.make_async_copy(total1.at[a], land.at[u], own_recv.at[u])
            apart(owner_dev(*xy(a, w)), lambda: copy.start(), lambda: local.start())

    def owner_sum(total1, land):
        total = None
        for a in range(4):
            rcopy(total1.at[0], land.at[a], own_send.at[0], own_recv.at[a], partner).wait_recv()
            total = land[a] if total is None else total + land[a]
        return total

    def owner_finish(total1, land):
        for a in range(4):
            copy = owner_copy(a, total1, land)
            pl.when(jnp.logical_not(is_me(owner_dev(*xy(a, w)))))(lambda: copy.wait_send())

    def slab_at(buf, h, block):
        return buf.at[pl.ds(3 * h, SLICES), :, pl.ds(pl.multiple_of(LANES * block, LANES), LANES)]

    def slab_piece(buf, xx, yy, lo):
        return slab_at(buf, lax.rem(yy, 2), 4 * xx + 2 * lo + lax.div(yy, 2))

    def slab_copy(buf, n, a, b, lo, slot, dev):
        xx, yy = xy(a, b)
        ref = slab_piece(buf, xx, yy, lo)
        return rcopy(ref, ref, sl_send.at[n, slot], sl_recv.at[n, 2 * (4 * xx + yy) + lo], dev)

    def second_dev(d):
        return plane_dev(pid(u, turn(w, d, 4)))

    def slab_wait(buf, n, a, b, lo):
        slab_copy(buf, n, a, b, lo, 0, partner).wait_recv()

    def swap_copy(src, buf, n):
        return rcopy(src, slab_at(buf, ylo, c), sl_send.at[n, 31],
                     sl_recv.at[n, 2 * (4 * zhi + 2 * core + ylo) + zlo], owner_dev(px, py))

    def swap_start(src, buf, n):
        local = pltpu.make_async_copy(src, slab_at(buf, ylo, c), sl_recv.at[n, 2 * (4 * zhi + 2 * core + ylo) + zlo])
        apart(owner_dev(px, py), lambda: swap_copy(src, buf, n).start(), lambda: local.start())

    def slab_near(buf, n, a, lo, slot):
        slab_copy(buf, n, a, w, lo, slot, second_dev(1)).start()
        slab_copy(buf, n, a, w, lo, slot + 1, second_dev(3)).start()

    def slab_first(buf, n):
        for i, d in enumerate((2, 1, 3)):
            slab_copy(buf, n, u, w, zlo, i, plane_dev(pid(turn(u, d, 4), w))).start()
        slab_near(buf, n, u, zlo, 7)
        for i, d in enumerate((2, 1, 3, 0)):
            slab_copy(buf, n, u, w, zlo, 3 + i, (2 * pid(turn(u, d, 4), w) + 1 - zlo, slab)).start()

    def slab_second(buf, n):
        for i, d in enumerate((1, 3, 2)):
            a = turn(u, d, 4)
            slab_wait(buf, n, a, w, zlo)
            slab_near(buf, n, a, zlo, 9 + 2 * i)
        for i, d in enumerate((0, 1, 3, 2)):
            a = turn(u, d, 4)
            slab_wait(buf, n, a, w, 1 - zlo)
            slab_near(buf, n, a, 1 - zlo, 15 + 2 * i)

    def slab_third(buf, n):
        for i, d in enumerate((0, 1, 3, 2)):
            a = turn(u, d, 4)
            slab_wait(buf, n, a, turn(w, 3, 4), 0)
            slab_copy(buf, n, a, turn(w, 3, 4), 0, 23 + 2 * i, second_dev(1)).start()
            slab_wait(buf, n, a, turn(w, 1, 4), 1)
            slab_copy(buf, n, a, turn(w, 1, 4), 1, 24 + 2 * i, second_dev(3)).start()

    def slab_rest(buf, n):
        for lo in range(2):
            for d in (3 if lo else 1, 2):
                @pl.loop(0, 4)
                def _(a):
                    slab_wait(buf, n, a, turn(w, d, 4), lo)

    def slab_finish(buf, n):
        @pl.loop(0, 31)
        def _(t):
            slab_copy(buf, n, u, w, zlo, t, partner).wait_send()

    def blk_copy(src, dst, n, d):
        k = turn(c, d, PIECES)
        return rcopy(src.at[k], dst.at[:, :, pl.ds(pl.multiple_of(LANES * c, LANES), LANES)], blk_send.at[n, d],
                     blk_recv.at[n, c], col_dev(k))

    def blk_send_all(src, dst, n):
        @pl.loop(1, PIECES)
        def _(d):
            blk_copy(src, dst, n, d).start()

        dst[:, :, pl.ds(pl.multiple_of(LANES * c, LANES), LANES)] = src[c]

    def blk_finish(src, dst, n):
        @pl.loop(1, PIECES)
        def _(d):
            k = turn(c, d, PIECES)
            rcopy(src.at[0], dst.at[:, :, pl.ds(pl.multiple_of(LANES * k, LANES), LANES)], blk_send.at[n, d],
                  blk_recv.at[n, k], partner).wait_recv()
            blk_copy(src, dst, n, d).wait_send()

    def gather_finish(buf, halo, n):
        if n:
            for d in range(1, 4):
                rcopy(buf.at[0], buf.at[0], ag_send.at[n, d - 1], ag_recv.at[n, 0], partner).wait_send()
        for da in range(4):
            for d in (1, 2, 3):
                gather_copy2(buf, n, da, d).wait_send()

        @pl.loop(0, PIECES)
        def _(t):
            for side in range(2):
                halo_copy(buf, halo, n, t, side).wait_send()

    def scatter_finish(src, land1, n):
        @pl.loop(0, 12)
        def _(t):
            rcopy(src.at[0], land1.at[0, 0], rs_send.at[n, t], rs_recv.at[n, 0], partner).wait_send()

    def smem_copy(n):
        return pltpu.make_async_copy(tables[n][1], tables[n][2], loc_sem.at[4 + n])

    for n in range(3):
        table_copy(n).wait()
        tabs[n].wait()
        smem_copy(n).start()
    for n in range(3):
        smem_copy(n).wait()

    def place_measured():
        @pl.loop(1, PIECES)
        def _(d):
            k = turn(c, d, PIECES)
            rcopy(msh.at[0], mbuf.at[k], m_send.at[d], m_recv.at[k], partner).wait_recv()

        for k in range(PIECES):
            rows = pl.ds(6 * (2 * (k // 4) + k % 2), 6)
            for e in range(2):
                for t in range(2):
                    wide[2 * ((k // 2) % 2) + e, t, rows, :] = mbuf[k, e, :, LANES * t:LANES * (t + 1)]

    def rows_of(blk):
        for k in range(PIECES):
            rows = pl.ds(6 * (2 * (k // 4) + k % 2), 6)
            for e in range(2):
                blk[k, e] = wide[2 * ((k // 2) % 2) + e, 0, rows, :]

    gather_project(xbuf, xhalo, 0, place_measured)
    for a in range(ANGLES):
        wide[a, 0] = wide[a, 0] - img[a, 0]
        wide[a, 1] = halo_mask(wide[a, 1] - img[a, 1])
    make_diff()

    back_scatter(part, rs1, 0, turn(u, 1, 4))
    rows_of(rblk)
    blk_send_all(rblk, rres, 0)
    own[...] = plane_sum(part, rs1, sum1, rs2, 0)
    gbuf[p] = own[...]
    gather_send1(gbuf, 1)
    swap_start(own, gslab, 0)
    img[...] = jnp.zeros_like(img)
    gather_project(gbuf, ghalo, 1, None)
    slab_wait(gslab, 0, u, w, zlo)
    slab_first(gslab, 0)

    norm = jnp.zeros((ROWS, LANES), F32)
    for a in range(ANGLES):
        mine = img[a, 0]
        wide[a, 0] = mine
        wide[a, 1] = halo_mask(img[a, 1])
        norm = norm + mine * mine
    make_diff()
    back_scatter(qpart, qrs1, 1, 0)

    tiles[...] = jnp.zeros_like(tiles)

    def down(v):
        return jnp.sum(v, axis=0, keepdims=True)

    def sum_copy(set_, n, d):
        at, dev, land = (
            (c, col_dev(turn(c, d, PIECES)), sc1),
            (px, plane_dev(4 * turn(px, d, 4) + py), sc2),
            (py, plane_dev(4 * px + turn(py, d, 4)), sc3),
        )[n]
        return rcopy(tiles.at[set_, n], land.at[set_, at], sc_send.at[set_, n, d], sc_recv.at[set_, n, at], dev)

    def sum_start(set_, n):
        @pl.loop(1, PIECES if n == 0 else 4)
        def _(d):
            sum_copy(set_, n, d).start()

        (sc1, sc2, sc3)[n][set_, (c, px, py)[n]] = tiles[set_, n]

    def sum_finish(set_, n):
        count = PIECES if n == 0 else 4
        land = (sc1, sc2, sc3)[n]

        @pl.loop(1, count)
        def _(d):
            k = turn((c, px, py)[n], d, count)
            rcopy(tiles.at[set_, n], land.at[set_, k], sc_send.at[set_, n, d], sc_recv.at[set_, n, k], partner).wait_recv()
            sum_copy(set_, n, d).wait_send()

        total = land[set_, 0]
        for k in range(1, count):
            total = total + land[set_, k]
        return total

    def sum_step(set_, n):
        tiles[set_, n + 1] = sum_finish(set_, n)
        sum_start(set_, n + 1)

    g = gbuf[p]
    tiles[0, 0, 0:1, :] = down(jnp.sum(g * g, axis=0))
    tiles[0, 0, 1:2, :] = down(norm)
    sum_start(0, 0)
    slab_second(gslab, 0)
    owner_start(qpart, qrs1, qsum1, qland, 1)
    sum_step(0, 0)
    rows_of(iblk)

    @pl.loop(1, PIECES)
    def _(d):
        m_copy(d).wait_send()

    gather_finish(xbuf, xhalo, 0)
    gather_finish(gbuf, ghalo, 1)
    scatter_finish(part, rs1, 0)
    for d in range(1, 4):
        scatter_copy2(sum1, rs2, 0, d).wait_send()
    x_each(lambda copy: copy.wait_send(), lambda copy: None)
    q = owner_sum(qsum1, qland)
    qslab[pl.ds(3 * ylo, SLICES), :, pl.ds(pl.multiple_of(LANES * (4 * px + 2 * zlo + yhi), LANES), LANES)] = q
    slab_first(qslab, 1)
    tiles[1, 0, 0:1, :] = down(jnp.sum(q * q, axis=0))
    sum_start(1, 0)
    blk_send_all(iblk, ires, 1)
    sum_step(0, 1)
    slab_third(gslab, 0)
    slab_second(qslab, 1)
    sum_step(1, 0)
    scatter_finish(qpart, qrs1, 1)
    owner_finish(qsum1, qland)
    sums = jnp.sum(sum_finish(0, 2), axis=1, keepdims=True)
    gamma = sums[0:1]
    alpha = gamma / sums[1:2]
    slab_third(qslab, 1)
    sum_step(1, 1)

    blk_finish(rblk, rres, 0)
    blk_finish(iblk, ires, 1)
    for e in range(2):
        res_out[:, e, :] = rres[e] - alpha * ires[e]

    def out_copy(src, dst, n, i):
        return pltpu.make_async_copy(src.at[i], dst.at[i], out_sem.at[n, i])

    slab_rest(gslab, 0)
    for i in range(6):
        volv[i] = xv[i] + alpha * gslab[i]
        out_copy(volv, vol_out, 0, i).start()
    scale = alpha * alpha * (jnp.sum(sum_finish(1, 2), axis=1, keepdims=True)[0:1] / gamma)
    slab_rest(qslab, 1)
    for i in range(6):
        dirv[i] = scale * gslab[i] - alpha * qslab[i]
        out_copy(dirv, dir_out, 1, i).start()

    slab_finish(gslab, 0)
    slab_finish(qslab, 1)
    pl.when(jnp.logical_not(is_me(owner_dev(px, py))))(lambda: swap_copy(own, gslab, 0).wait_send())
    for i in range(6):
        out_copy(volv, vol_out, 0, i).wait()
        out_copy(dirv, dir_out, 1, i).wait()


def per_device(start_volume, measured, row_shift, col_shift, col_frac):
    piece = (SLICES, LINES, LANES)
    vmem = pltpu.VMEM
    dma = pltpu.SemaphoreType.DMA
    scratch = [
        vmem(start_volume.shape, F32), vmem(start_volume.shape, F32), vmem(start_volume.shape, F32),
        vmem(start_volume.shape, F32), vmem(start_volume.shape, F32),
        vmem((6, 2, X), F32),
        vmem((PIECES, 2, 6, 2 * LANES), F32),
        vmem((PIECES, 2, 6, 2 * LANES), F32),
        vmem((2, 2, 48), jnp.int32), vmem((2, 2, 48), jnp.int32), vmem((2, 2, 48), F32),
        pltpu.SMEM((2, 2, 48), jnp.int32), pltpu.SMEM((2, 2, 48), jnp.int32), pltpu.SMEM((2, 2, 48), F32),
        vmem((PIECES,) + piece, F32), vmem((PIECES, 2) + piece, F32),
        vmem((PIECES,) + piece, F32), vmem((PIECES, 2) + piece, F32),
        vmem((ANGLES * SLICES, 2, 3 * LINES, LANES), F32),
        vmem((ANGLES, 2, ROWS, LANES), F32),
        vmem((ANGLES, 2, ROWS, LANES), F32),
        vmem((ANGLES, 2, ROWS, LANES), F32),
        vmem((PIECES,) + piece, F32), vmem((3, 4) + piece, F32), vmem((4,) + piece, F32), vmem((3,) + piece, F32), vmem(piece, F32),
        vmem((PIECES,) + piece, F32), vmem((3, 4) + piece, F32), vmem((4,) + piece, F32), vmem((4,) + piece, F32),
        vmem((PIECES, 2, 6, LANES), F32), vmem((PIECES, 2, 6, LANES), F32),
        vmem(measured.shape, F32), vmem(measured.shape, F32),
        vmem((2, 3, 8, LANES), F32), vmem((2, PIECES, 8, LANES), F32), vmem((2, 4, 8, LANES), F32), vmem((2, 4, 8, LANES), F32),
        dma((8,)), dma((3,)), dma((3,)), dma((PIECES,)), dma((PIECES,)), dma((4, 3)),
        dma((2, 15)), dma((2, PIECES)), dma((2, 2, PIECES)), dma((2, 2, PIECES)),
        dma((2, 12)), dma((2, 12)), dma((1, 3)), dma((1, 3)), dma((4,)), dma((4,)),
        dma((2, 32)), dma((2, 32)), dma((2, PIECES)), dma((2, PIECES)), dma((2, 3, PIECES)), dma((2, 3, PIECES)), dma((2, 6)),
    ]
    whole = pl.BlockSpec(memory_space=pltpu.VMEM)
    far = pl.BlockSpec(memory_space=pltpu.HBM)
    rows = jnp.transpose(measured, (1, 0, 2))
    volume, residual, direction = pl.pallas_call(
        kernel,
        out_shape=(
            jax.ShapeDtypeStruct(start_volume.shape, F32),
            jax.ShapeDtypeStruct(rows.shape, F32),
            jax.ShapeDtypeStruct(start_volume.shape, F32),
        ),
        in_specs=[far] * 5,
        out_specs=(far, whole, far),
        scratch_shapes=scratch,
        compiler_params=pltpu.CompilerParams(
            collective_id=0, has_side_effects=True, vmem_limit_bytes=60 * 2**20
        ),
    )(start_volume, rows, row_shift, col_shift, col_frac)
    return volume, jnp.transpose(residual, (1, 0, 2)), direction


def solution(mesh):
    return jax.shard_map(
        per_device,
        mesh=mesh,
        in_specs=(
            P("slab", None, None),
            P("ang", "slab", None),
            P("ang", None),
            P("ang", None),
            P("ang", None),
        ),
        out_specs=(P("slab", None, None), P("ang", "slab", None), P("slab", None, None)),
        check_vma=False,
    )
```

```python
import jax
import jax.numpy as jnp
from jax import lax
from jax.experimental import pallas as pl
from jax.experimental.pallas import tpu as pltpu
from jax.sharding import PartitionSpec as P

MESH = pl.DeviceIdType.MESH
F32 = jnp.float32
PIECES = 16
SLICES = 3
LINES = 24
ROWS = 48
ANGLES = 4
LANES = 128
X = 2048


def rcopy(src, dst, send, recv, dev):
    return pltpu.make_async_remote_copy(
        src_ref=src, dst_ref=dst, send_sem=send, recv_sem=recv, device_id=dev, device_id_type=MESH
    )


def lanes_of(shape):
    return lax.broadcasted_iota(jnp.int32, shape, len(shape) - 1)


def kernel(
    x_hbm, m_hbm, rt_ref, ct_ref, ft_ref,
    vol_out, res_out, dir_out,
    xv, volv, dirv, gslab, qslab, m_ref, msh, mbuf, rtv, ctv, ftv, rts, cts, fts,
    xbuf, xhalo, gbuf, ghalo, pad, img, wide, diff,
    part, rs1, sum1, rs2, own, qpart, qrs1, qsum1, qland,
    rblk, iblk, rres, ires, tiles, sc1, sc2, sc3,
    loc_sem, tab_send, tab_recv, tab_loc, m_send, m_recv, x_send,
    ag_send, ag_recv, hl_send, hl_recv,
    rs_send, rs_recv, rt_send, rt_recv, own_send, own_recv,
    sl_send, sl_recv, blk_send, blk_recv, sc_send, sc_recv, out_sem,
):
    ang = lax.axis_index("ang")
    slab = lax.axis_index("slab")
    p = lax.div(ang, 2)
    zlo = lax.rem(ang, 2)
    px = lax.div(p, 4)
    py = lax.rem(p, 4)
    zhi = lax.div(slab, 2)
    core = lax.rem(slab, 2)
    z = 2 * zhi + zlo
    c = 2 * z + core
    even = core == 0
    u = jnp.where(even, px, py)
    w = jnp.where(even, py, px)

    def pid(a, b):
        return jnp.where(even, 4 * a + b, 4 * b + a)

    def plane_dev(q):
        return (2 * q + zlo, slab)

    def col_dev(k):
        zz = lax.div(k, 2)
        return (2 * p + lax.rem(zz, 2), 2 * lax.div(zz, 2) + lax.rem(k, 2))

    def turn(v, d, n):
        return lax.rem(v + d, n)

    lane = lanes_of((8, LANES))
    exist = jnp.where(lane < 64, jnp.where(c < PIECES - 1, 1, 0), jnp.where(c > 0, 1, 0)) > 0
    me_dev = (ang, slab)

    def xy(a, b):
        return jnp.where(even, a, b), jnp.where(even, b, a)

    def is_me(dev):
        return jnp.logical_and(dev[0] == ang, dev[1] == slab)

    def apart(dev, then, here):
        pl.when(jnp.logical_not(is_me(dev)))(then)
        pl.when(is_me(dev))(here)

    def owner_dev(xx, yy):
        return (2 * (4 * zhi + 2 * core + lax.rem(yy, 2)) + zlo, 2 * xx + lax.div(yy, 2))

    partner = (2 * p + (1 - zlo), slab)
    yhi = lax.div(py, 2)
    ylo = lax.rem(py, 2)

    tables = ((rt_ref, rtv, rts), (ct_ref, ctv, cts), (ft_ref, ftv, fts))

    def table_copy(n):
        return pltpu.make_async_copy(tables[n][0], tables[n][2].at[zlo], loc_sem.at[4 + n])

    barrier = pltpu.get_barrier_semaphore()

    def greet(dev):
        pl.semaphore_signal(barrier, inc=1, device_id=dev, device_id_type=MESH)

    @pl.loop(1, PIECES)
    def _(d):
        greet(col_dev(turn(c, d, PIECES)))

    for d in range(1, 4):
        greet(plane_dev(pid(turn(u, d, 4), w)))
        greet(plane_dev(pid(u, turn(w, d, 4))))
    for a in range(4):
        greet((2 * pid(a, w) + 1 - zlo, slab))
    mine = 0
    for a in range(4):
        to = owner_dev(*xy(a, w))
        pl.when(jnp.logical_not(is_me(to)))(lambda to=to: greet(to))
        mine = mine + jnp.where(is_me(to), 1, 0)
        at_x, at_y = zhi, 2 * core + ylo
        come = (2 * jnp.where(yhi == 0, 4 * a + at_y, 4 * at_x + a) + zlo, 2 * px + yhi)
        pl.when(jnp.logical_not(is_me(come)))(lambda come=come: greet(come))

    mload = pltpu.make_async_copy(m_hbm, m_ref, loc_sem.at[0])
    mload.start()
    for n in range(3):
        table_copy(n).start()
    xload = pltpu.make_async_copy(x_hbm, xv, loc_sem.at[1])
    xload.start()

    pad[...] = jnp.zeros_like(pad)
    img[...] = jnp.zeros_like(img)
    xload.wait()
    pl.semaphore_wait(barrier, 15 + 6 + 4 + 8 - 2 * mine)

    tabs = []
    for n, (src, dst, _) in enumerate(tables):
        t = rcopy(src, dst, tab_send.at[n], tab_recv.at[n], partner)
        t.start()
        tabs.append(t)

    near = turn(zhi, 3 + 2 * zlo, 4)
    served = ((zhi, zlo), (near, 0), (near, 1), (turn(zhi, 2, 4), 1 - zlo))

    def x_each(act_far, act_here):
        for to, (to_hi, to_lo) in enumerate(served):
            for h in range(3):
                cc = 4 * to_hi + 2 * to_lo + (1 if h < 2 else 0)
                half = h if h < 2 else ylo
                k = 4 * zhi + 2 * core + half
                src = xv.at[pl.ds(3 * half, SLICES), :, pl.ds(pl.multiple_of(LANES * cc, LANES), LANES)]
                copy = rcopy(src, xbuf.at[k], x_send.at[to, h], ag_recv.at[0, k], col_dev(cc))
                local = pltpu.make_async_copy(src, xbuf.at[k], ag_recv.at[0, k])

                def act(copy=copy, local=local, cc=cc):
                    apart(col_dev(cc), lambda: act_far(copy), lambda: act_here(local))

                pl.when(zhi == px if h < 2 else core == yhi)(act)

    x_each(lambda copy: copy.start(), lambda copy: copy.start())

    lane6 = lanes_of((6, LANES))
    mload.wait()
    for a in range(2):
        for t in range(PIECES):
            here = m_ref[:, a, pl.ds(LANES * t, LANES)]
            right = m_ref[:, a, pl.ds(LANES * min(t + 1, 15), LANES)]
            left = m_ref[:, a, pl.ds(LANES * max(t - 1, 0), LANES)]
            msh[t, a, :, :LANES] = here
            msh[t, a, :, LANES:] = jnp.where(lane6 < 64, right, left)

    def m_copy(d):
        k = turn(c, d, PIECES)
        return rcopy(msh.at[k], mbuf.at[c], m_send.at[d], m_recv.at[c], col_dev(k))

    def m_start():
        @pl.loop(1, PIECES)
        def _(d):
            m_copy(d).start()

    mbuf[c] = msh[c]

    def step(q):
        return jnp.where(q < 2, q, 5 - q)

    def piece_order(t):
        late = t - 9
        dx = jnp.where(t < 9, step(lax.rem(t, 3)), jnp.where(late < 4, 2, step(late - 4)))
        dy = jnp.where(t < 9, step(lax.div(t, 3)), jnp.where(late < 4, step(late), 2))
        return 4 * turn(px, 4 - dx, 4) + turn(py, 4 - dy, 4)

    def gather_send1(buf, n):
        for d in range(1, 4):
            rcopy(buf.at[p], buf.at[p], ag_send.at[n, d - 1], ag_recv.at[n, p],
                  plane_dev(pid(turn(u, d, 4), w))).start()

    def gather_copy2(buf, n, da, d):
        k = pid(turn(u, 4 - da, 4), w)
        return rcopy(buf.at[k], buf.at[k], ag_send.at[n, 3 + 3 * da + d - 1], ag_recv.at[n, k],
                     plane_dev(pid(u, turn(w, d, 4))))

    def halo_copy(buf, halo, n, k, side):
        to = turn(c, 1 if side == 0 else PIECES - 1, PIECES)
        return rcopy(buf.at[k], halo.at[k, side], hl_send.at[n, side, k], hl_recv.at[n, side, k], col_dev(to))

    def halo_start(buf, halo, n, k):
        for side in range(2):
            halo_copy(buf, halo, n, k, side).start()

    def gather_wait(buf, n, k):
        rcopy(buf.at[k], buf.at[k], ag_send.at[n, 0], ag_recv.at[n, k], partner).wait_recv()

    tiles3 = (SLICES, 8, LANES)

    def project_piece(buf, halo, k):
        for s in range(SLICES):
            w0 = buf[k, s].reshape(tiles3)
            left = halo[k, 0, s].reshape(tiles3)
            right = halo[k, 1, s].reshape(tiles3)
            w1 = jnp.where(exist, jnp.where(lane < 64, right, left), 0.0)
            s0 = pltpu.roll(w0, 1, 2)
            s1 = pltpu.roll(w1, 1, 2)
            d0 = jnp.where(lane < 1, s1, s0) - w0
            d1 = jnp.where(lane < 1, s0, s1) - w1
            at = SLICES * k + s
            for a in range(ANGLES):
                f = fts[a // 2, a % 2, at]
                cs = cts[a // 2, a % 2, at]
                v0 = w0 + f * d0
                v1 = w1 + f * d1
                other = jnp.logical_or(lane >= LANES - cs, lane < -cs)
                sh = lax.rem(cs + LANES, LANES)
                full = (LINES, LANES)
                pad[SLICES * a + s, 0, pl.ds(LINES, LINES), :] = pltpu.roll(jnp.where(other, v1, v0), sh, 2).reshape(full)
                pad[SLICES * a + s, 1, pl.ds(LINES, LINES), :] = pltpu.roll(jnp.where(other, v0, v1), sh, 2).reshape(full)
        for a in range(ANGLES):
            for t in range(2):
                acc = img[a, t]
                for s in range(SLICES):
                    rs = rts[a // 2, a % 2, SLICES * k + s]
                    acc = acc + pad[SLICES * a + s, t, pl.ds(LINES - rs, ROWS), :]
                img[a, t] = acc

    def smem_copy(n):
        return pltpu.make_async_copy(tables[n][1], tables[n][2].at[1 - zlo], tab_loc.at[n])

    def gather_project(buf, halo, n, during):
        for da in (0, 1, 3, 2):
            k = pid(turn(u, 4 - da, 4), w)
            if n == 0 or da:
                gather_wait(buf, n, k)
            for d in (2, 1, 3):
                gather_copy2(buf, n, da, d).start()
            halo_start(buf, halo, n, k)

        if n == 0:
            for i in range(3):
                tabs[i].wait()
                smem_copy(i).start()

        @pl.loop(0, 8)
        def _(t):
            k = pid(turn(u, 4 - step(lax.div(t, 2)), 4), turn(w, 3 - 2 * lax.rem(t, 2), 4))
            gather_wait(buf, n, k)
            halo_start(buf, halo, n, k)

        if n == 0:
            m_start()
            for i in range(3):
                smem_copy(i).wait()
                table_copy(i).wait()

        @pl.loop(0, PIECES)
        def _(t):
            if during is not None:
                pl.when(t == 10)(during)

            @pl.when(jnp.logical_and(t >= 4, t < 8))
            def _():
                k = pid(turn(u, 4 - step(t - 4), 4), turn(w, 2, 4))
                gather_wait(buf, n, k)
                halo_start(buf, halo, n, k)

            k = piece_order(t)
            for side in range(2):
                halo_copy(buf, halo, n, k, side).wait_recv()
            project_piece(buf, halo, k)

    def halo_mask(v):
        return jnp.where(exist, v.reshape(ROWS // 8, 8, LANES), 0.0).reshape(ROWS, LANES)

    def make_diff():
        last = lanes_of((ROWS, LANES)) == LANES - 1
        for a in range(ANGLES):
            v0 = wide[a, 0]
            v1 = wide[a, 1]
            s0 = pltpu.roll(v0, LANES - 1, 1)
            s1 = pltpu.roll(v1, LANES - 1, 1)
            diff[a, 0] = jnp.where(last, s1, s0) - v0
            diff[a, 1] = jnp.where(last, s0, s1) - v1

    def back_piece(dst, k):
        for s in range(SLICES):
            at = SLICES * k + s
            acc = None
            for a in range(ANGLES):
                rs = rts[a // 2, a % 2, at]
                cs = cts[a // 2, a % 2, at]
                f = fts[a // 2, a % 2, at]
                other = jnp.logical_or(lane < cs, lane >= LANES + cs)

                def rows_at(ref, t):
                    return ref[a, t, pl.ds(rs, LINES), :].reshape(tiles3)

                v = jnp.where(other, rows_at(wide, 1), rows_at(wide, 0))
                e = jnp.where(other, rows_at(diff, 1), rows_at(diff, 0))
                term = pltpu.roll(v + f * e, lax.rem(LANES - cs, LANES), 2)
                acc = term if acc is None else acc + term
            dst[k, s] = acc.reshape(LINES, LANES)

    def scatter_copy1(src, land, n, d, a):
        return rcopy(src.at[pid(a, turn(w, d, 4))], land.at[d - 1, a], rs_send.at[n, 4 * (d - 1) + a],
                     rs_recv.at[n, 4 * (d - 1) + a], plane_dev(pid(u, turn(w, d, 4))))

    def scatter_copy2(src, dst, n, d):
        a = turn(u, d, 4)
        return rcopy(src.at[a], dst.at[d - 1], rt_send.at[n, d - 1], rt_recv.at[n, d - 1], plane_dev(pid(a, w)))

    def back_scatter(dst, land, n, first):
        @pl.loop(0, PIECES)
        def _(t):
            i = lax.rem(t, 3)
            d = jnp.where(t >= 12, 0, jnp.where(i == 0, 2, 2 * i - 1))
            a = turn(first, jnp.where(t >= 12, t - 12, lax.div(t, 3)), 4)
            back_piece(dst, pid(a, turn(w, d, 4)))

            @pl.when(t < 12)
            def _():
                scatter_copy1(dst, land, n, d, a).start()

    def line_sum(dst, land, n, a):
        total = dst[pid(a, w)]
        for d in (1, 3, 2):
            scatter_copy1(dst, land, n, d, a).wait_recv()
            total = total + land[d - 1, a]
        return total

    def plane_sum(dst, land, total1, land2, n):
        for da in (1, 2, 3, 0):
            a = turn(u, da, 4)
            total1[a] = line_sum(dst, land, n, a)
            if da:
                scatter_copy2(total1, land2, n, da).start()
        total = total1[u]
        for d in (1, 3, 2):
            scatter_copy2(total1, land2, n, d).wait_recv()
            total = total + land2[d - 1]
        return total

    def owner_copy(a, total1, land):
        return rcopy(total1.at[a], land.at[u], own_send.at[a], own_recv.at[u], owner_dev(*xy(a, w)))

    def owner_start(dst, land1, total1, land, n):
        for a in range(4):
            total1[a] = line_sum(dst, land1, n, a)
            copy = owner_copy(a, total1, land)
            local = pltpu.make_async_copy(total1.at[a], land.at[u], own_recv.at[u])
            apart(owner_dev(*xy(a, w)), lambda: copy.start(), lambda: local.start())

    def owner_sum(total1, land):
        total = None
        for a in range(4):
            rcopy(total1.at[0], land.at[a], own_send.at[0], own_recv.at[a], partner).wait_recv()
            total = land[a] if total is None else total + land[a]
        return total

    def owner_finish(total1, land):
        for a in range(4):
            copy = owner_copy(a, total1, land)
            pl.when(jnp.logical_not(is_me(owner_dev(*xy(a, w)))))(lambda: copy.wait_send())

    def slab_at(buf, h, block):
        return buf.at[pl.ds(3 * h, SLICES), :, pl.ds(pl.multiple_of(LANES * block, LANES), LANES)]

    def slab_piece(buf, xx, yy, lo):
        return slab_at(buf, lax.rem(yy, 2), 4 * xx + 2 * lo + lax.div(yy, 2))

    def slab_copy(buf, n, a, b, lo, slot, dev):
        xx, yy = xy(a, b)
        ref = slab_piece(buf, xx, yy, lo)
        return rcopy(ref, ref, sl_send.at[n, slot], sl_recv.at[n, 2 * (4 * xx + yy) + lo], dev)

    def second_dev(d):
        return plane_dev(pid(u, turn(w, d, 4)))

    def slab_wait(buf, n, a, b, lo):
        slab_copy(buf, n, a, b, lo, 0, partner).wait_recv()

    def swap_copy(src, buf, n):
        return rcopy(src, slab_at(buf, ylo, c), sl_send.at[n, 31],
                     sl_recv.at[n, 2 * (4 * zhi + 2 * core + ylo) + zlo], owner_dev(px, py))

    def swap_start(src, buf, n):
        local = pltpu.make_async_copy(src, slab_at(buf, ylo, c), sl_recv.at[n, 2 * (4 * zhi + 2 * core + ylo) + zlo])
        apart(owner_dev(px, py), lambda: swap_copy(src, buf, n).start(), lambda: local.start())

    def slab_near(buf, n, a, lo, slot):
        slab_copy(buf, n, a, w, lo, slot, second_dev(1)).start()
        slab_copy(buf, n, a, w, lo, slot + 1, second_dev(3)).start()

    def slab_first(buf, n):
        for i, d in enumerate((2, 1, 3)):
            slab_copy(buf, n, u, w, zlo, i, plane_dev(pid(turn(u, d, 4), w))).start()
        slab_near(buf, n, u, zlo, 7)
        for i, d in enumerate((2, 1, 3, 0)):
            slab_copy(buf, n, u, w, zlo, 3 + i, (2 * pid(turn(u, d, 4), w) + 1 - zlo, slab)).start()

    def slab_second(buf, n):
        for i, d in enumerate((1, 3, 2)):
            a = turn(u, d, 4)
            slab_wait(buf, n, a, w, zlo)
            slab_near(buf, n, a, zlo, 9 + 2 * i)
        for i, d in enumerate((0, 1, 3, 2)):
            a = turn(u, d, 4)
            slab_wait(buf, n, a, w, 1 - zlo)
            slab_near(buf, n, a, 1 - zlo, 15 + 2 * i)

    def slab_third(buf, n):
        for i, d in enumerate((0, 1, 3, 2)):
            a = turn(u, d, 4)
            slab_wait(buf, n, a, turn(w, 3, 4), 0)
            slab_copy(buf, n, a, turn(w, 3, 4), 0, 23 + 2 * i, second_dev(1)).start()
            slab_wait(buf, n, a, turn(w, 1, 4), 1)
            slab_copy(buf, n, a, turn(w, 1, 4), 1, 24 + 2 * i, second_dev(3)).start()

    def slab_rest(buf, n):
        for lo in range(2):
            for d in (3 if lo else 1, 2):
                @pl.loop(0, 4)
                def _(a):
                    slab_wait(buf, n, a, turn(w, d, 4), lo)

    def slab_finish(buf, n):
        @pl.loop(0, 31)
        def _(t):
            slab_copy(buf, n, u, w, zlo, t, partner).wait_send()

    def blk_copy(src, dst, n, d):
        k = turn(c, d, PIECES)
        return rcopy(src.at[k], dst.at[:, :, pl.ds(pl.multiple_of(LANES * c, LANES), LANES)], blk_send.at[n, d],
                     blk_recv.at[n, c], col_dev(k))

    def blk_send_all(src, dst, n):
        @pl.loop(1, PIECES)
        def _(d):
            blk_copy(src, dst, n, d).start()

        dst[:, :, pl.ds(pl.multiple_of(LANES * c, LANES), LANES)] = src[c]

    def blk_finish(src, dst, n):
        @pl.loop(1, PIECES)
        def _(d):
            k = turn(c, d, PIECES)
            rcopy(src.at[0], dst.at[:, :, pl.ds(pl.multiple_of(LANES * k, LANES), LANES)], blk_send.at[n, d],
                  blk_recv.at[n, k], partner).wait_recv()
            blk_copy(src, dst, n, d).wait_send()

    def gather_finish(buf, halo, n):
        if n:
            for d in range(1, 4):
                rcopy(buf.at[0], buf.at[0], ag_send.at[n, d - 1], ag_recv.at[n, 0], partner).wait_send()
        for da in range(4):
            for d in (1, 2, 3):
                gather_copy2(buf, n, da, d).wait_send()

        @pl.loop(0, PIECES)
        def _(t):
            for side in range(2):
                halo_copy(buf, halo, n, t, side).wait_send()

    def scatter_finish(src, land1, n):
        @pl.loop(0, 12)
        def _(t):
            rcopy(src.at[0], land1.at[0, 0], rs_send.at[n, t], rs_recv.at[n, 0], partner).wait_send()

    def place_measured():
        @pl.loop(1, PIECES)
        def _(d):
            k = turn(c, d, PIECES)
            rcopy(msh.at[0], mbuf.at[k], m_send.at[d], m_recv.at[k], partner).wait_recv()

        for k in range(PIECES):
            rows = pl.ds(6 * (2 * (k // 4) + k % 2), 6)
            for e in range(2):
                for t in range(2):
                    wide[2 * ((k // 2) % 2) + e, t, rows, :] = mbuf[k, e, :, LANES * t:LANES * (t + 1)]

    def rows_of(blk):
        for k in range(PIECES):
            rows = pl.ds(6 * (2 * (k // 4) + k % 2), 6)
            for e in range(2):
                blk[k, e] = wide[2 * ((k // 2) % 2) + e, 0, rows, :]

    gather_project(xbuf, xhalo, 0, place_measured)
    for a in range(ANGLES):
        wide[a, 0] = wide[a, 0] - img[a, 0]
        wide[a, 1] = halo_mask(wide[a, 1] - img[a, 1])
    make_diff()

    back_scatter(part, rs1, 0, turn(u, 1, 4))
    rows_of(rblk)
    blk_send_all(rblk, rres, 0)
    own[...] = plane_sum(part, rs1, sum1, rs2, 0)
    gbuf[p] = own[...]
    gather_send1(gbuf, 1)
    swap_start(own, gslab, 0)
    img[...] = jnp.zeros_like(img)
    gather_project(gbuf, ghalo, 1, None)
    slab_wait(gslab, 0, u, w, zlo)
    slab_first(gslab, 0)

    norm = jnp.zeros((ROWS, LANES), F32)
    for a in range(ANGLES):
        mine = img[a, 0]
        wide[a, 0] = mine
        wide[a, 1] = halo_mask(img[a, 1])
        norm = norm + mine * mine
    make_diff()
    back_scatter(qpart, qrs1, 1, 0)

    tiles[...] = jnp.zeros_like(tiles)

    def down(v):
        return jnp.sum(v, axis=0, keepdims=True)

    def sum_copy(set_, n, d):
        at, dev, land = (
            (c, col_dev(turn(c, d, PIECES)), sc1),
            (px, plane_dev(4 * turn(px, d, 4) + py), sc2),
            (py, plane_dev(4 * px + turn(py, d, 4)), sc3),
        )[n]
        return rcopy(tiles.at[set_, n], land.at[set_, at], sc_send.at[set_, n, d], sc_recv.at[set_, n, at], dev)

    def sum_start(set_, n):
        @pl.loop(1, PIECES if n == 0 else 4)
        def _(d):
            sum_copy(set_, n, d).start()

        (sc1, sc2, sc3)[n][set_, (c, px, py)[n]] = tiles[set_, n]

    def sum_finish(set_, n):
        count = PIECES if n == 0 else 4
        land = (sc1, sc2, sc3)[n]

        @pl.loop(1, count)
        def _(d):
            k = turn((c, px, py)[n], d, count)
            rcopy(tiles.at[set_, n], land.at[set_, k], sc_send.at[set_, n, d], sc_recv.at[set_, n, k], partner).wait_recv()
            sum_copy(set_, n, d).wait_send()

        total = land[set_, 0]
        for k in range(1, count):
            total = total + land[set_, k]
        return total

    def sum_step(set_, n):
        tiles[set_, n + 1] = sum_finish(set_, n)
        sum_start(set_, n + 1)

    g = gbuf[p]
    tiles[0, 0, 0:1, :] = down(jnp.sum(g * g, axis=0))
    tiles[0, 0, 1:2, :] = down(norm)
    sum_start(0, 0)
    slab_second(gslab, 0)
    owner_start(qpart, qrs1, qsum1, qland, 1)
    sum_step(0, 0)
    rows_of(iblk)

    @pl.loop(1, PIECES)
    def _(d):
        m_copy(d).wait_send()

    gather_finish(xbuf, xhalo, 0)
    gather_finish(gbuf, ghalo, 1)
    scatter_finish(part, rs1, 0)
    for d in range(1, 4):
        scatter_copy2(sum1, rs2, 0, d).wait_send()
    x_each(lambda copy: copy.wait_send(), lambda copy: None)
    q = owner_sum(qsum1, qland)
    qslab[pl.ds(3 * ylo, SLICES), :, pl.ds(pl.multiple_of(LANES * (4 * px + 2 * zlo + yhi), LANES), LANES)] = q
    slab_first(qslab, 1)
    tiles[1, 0, 0:1, :] = down(jnp.sum(q * q, axis=0))
    sum_start(1, 0)
    blk_send_all(iblk, ires, 1)
    sum_step(0, 1)
    slab_third(gslab, 0)
    slab_second(qslab, 1)
    sum_step(1, 0)
    scatter_finish(qpart, qrs1, 1)
    owner_finish(qsum1, qland)
    sums = jnp.sum(sum_finish(0, 2), axis=1, keepdims=True)
    gamma = sums[0:1]
    alpha = gamma / sums[1:2]
    slab_third(qslab, 1)
    sum_step(1, 1)

    blk_finish(rblk, rres, 0)
    blk_finish(iblk, ires, 1)
    for e in range(2):
        res_out[:, e, :] = rres[e] - alpha * ires[e]

    def out_copy(src, dst, n, i):
        return pltpu.make_async_copy(src.at[i], dst.at[i], out_sem.at[n, i])

    slab_rest(gslab, 0)
    for i in range(6):
        volv[i] = xv[i] + alpha * gslab[i]
        out_copy(volv, vol_out, 0, i).start()
    scale = alpha * alpha * (jnp.sum(sum_finish(1, 2), axis=1, keepdims=True)[0:1] / gamma)
    slab_rest(qslab, 1)
    for i in range(6):
        dirv[i] = scale * gslab[i] - alpha * qslab[i]
        out_copy(dirv, dir_out, 1, i).start()

    slab_finish(gslab, 0)
    slab_finish(qslab, 1)
    pl.when(jnp.logical_not(is_me(owner_dev(px, py))))(lambda: swap_copy(own, gslab, 0).wait_send())
    for i in range(6):
        out_copy(volv, vol_out, 0, i).wait()
        out_copy(dirv, dir_out, 1, i).wait()


def per_device(start_volume, measured, row_shift, col_shift, col_frac):
    piece = (SLICES, LINES, LANES)
    vmem = pltpu.VMEM
    dma = pltpu.SemaphoreType.DMA
    scratch = [
        vmem(start_volume.shape, F32), vmem(start_volume.shape, F32), vmem(start_volume.shape, F32),
        vmem(start_volume.shape, F32), vmem(start_volume.shape, F32),
        vmem((6, 2, X), F32),
        vmem((PIECES, 2, 6, 2 * LANES), F32),
        vmem((PIECES, 2, 6, 2 * LANES), F32),
        vmem((2, 48), jnp.int32), vmem((2, 48), jnp.int32), vmem((2, 48), F32),
        pltpu.SMEM((2, 2, 48), jnp.int32), pltpu.SMEM((2, 2, 48), jnp.int32), pltpu.SMEM((2, 2, 48), F32),
        vmem((PIECES,) + piece, F32), vmem((PIECES, 2) + piece, F32),
        vmem((PIECES,) + piece, F32), vmem((PIECES, 2) + piece, F32),
        vmem((ANGLES * SLICES, 2, 3 * LINES, LANES), F32),
        vmem((ANGLES, 2, ROWS, LANES), F32),
        vmem((ANGLES, 2, ROWS, LANES), F32),
        vmem((ANGLES, 2, ROWS, LANES), F32),
        vmem((PIECES,) + piece, F32), vmem((3, 4) + piece, F32), vmem((4,) + piece, F32), vmem((3,) + piece, F32), vmem(piece, F32),
        vmem((PIECES,) + piece, F32), vmem((3, 4) + piece, F32), vmem((4,) + piece, F32), vmem((4,) + piece, F32),
        vmem((PIECES, 2, 6, LANES), F32), vmem((PIECES, 2, 6, LANES), F32),
        vmem(measured.shape, F32), vmem(measured.shape, F32),
        vmem((2, 3, 8, LANES), F32), vmem((2, PIECES, 8, LANES), F32), vmem((2, 4, 8, LANES), F32), vmem((2, 4, 8, LANES), F32),
        dma((8,)), dma((3,)), dma((3,)), dma((3,)), dma((PIECES,)), dma((PIECES,)), dma((4, 3)),
        dma((2, 15)), dma((2, PIECES)), dma((2, 2, PIECES)), dma((2, 2, PIECES)),
        dma((2, 12)), dma((2, 12)), dma((1, 3)), dma((1, 3)), dma((4,)), dma((4,)),
        dma((2, 32)), dma((2, 32)), dma((2, PIECES)), dma((2, PIECES)), dma((2, 3, PIECES)), dma((2, 3, PIECES)), dma((2, 6)),
    ]
    whole = pl.BlockSpec(memory_space=pltpu.VMEM)
    far = pl.BlockSpec(memory_space=pltpu.HBM)
    rows = jnp.transpose(measured, (1, 0, 2))
    volume, residual, direction = pl.pallas_call(
        kernel,
        out_shape=(
            jax.ShapeDtypeStruct(start_volume.shape, F32),
            jax.ShapeDtypeStruct(rows.shape, F32),
            jax.ShapeDtypeStruct(start_volume.shape, F32),
        ),
        in_specs=[far] * 5,
        out_specs=(far, whole, far),
        scratch_shapes=scratch,
        compiler_params=pltpu.CompilerParams(
            collective_id=0, has_side_effects=True, vmem_limit_bytes=60 * 2**20
        ),
    )(start_volume, rows, row_shift, col_shift, col_frac)
    return volume, jnp.transpose(residual, (1, 0, 2)), direction


def solution(mesh):
    return jax.shard_map(
        per_device,
        mesh=mesh,
        in_specs=(
            P("slab", None, None),
            P("ang", "slab", None),
            P("ang", None),
            P("ang", None),
            P("ang", None),
        ),
        out_specs=(P("slab", None, None), P("ang", "slab", None), P("slab", None, None)),
        check_vma=False,
    )
```

```python
import jax
import jax.numpy as jnp
from jax import lax
from jax.experimental import pallas as pl
from jax.experimental.pallas import tpu as pltpu
from jax.sharding import PartitionSpec as P

MESH = pl.DeviceIdType.MESH
F32 = jnp.float32
PIECES = 16
SLICES = 3
LINES = 24
ROWS = 48
ANGLES = 4
LANES = 128
X = 2048


def rcopy(src, dst, send, recv, dev):
    return pltpu.make_async_remote_copy(
        src_ref=src, dst_ref=dst, send_sem=send, recv_sem=recv, device_id=dev, device_id_type=MESH
    )


def lanes_of(shape):
    return lax.broadcasted_iota(jnp.int32, shape, len(shape) - 1)


def kernel(
    x_hbm, m_hbm, rt_ref, ct_ref, ft_ref,
    vol_out, res_out, dir_out,
    xv, volv, dirv, gslab, qslab, m_ref, msh, mbuf, rtv, ctv, ftv, rts, cts, fts,
    xbuf, xhalo, gbuf, ghalo, pad, img, wide, diff,
    part, rs1, sum1, rs2, own, qpart, qrs1, qsum1, qland,
    rows_out, rows_in, tiles, sc1, sc2, sc3,
    loc_sem, tab_send, tab_recv, tab_loc, m_send, m_recv, x_send,
    ag_send, ag_recv, hl_send, hl_recv,
    rs_send, rs_recv, rt_send, rt_recv, own_send, own_recv,
    sl_send, sl_recv, blk_send, blk_recv, sc_send, sc_recv, out_sem,
):
    ang = lax.axis_index("ang")
    slab = lax.axis_index("slab")
    p = lax.div(ang, 2)
    zlo = lax.rem(ang, 2)
    px = lax.div(p, 4)
    py = lax.rem(p, 4)
    zhi = lax.div(slab, 2)
    core = lax.rem(slab, 2)
    z = 2 * zhi + zlo
    c = 2 * z + core
    even = core == 0
    u = jnp.where(even, px, py)
    w = jnp.where(even, py, px)

    def pid(a, b):
        return jnp.where(even, 4 * a + b, 4 * b + a)

    def plane_dev(q):
        return (2 * q + zlo, slab)

    def col_dev(k):
        zz = lax.div(k, 2)
        return (2 * p + lax.rem(zz, 2), 2 * lax.div(zz, 2) + lax.rem(k, 2))

    def turn(v, d, n):
        return lax.rem(v + d, n)

    lane = lanes_of((8, LANES))
    exist = jnp.where(lane < 64, jnp.where(c < PIECES - 1, 1, 0), jnp.where(c > 0, 1, 0)) > 0
    me_dev = (ang, slab)

    def xy(a, b):
        return jnp.where(even, a, b), jnp.where(even, b, a)

    def is_me(dev):
        return jnp.logical_and(dev[0] == ang, dev[1] == slab)

    def apart(dev, then, here):
        pl.when(jnp.logical_not(is_me(dev)))(then)
        pl.when(is_me(dev))(here)

    def owner_dev(xx, yy):
        return (2 * (4 * zhi + 2 * core + lax.rem(yy, 2)) + zlo, 2 * xx + lax.div(yy, 2))

    partner = (2 * p + (1 - zlo), slab)
    yhi = lax.div(py, 2)
    ylo = lax.rem(py, 2)

    tables = ((rt_ref, rtv, rts), (ct_ref, ctv, cts), (ft_ref, ftv, fts))

    def table_copy(n):
        return pltpu.make_async_copy(tables[n][0], tables[n][2].at[zlo], loc_sem.at[4 + n])

    barrier = pltpu.get_barrier_semaphore()

    def greet(dev):
        pl.semaphore_signal(barrier, inc=1, device_id=dev, device_id_type=MESH)

    @pl.loop(1, PIECES)
    def _(d):
        greet(col_dev(turn(c, d, PIECES)))

    for d in range(1, 4):
        greet(plane_dev(pid(turn(u, d, 4), w)))
        greet(plane_dev(pid(u, turn(w, d, 4))))
    for a in range(4):
        greet((2 * pid(a, w) + 1 - zlo, slab))
    mine = 0
    for a in range(4):
        to = owner_dev(*xy(a, w))
        pl.when(jnp.logical_not(is_me(to)))(lambda to=to: greet(to))
        mine = mine + jnp.where(is_me(to), 1, 0)
        at_x, at_y = zhi, 2 * core + ylo
        come = (2 * jnp.where(yhi == 0, 4 * a + at_y, 4 * at_x + a) + zlo, 2 * px + yhi)
        pl.when(jnp.logical_not(is_me(come)))(lambda come=come: greet(come))

    mload = pltpu.make_async_copy(m_hbm, m_ref, loc_sem.at[0])
    mload.start()
    for n in range(3):
        table_copy(n).start()
    xload = pltpu.make_async_copy(x_hbm, xv, loc_sem.at[1])
    xload.start()

    lane6 = lanes_of((6, LANES))
    mload.wait()
    for a in range(2):
        for t in range(PIECES):
            here = m_ref[:, a, pl.ds(LANES * t, LANES)]
            right = m_ref[:, a, pl.ds(LANES * min(t + 1, 15), LANES)]
            left = m_ref[:, a, pl.ds(LANES * max(t - 1, 0), LANES)]
            msh[t, pl.ds(6 * a, 6), :] = here
            msh[t, pl.ds(12 + 6 * a, 6), :] = jnp.where(lane6 < 64, right, left)

    xload.wait()
    pl.semaphore_wait(barrier, 15 + 6 + 4 + 8 - 2 * mine)

    tabs = []
    for n, (src, dst, _) in enumerate(tables):
        t = rcopy(src, dst, tab_send.at[n], tab_recv.at[n], partner)
        t.start()
        tabs.append(t)

    near = turn(zhi, 3 + 2 * zlo, 4)
    served = ((zhi, zlo), (near, 0), (near, 1), (turn(zhi, 2, 4), 1 - zlo))

    def x_each(act_far, act_here):
        for to, (to_hi, to_lo) in enumerate(served):
            for h in range(3):
                cc = 4 * to_hi + 2 * to_lo + (1 if h < 2 else 0)
                half = h if h < 2 else ylo
                k = 4 * zhi + 2 * core + half
                src = xv.at[pl.ds(3 * half, SLICES), :, pl.ds(pl.multiple_of(LANES * cc, LANES), LANES)]
                copy = rcopy(src, xbuf.at[k], x_send.at[to, h], ag_recv.at[0, k], col_dev(cc))
                local = pltpu.make_async_copy(src, xbuf.at[k], ag_recv.at[0, k])

                def act(copy=copy, local=local, cc=cc):
                    apart(col_dev(cc), lambda: act_far(copy), lambda: act_here(local))

                pl.when(zhi == px if h < 2 else core == yhi)(act)

    x_each(lambda copy: copy.start(), lambda copy: copy.start())

    def m_copy(d):
        k = turn(c, d, PIECES)
        return rcopy(msh.at[k], mbuf.at[c], m_send.at[d], m_recv.at[c], col_dev(k))

    @pl.loop(1, PIECES)
    def _(d):
        m_copy(d).start()

    mbuf[c] = msh[c]

    pad[...] = jnp.zeros_like(pad)
    img[...] = jnp.zeros_like(img)

    def step(q):
        return jnp.where(q < 2, q, 5 - q)

    def piece_order(t):
        late = t - 9
        dx = jnp.where(t < 9, step(lax.rem(t, 3)), jnp.where(late < 4, 2, step(late - 4)))
        dy = jnp.where(t < 9, step(lax.div(t, 3)), jnp.where(late < 4, step(late), 2))
        return 4 * turn(px, 4 - dx, 4) + turn(py, 4 - dy, 4)

    def gather_send1(buf, n):
        for d in range(1, 4):
            rcopy(buf.at[p], buf.at[p], ag_send.at[n, d - 1], ag_recv.at[n, p],
                  plane_dev(pid(turn(u, d, 4), w))).start()

    def gather_copy2(buf, n, da, d):
        k = pid(turn(u, 4 - da, 4), w)
        return rcopy(buf.at[k], buf.at[k], ag_send.at[n, 3 + 3 * da + d - 1], ag_recv.at[n, k],
                     plane_dev(pid(u, turn(w, d, 4))))

    def halo_copy(buf, halo, n, k, side):
        to = turn(c, 1 if side == 0 else PIECES - 1, PIECES)
        return rcopy(buf.at[k], halo.at[k, side], hl_send.at[n, side, k], hl_recv.at[n, side, k], col_dev(to))

    def halo_start(buf, halo, n, k):
        for side in range(2):
            halo_copy(buf, halo, n, k, side).start()

    def gather_wait(buf, n, k):
        rcopy(buf.at[k], buf.at[k], ag_send.at[n, 0], ag_recv.at[n, k], partner).wait_recv()

    tiles3 = (SLICES, 8, LANES)

    def project_piece(buf, halo, k):
        for s in range(SLICES):
            w0 = buf[k, s].reshape(tiles3)
            left = halo[k, 0, s].reshape(tiles3)
            right = halo[k, 1, s].reshape(tiles3)
            w1 = jnp.where(exist, jnp.where(lane < 64, right, left), 0.0)
            s0 = pltpu.roll(w0, 1, 2)
            s1 = pltpu.roll(w1, 1, 2)
            d0 = jnp.where(lane < 1, s1, s0) - w0
            d1 = jnp.where(lane < 1, s0, s1) - w1
            at = SLICES * k + s
            for a in range(ANGLES):
                f = fts[a // 2, a % 2, at]
                cs = cts[a // 2, a % 2, at]
                v0 = w0 + f * d0
                v1 = w1 + f * d1
                other = jnp.logical_or(lane >= LANES - cs, lane < -cs)
                sh = lax.rem(cs + LANES, LANES)
                full = (LINES, LANES)
                pad[SLICES * a + s, 0, pl.ds(LINES, LINES), :] = pltpu.roll(jnp.where(other, v1, v0), sh, 2).reshape(full)
                pad[SLICES * a + s, 1, pl.ds(LINES, LINES), :] = pltpu.roll(jnp.where(other, v0, v1), sh, 2).reshape(full)
        for a in range(ANGLES):
            for t in range(2):
                acc = img[a, t]
                for s in range(SLICES):
                    rs = rts[a // 2, a % 2, SLICES * k + s]
                    acc = acc + pad[SLICES * a + s, t, pl.ds(LINES - rs, ROWS), :]
                img[a, t] = acc

    def smem_copy(n):
        return pltpu.make_async_copy(tables[n][1], tables[n][2].at[1 - zlo], tab_loc.at[n])

    def gather_project(buf, halo, n, during):
        for da in (0, 1, 3, 2):
            k = pid(turn(u, 4 - da, 4), w)
            if n == 0 or da:
                gather_wait(buf, n, k)
            for d in (2, 1, 3):
                gather_copy2(buf, n, da, d).start()
            halo_start(buf, halo, n, k)

        if n == 0:
            for i in range(3):
                tabs[i].wait()
                smem_copy(i).start()

        @pl.loop(0, 8)
        def _(t):
            k = pid(turn(u, 4 - step(lax.div(t, 2)), 4), turn(w, 3 - 2 * lax.rem(t, 2), 4))
            gather_wait(buf, n, k)
            halo_start(buf, halo, n, k)

        if n == 0:
            for i in range(3):
                smem_copy(i).wait()
                table_copy(i).wait()

        @pl.loop(0, PIECES)
        def _(t):
            if during is not None:
                pl.when(t == 10)(during)

            @pl.when(jnp.logical_and(t >= 4, t < 8))
            def _():
                k = pid(turn(u, 4 - step(t - 4), 4), turn(w, 2, 4))
                gather_wait(buf, n, k)
                halo_start(buf, halo, n, k)

            k = piece_order(t)
            for side in range(2):
                halo_copy(buf, halo, n, k, side).wait_recv()
            project_piece(buf, halo, k)

    def halo_mask(v):
        return jnp.where(exist, v.reshape(ROWS // 8, 8, LANES), 0.0).reshape(ROWS, LANES)

    def make_diff():
        last = lanes_of((ROWS, LANES)) == LANES - 1
        for a in range(ANGLES):
            v0 = wide[a, 0]
            v1 = wide[a, 1]
            s0 = pltpu.roll(v0, LANES - 1, 1)
            s1 = pltpu.roll(v1, LANES - 1, 1)
            diff[a, 0] = jnp.where(last, s1, s0) - v0
            diff[a, 1] = jnp.where(last, s0, s1) - v1

    def back_piece(dst, k):
        for s in range(SLICES):
            at = SLICES * k + s
            acc = None
            for a in range(ANGLES):
                rs = rts[a // 2, a % 2, at]
                cs = cts[a // 2, a % 2, at]
                f = fts[a // 2, a % 2, at]
                other = jnp.logical_or(lane < cs, lane >= LANES + cs)

                def rows_at(ref, t):
                    return ref[a, t, pl.ds(rs, LINES), :].reshape(tiles3)

                v = jnp.where(other, rows_at(wide, 1), rows_at(wide, 0))
                e = jnp.where(other, rows_at(diff, 1), rows_at(diff, 0))
                term = pltpu.roll(v + f * e, lax.rem(LANES - cs, LANES), 2)
                acc = term if acc is None else acc + term
            dst[k, s] = acc.reshape(LINES, LANES)

    def scatter_copy1(src, land, n, d, a):
        return rcopy(src.at[pid(a, turn(w, d, 4))], land.at[d - 1, a], rs_send.at[n, 4 * (d - 1) + a],
                     rs_recv.at[n, 4 * (d - 1) + a], plane_dev(pid(u, turn(w, d, 4))))

    def scatter_copy2(src, dst, n, d):
        a = turn(u, d, 4)
        return rcopy(src.at[a], dst.at[d - 1], rt_send.at[n, d - 1], rt_recv.at[n, d - 1], plane_dev(pid(a, w)))

    def back_scatter(dst, land, n, first):
        @pl.loop(0, PIECES)
        def _(t):
            i = lax.rem(t, 3)
            d = jnp.where(t >= 12, 0, jnp.where(i == 0, 2, 2 * i - 1))
            a = turn(first, jnp.where(t >= 12, t - 12, lax.div(t, 3)), 4)
            back_piece(dst, pid(a, turn(w, d, 4)))

            @pl.when(t < 12)
            def _():
                scatter_copy1(dst, land, n, d, a).start()

    def line_sum(dst, land, n, a):
        total = dst[pid(a, w)]
        for d in (1, 3, 2):
            scatter_copy1(dst, land, n, d, a).wait_recv()
            total = total + land[d - 1, a]
        return total

    def plane_sum(dst, land, total1, land2, n):
        for da in (1, 2, 3, 0):
            a = turn(u, da, 4)
            total1[a] = line_sum(dst, land, n, a)
            if da:
                scatter_copy2(total1, land2, n, da).start()
        total = total1[u]
        for d in (1, 3, 2):
            scatter_copy2(total1, land2, n, d).wait_recv()
            total = total + land2[d - 1]
        return total

    def owner_copy(a, total1, land):
        return rcopy(total1.at[a], land.at[u], own_send.at[a], own_recv.at[u], owner_dev(*xy(a, w)))

    def owner_start(dst, land1, total1, land, n):
        for a in range(4):
            total1[a] = line_sum(dst, land1, n, a)
            copy = owner_copy(a, total1, land)
            local = pltpu.make_async_copy(total1.at[a], land.at[u], own_recv.at[u])
            apart(owner_dev(*xy(a, w)), lambda: copy.start(), lambda: local.start())

    def owner_sum(total1, land):
        total = None
        for a in range(4):
            rcopy(total1.at[0], land.at[a], own_send.at[0], own_recv.at[a], partner).wait_recv()
            total = land[a] if total is None else total + land[a]
        return total

    def owner_finish(total1, land):
        for a in range(4):
            copy = owner_copy(a, total1, land)
            pl.when(jnp.logical_not(is_me(owner_dev(*xy(a, w)))))(lambda: copy.wait_send())

    def slab_piece(buf, xx, yy, lo):
        return buf.at[2 * (4 * xx + yy) + lo]

    def slab_copy(buf, n, a, b, lo, slot, dev):
        xx, yy = xy(a, b)
        ref = slab_piece(buf, xx, yy, lo)
        return rcopy(ref, ref, sl_send.at[n, slot], sl_recv.at[n, 2 * (4 * xx + yy) + lo], dev)

    def second_dev(d):
        return plane_dev(pid(u, turn(w, d, 4)))

    def slab_wait(buf, n, a, b, lo):
        slab_copy(buf, n, a, b, lo, 0, partner).wait_recv()

    def swap_copy(src, buf, n):
        return rcopy(src, slab_piece(buf, zhi, 2 * core + ylo, zlo), sl_send.at[n, 31],
                     sl_recv.at[n, 2 * (4 * zhi + 2 * core + ylo) + zlo], owner_dev(px, py))

    def swap_start(src, buf, n):
        local = pltpu.make_async_copy(src, slab_piece(buf, zhi, 2 * core + ylo, zlo), sl_recv.at[n, 2 * (4 * zhi + 2 * core + ylo) + zlo])
        apart(owner_dev(px, py), lambda: swap_copy(src, buf, n).start(), lambda: local.start())

    def slab_near(buf, n, a, lo, slot):
        slab_copy(buf, n, a, w, lo, slot, second_dev(1)).start()
        slab_copy(buf, n, a, w, lo, slot + 1, second_dev(3)).start()

    def slab_first(buf, n):
        for i, d in enumerate((2, 1, 3)):
            slab_copy(buf, n, u, w, zlo, i, plane_dev(pid(turn(u, d, 4), w))).start()
        slab_near(buf, n, u, zlo, 7)
        for i, d in enumerate((2, 1, 3, 0)):
            slab_copy(buf, n, u, w, zlo, 3 + i, (2 * pid(turn(u, d, 4), w) + 1 - zlo, slab)).start()

    def slab_second(buf, n):
        for i, d in enumerate((1, 3, 2)):
            a = turn(u, d, 4)
            slab_wait(buf, n, a, w, zlo)
            slab_near(buf, n, a, zlo, 9 + 2 * i)
        for i, d in enumerate((0, 1, 3, 2)):
            a = turn(u, d, 4)
            slab_wait(buf, n, a, w, 1 - zlo)
            slab_near(buf, n, a, 1 - zlo, 15 + 2 * i)

    def slab_third(buf, n):
        for i, d in enumerate((0, 1, 3, 2)):
            a = turn(u, d, 4)
            slab_wait(buf, n, a, turn(w, 3, 4), 0)
            slab_copy(buf, n, a, turn(w, 3, 4), 0, 23 + 2 * i, second_dev(1)).start()
            slab_wait(buf, n, a, turn(w, 1, 4), 1)
            slab_copy(buf, n, a, turn(w, 1, 4), 1, 24 + 2 * i, second_dev(3)).start()

    def slab_rest(buf, n):
        for lo in range(2):
            for d in (3 if lo else 1, 2):
                @pl.loop(0, 4)
                def _(a):
                    slab_wait(buf, n, a, turn(w, d, 4), lo)

    def slab_finish(buf, n):
        @pl.loop(0, 31)
        def _(t):
            slab_copy(buf, n, u, w, zlo, t, partner).wait_send()

    def blk_copy(d):
        k = turn(c, d, PIECES)
        return rcopy(rows_out.at[k], rows_in.at[c], blk_send.at[d], blk_recv.at[c], col_dev(k))

    def blk_start():
        @pl.loop(1, PIECES)
        def _(d):
            blk_copy(d).start()

        rows_in[c] = rows_out[c]

    def blk_finish():
        @pl.loop(1, PIECES)
        def _(d):
            k = turn(c, d, PIECES)
            rcopy(rows_out.at[0], rows_in.at[k], blk_send.at[d], blk_recv.at[k], partner).wait_recv()
            blk_copy(d).wait_send()

    def gather_finish(buf, halo, n):
        if n:
            for d in range(1, 4):
                rcopy(buf.at[0], buf.at[0], ag_send.at[n, d - 1], ag_recv.at[n, 0], partner).wait_send()
        for da in range(4):
            for d in (1, 2, 3):
                gather_copy2(buf, n, da, d).wait_send()

        @pl.loop(0, PIECES)
        def _(t):
            for side in range(2):
                halo_copy(buf, halo, n, t, side).wait_send()

    def scatter_finish(src, land1, n):
        @pl.loop(0, 12)
        def _(t):
            rcopy(src.at[0], land1.at[0, 0], rs_send.at[n, t], rs_recv.at[n, 0], partner).wait_send()

    def place_measured():
        @pl.loop(1, PIECES)
        def _(d):
            k = turn(c, d, PIECES)
            rcopy(msh.at[0], mbuf.at[k], m_send.at[d], m_recv.at[k], partner).wait_recv()

        for k in range(PIECES):
            rows = pl.ds(6 * (2 * (k // 4) + k % 2), 6)
            for e in range(2):
                for t in range(2):
                    wide[2 * ((k // 2) % 2) + e, t, rows, :] = mbuf[k, pl.ds(12 * t + 6 * e, 6), :]

    def rows_of(kind):
        for k in range(PIECES):
            rows = pl.ds(6 * (2 * (k // 4) + k % 2), 6)
            for e in range(2):
                rows_out[k, pl.ds(12 * kind + 6 * e, 6), :] = wide[2 * ((k // 2) % 2) + e, 0, rows, :]

    gather_project(xbuf, xhalo, 0, place_measured)
    for a in range(ANGLES):
        wide[a, 0] = wide[a, 0] - img[a, 0]
        wide[a, 1] = halo_mask(wide[a, 1] - img[a, 1])
    make_diff()

    back_scatter(part, rs1, 0, turn(u, 1, 4))
    rows_of(0)
    own[...] = plane_sum(part, rs1, sum1, rs2, 0)
    gbuf[p] = own[...]
    gather_send1(gbuf, 1)
    swap_start(own, gslab, 0)
    img[...] = jnp.zeros_like(img)
    gather_project(gbuf, ghalo, 1, None)
    slab_wait(gslab, 0, u, w, zlo)
    slab_first(gslab, 0)

    norm = jnp.zeros((ROWS, LANES), F32)
    for a in range(ANGLES):
        mine = img[a, 0]
        wide[a, 0] = mine
        wide[a, 1] = halo_mask(img[a, 1])
        norm = norm + mine * mine
    make_diff()
    back_scatter(qpart, qrs1, 1, 0)

    tiles[...] = jnp.zeros_like(tiles)

    def down(v):
        return jnp.sum(v, axis=0, keepdims=True)

    def sum_copy(set_, n, d):
        at, dev, land = (
            (c, col_dev(turn(c, d, PIECES)), sc1),
            (px, plane_dev(4 * turn(px, d, 4) + py), sc2),
            (py, plane_dev(4 * px + turn(py, d, 4)), sc3),
        )[n]
        return rcopy(tiles.at[set_, n], land.at[set_, at], sc_send.at[set_, n, d], sc_recv.at[set_, n, at], dev)

    def sum_start(set_, n):
        @pl.loop(1, PIECES if n == 0 else 4)
        def _(d):
            sum_copy(set_, n, d).start()

        (sc1, sc2, sc3)[n][set_, (c, px, py)[n]] = tiles[set_, n]

    def sum_finish(set_, n):
        count = PIECES if n == 0 else 4
        land = (sc1, sc2, sc3)[n]

        @pl.loop(1, count)
        def _(d):
            k = turn((c, px, py)[n], d, count)
            rcopy(tiles.at[set_, n], land.at[set_, k], sc_send.at[set_, n, d], sc_recv.at[set_, n, k], partner).wait_recv()
            sum_copy(set_, n, d).wait_send()

        total = land[set_, 0]
        for k in range(1, count):
            total = total + land[set_, k]
        return total

    def sum_step(set_, n):
        tiles[set_, n + 1] = sum_finish(set_, n)
        sum_start(set_, n + 1)

    g = gbuf[p]
    tiles[0, 0, 0:1, :] = down(jnp.sum(g * g, axis=0))
    tiles[0, 0, 1:2, :] = down(norm)
    sum_start(0, 0)
    slab_second(gslab, 0)
    owner_start(qpart, qrs1, qsum1, qland, 1)
    sum_step(0, 0)
    rows_of(1)

    @pl.loop(1, PIECES)
    def _(d):
        m_copy(d).wait_send()

    gather_finish(xbuf, xhalo, 0)
    gather_finish(gbuf, ghalo, 1)
    scatter_finish(part, rs1, 0)
    for d in range(1, 4):
        scatter_copy2(sum1, rs2, 0, d).wait_send()
    x_each(lambda copy: copy.wait_send(), lambda copy: None)
    q = owner_sum(qsum1, qland)
    qslab[2 * p + zlo] = q
    slab_first(qslab, 1)
    tiles[1, 0, 0:1, :] = down(jnp.sum(q * q, axis=0))
    sum_start(1, 0)
    blk_start()
    sum_step(0, 1)
    slab_third(gslab, 0)
    slab_second(qslab, 1)
    sum_step(1, 0)
    scatter_finish(qpart, qrs1, 1)
    owner_finish(qsum1, qland)
    sums = jnp.sum(sum_finish(0, 2), axis=1, keepdims=True)
    gamma = sums[0:1]
    alpha = gamma / sums[1:2]
    slab_third(qslab, 1)
    sum_step(1, 1)

    blk_finish()
    for k in range(PIECES):
        for e in range(2):
            at = pl.ds(LANES * k, LANES)
            res_out[:, e, at] = rows_in[k, pl.ds(6 * e, 6), :] - alpha * rows_in[k, pl.ds(12 + 6 * e, 6), :]

    def out_copy(src, dst, n, i):
        return pltpu.make_async_copy(src.at[i], dst.at[i], out_sem.at[n, i])

    def each_piece(h):
        for xx in range(4):
            for yy in (h, h + 2):
                for lo in range(2):
                    block = LANES * (4 * xx + 2 * lo + yy // 2)
                    yield 2 * (4 * xx + yy) + lo, (slice(3 * h, 3 * h + 3), slice(None), slice(block, block + LANES))

    slab_rest(gslab, 0)
    for h in range(2):
        for k, at in each_piece(h):
            volv[at] = xv[at] + alpha * gslab[k]
        for i in range(3 * h, 3 * h + 3):
            out_copy(volv, vol_out, 0, i).start()
    scale = alpha * alpha * (jnp.sum(sum_finish(1, 2), axis=1, keepdims=True)[0:1] / gamma)
    slab_rest(qslab, 1)
    for h in range(2):
        for k, at in each_piece(h):
            dirv[at] = scale * gslab[k] - alpha * qslab[k]
        for i in range(3 * h, 3 * h + 3):
            out_copy(dirv, dir_out, 1, i).start()

    slab_finish(gslab, 0)
    slab_finish(qslab, 1)
    pl.when(jnp.logical_not(is_me(owner_dev(px, py))))(lambda: swap_copy(own, gslab, 0).wait_send())
    for i in range(6):
        out_copy(volv, vol_out, 0, i).wait()
        out_copy(dirv, dir_out, 1, i).wait()


def per_device(start_volume, measured, row_shift, col_shift, col_frac):
    piece = (SLICES, LINES, LANES)
    vmem = pltpu.VMEM
    dma = pltpu.SemaphoreType.DMA
    scratch = [
        vmem(start_volume.shape, F32), vmem(start_volume.shape, F32), vmem(start_volume.shape, F32),
        vmem((32,) + piece, F32), vmem((32,) + piece, F32),
        vmem((6, 2, X), F32),
        vmem((PIECES, 24, LANES), F32),
        vmem((PIECES, 24, LANES), F32),
        vmem((2, 48), jnp.int32), vmem((2, 48), jnp.int32), vmem((2, 48), F32),
        pltpu.SMEM((2, 2, 48), jnp.int32), pltpu.SMEM((2, 2, 48), jnp.int32), pltpu.SMEM((2, 2, 48), F32),
        vmem((PIECES,) + piece, F32), vmem((PIECES, 2) + piece, F32),
        vmem((PIECES,) + piece, F32), vmem((PIECES, 2) + piece, F32),
        vmem((ANGLES * SLICES, 2, 3 * LINES, LANES), F32),
        vmem((ANGLES, 2, ROWS, LANES), F32),
        vmem((ANGLES, 2, ROWS, LANES), F32),
        vmem((ANGLES, 2, ROWS, LANES), F32),
        vmem((PIECES,) + piece, F32), vmem((3, 4) + piece, F32), vmem((4,) + piece, F32), vmem((3,) + piece, F32), vmem(piece, F32),
        vmem((PIECES,) + piece, F32), vmem((3, 4) + piece, F32), vmem((4,) + piece, F32), vmem((4,) + piece, F32),
        vmem((PIECES, 24, LANES), F32), vmem((PIECES, 24, LANES), F32),
        vmem((2, 3, 8, LANES), F32), vmem((2, PIECES, 8, LANES), F32), vmem((2, 4, 8, LANES), F32), vmem((2, 4, 8, LANES), F32),
        dma((8,)), dma((3,)), dma((3,)), dma((3,)), dma((PIECES,)), dma((PIECES,)), dma((4, 3)),
        dma((2, 15)), dma((2, PIECES)), dma((2, 2, PIECES)), dma((2, 2, PIECES)),
        dma((2, 12)), dma((2, 12)), dma((1, 3)), dma((1, 3)), dma((4,)), dma((4,)),
        dma((2, 32)), dma((2, 32)), dma((PIECES,)), dma((PIECES,)), dma((2, 3, PIECES)), dma((2, 3, PIECES)), dma((2, 6)),
    ]
    whole = pl.BlockSpec(memory_space=pltpu.VMEM)
    far = pl.BlockSpec(memory_space=pltpu.HBM)
    rows = jnp.transpose(measured, (1, 0, 2))
    volume, residual, direction = pl.pallas_call(
        kernel,
        out_shape=(
            jax.ShapeDtypeStruct(start_volume.shape, F32),
            jax.ShapeDtypeStruct(rows.shape, F32),
            jax.ShapeDtypeStruct(start_volume.shape, F32),
        ),
        in_specs=[far] * 5,
        out_specs=(far, whole, far),
        scratch_shapes=scratch,
        compiler_params=pltpu.CompilerParams(
            collective_id=0, has_side_effects=True, vmem_limit_bytes=60 * 2**20
        ),
    )(start_volume, rows, row_shift, col_shift, col_frac)
    return volume, jnp.transpose(residual, (1, 0, 2)), direction


def solution(mesh):
    return jax.shard_map(
        per_device,
        mesh=mesh,
        in_specs=(
            P("slab", None, None),
            P("ang", "slab", None),
            P("ang", None),
            P("ang", None),
            P("ang", None),
        ),
        out_specs=(P("slab", None, None), P("ang", "slab", None), P("slab", None, None)),
        check_vma=False,
    )
```

```python
import jax
import jax.numpy as jnp
from jax import lax
from jax.experimental import pallas as pl
from jax.experimental.pallas import tpu as pltpu
from jax.sharding import PartitionSpec as P

MESH = pl.DeviceIdType.MESH
F32 = jnp.float32
PIECES = 16
SLICES = 3
LINES = 24
ROWS = 48
ANGLES = 4
LANES = 128
X = 2048


def rcopy(src, dst, send, recv, dev):
    return pltpu.make_async_remote_copy(
        src_ref=src, dst_ref=dst, send_sem=send, recv_sem=recv, device_id=dev, device_id_type=MESH
    )


def lanes_of(shape):
    return lax.broadcasted_iota(jnp.int32, shape, len(shape) - 1)


def kernel(
    x_hbm, m_hbm, rt_ref, ct_ref, ft_ref,
    vol_out, res_out, dir_out,
    xv, volv, dirv, gslab, qslab, m_ref, msh, mbuf, rtv, ctv, ftv, rts, cts, fts,
    xbuf, xhalo, gbuf, ghalo, pad, img, wide, diff,
    part, rs1, sum1, rs2, own, qpart, qrs1, qsum1, qland,
    rblk, iblk, rres, ires, tiles, sc1, sc2, sc3,
    loc_sem, tab_send, tab_recv, m_send, m_recv, x_send,
    ag_send, ag_recv, hl_send, hl_recv,
    rs_send, rs_recv, rt_send, rt_recv, own_send, own_recv,
    sl_send, sl_recv, blk_send, blk_recv, sc_send, sc_recv, out_sem,
):
    ang = lax.axis_index("ang")
    slab = lax.axis_index("slab")
    p = lax.div(ang, 2)
    zlo = lax.rem(ang, 2)
    px = lax.div(p, 4)
    py = lax.rem(p, 4)
    zhi = lax.div(slab, 2)
    core = lax.rem(slab, 2)
    z = 2 * zhi + zlo
    c = 2 * z + core
    even = core == 0
    u = jnp.where(even, px, py)
    w = jnp.where(even, py, px)

    def pid(a, b):
        return jnp.where(even, 4 * a + b, 4 * b + a)

    def plane_dev(q):
        return (2 * q + zlo, slab)

    def col_dev(k):
        zz = lax.div(k, 2)
        return (2 * p + lax.rem(zz, 2), 2 * lax.div(zz, 2) + lax.rem(k, 2))

    def turn(v, d, n):
        return lax.rem(v + d, n)

    lane = lanes_of((8, LANES))
    exist = jnp.where(lane < 64, jnp.where(c < PIECES - 1, 1, 0), jnp.where(c > 0, 1, 0)) > 0
    me_dev = (ang, slab)

    def xy(a, b):
        return jnp.where(even, a, b), jnp.where(even, b, a)

    def is_me(dev):
        return jnp.logical_and(dev[0] == ang, dev[1] == slab)

    def apart(dev, then, here):
        pl.when(jnp.logical_not(is_me(dev)))(then)
        pl.when(is_me(dev))(here)

    def owner_dev(xx, yy):
        return (2 * (4 * zhi + 2 * core + lax.rem(yy, 2)) + zlo, 2 * xx + lax.div(yy, 2))

    partner = (2 * p + (1 - zlo), slab)
    yhi = lax.div(py, 2)
    ylo = lax.rem(py, 2)

    mload = pltpu.make_async_copy(m_hbm, m_ref, loc_sem.at[0])
    mload.start()
    tables = ((rt_ref, rtv, rts), (ct_ref, ctv, cts), (ft_ref, ftv, fts))

    def table_copy(n):
        return pltpu.make_async_copy(tables[n][0], tables[n][1].at[zlo], loc_sem.at[4 + n])

    for n in range(3):
        table_copy(n).start()
    xload = pltpu.make_async_copy(x_hbm, xv, loc_sem.at[1])
    xload.start()

    barrier = pltpu.get_barrier_semaphore()

    def greet(dev):
        pl.semaphore_signal(barrier, inc=1, device_id=dev, device_id_type=MESH)

    @pl.loop(1, PIECES)
    def _(d):
        greet(col_dev(turn(c, d, PIECES)))

    for d in range(1, 4):
        greet(plane_dev(pid(turn(u, d, 4), w)))
        greet(plane_dev(pid(u, turn(w, d, 4))))
    for a in range(4):
        greet((2 * pid(a, w) + 1 - zlo, slab))
    mine = 0
    for a in range(4):
        to = owner_dev(*xy(a, w))
        pl.when(jnp.logical_not(is_me(to)))(lambda to=to: greet(to))
        mine = mine + jnp.where(is_me(to), 1, 0)
        at_x, at_y = zhi, 2 * core + ylo
        come = (2 * jnp.where(yhi == 0, 4 * a + at_y, 4 * at_x + a) + zlo, 2 * px + yhi)
        pl.when(jnp.logical_not(is_me(come)))(lambda come=come: greet(come))

    lane6 = lanes_of((6, LANES))
    mload.wait()
    for a in range(2):
        for t in range(PIECES):
            here = m_ref[:, a, pl.ds(LANES * t, LANES)]
            right = m_ref[:, a, pl.ds(LANES * min(t + 1, 15), LANES)]
            left = m_ref[:, a, pl.ds(LANES * max(t - 1, 0), LANES)]
            msh[t, a, :, :LANES] = here
            msh[t, a, :, LANES:] = jnp.where(lane6 < 64, right, left)

    pad[...] = jnp.zeros_like(pad)
    img[...] = jnp.zeros_like(img)
    xload.wait()
    pl.semaphore_wait(barrier, 15 + 6 + 4 + 8 - 2 * mine)

    near = turn(zhi, 3 + 2 * zlo, 4)
    served = ((zhi, zlo), (near, 0), (near, 1), (turn(zhi, 2, 4), 1 - zlo))

    def x_each(act_far, act_here):
        for to, (to_hi, to_lo) in enumerate(served):
            for h in range(3):
                cc = 4 * to_hi + 2 * to_lo + (1 if h < 2 else 0)
                half = h if h < 2 else ylo
                k = 4 * zhi + 2 * core + half
                src = xv.at[pl.ds(3 * half, SLICES), :, pl.ds(pl.multiple_of(LANES * cc, LANES), LANES)]
                copy = rcopy(src, xbuf.at[k], x_send.at[to, h], ag_recv.at[0, k], col_dev(cc))
                local = pltpu.make_async_copy(src, xbuf.at[k], ag_recv.at[0, k])

                def act(copy=copy, local=local, cc=cc):
                    apart(col_dev(cc), lambda: act_far(copy), lambda: act_here(local))

                pl.when(zhi == px if h < 2 else core == yhi)(act)

    x_each(lambda copy: copy.start(), lambda copy: copy.start())

    tabs = []
    for n, (src, dst, _) in enumerate(tables):
        t = rcopy(src, dst.at[zlo], tab_send.at[n], tab_recv.at[n], partner)
        t.start()
        tabs.append(t)

    def m_copy(d):
        k = turn(c, d, PIECES)
        return rcopy(msh.at[k], mbuf.at[c], m_send.at[d], m_recv.at[c], col_dev(k))

    def m_start():
        @pl.loop(1, PIECES)
        def _(d):
            m_copy(d).start()

    mbuf[c] = msh[c]

    def step(q):
        return jnp.where(q < 2, q, 5 - q)

    def piece_order(t):
        late = t - 9
        dx = jnp.where(t < 9, step(lax.rem(t, 3)), jnp.where(late < 4, 2, step(late - 4)))
        dy = jnp.where(t < 9, step(lax.div(t, 3)), jnp.where(late < 4, step(late), 2))
        return 4 * turn(px, 4 - dx, 4) + turn(py, 4 - dy, 4)

    def gather_send1(buf, n):
        for d in range(1, 4):
            rcopy(buf.at[p], buf.at[p], ag_send.at[n, d - 1], ag_recv.at[n, p],
                  plane_dev(pid(turn(u, d, 4), w))).start()

    def gather_copy2(buf, n, da, d):
        k = pid(turn(u, 4 - da, 4), w)
        return rcopy(buf.at[k], buf.at[k], ag_send.at[n, 3 + 3 * da + d - 1], ag_recv.at[n, k],
                     plane_dev(pid(u, turn(w, d, 4))))

    def halo_copy(buf, halo, n, k, side):
        to = turn(c, 1 if side == 0 else PIECES - 1, PIECES)
        return rcopy(buf.at[k], halo.at[k, side], hl_send.at[n, side, k], hl_recv.at[n, side, k], col_dev(to))

    def halo_start(buf, halo, n, k):
        for side in range(2):
            halo_copy(buf, halo, n, k, side).start()

    def gather_wait(buf, n, k):
        rcopy(buf.at[k], buf.at[k], ag_send.at[n, 0], ag_recv.at[n, k], partner).wait_recv()

    tiles3 = (SLICES, 8, LANES)

    def project_piece(buf, halo, k):
        for s in range(SLICES):
            w0 = buf[k, s].reshape(tiles3)
            left = halo[k, 0, s].reshape(tiles3)
            right = halo[k, 1, s].reshape(tiles3)
            w1 = jnp.where(exist, jnp.where(lane < 64, right, left), 0.0)
            s0 = pltpu.roll(w0, 1, 2)
            s1 = pltpu.roll(w1, 1, 2)
            d0 = jnp.where(lane < 1, s1, s0) - w0
            d1 = jnp.where(lane < 1, s0, s1) - w1
            at = SLICES * k + s
            for a in range(ANGLES):
                f = fts[a // 2, a % 2, at]
                cs = cts[a // 2, a % 2, at]
                v0 = w0 + f * d0
                v1 = w1 + f * d1
                other = jnp.logical_or(lane >= LANES - cs, lane < -cs)
                sh = lax.rem(cs + LANES, LANES)
                full = (LINES, LANES)
                pad[SLICES * a + s, 0, pl.ds(LINES, LINES), :] = pltpu.roll(jnp.where(other, v1, v0), sh, 2).reshape(full)
                pad[SLICES * a + s, 1, pl.ds(LINES, LINES), :] = pltpu.roll(jnp.where(other, v0, v1), sh, 2).reshape(full)
        for a in range(ANGLES):
            for t in range(2):
                acc = img[a, t]
                for s in range(SLICES):
                    rs = rts[a // 2, a % 2, SLICES * k + s]
                    acc = acc + pad[SLICES * a + s, t, pl.ds(LINES - rs, ROWS), :]
                img[a, t] = acc

    def gather_project(buf, halo, n, during):
        for da in (0, 1, 3, 2):
            k = pid(turn(u, 4 - da, 4), w)
            if n == 0 or da:
                gather_wait(buf, n, k)
            for d in (1, 3, 2):
                gather_copy2(buf, n, da, d).start()
            halo_start(buf, halo, n, k)

        @pl.loop(0, 8)
        def _(t):
            k = pid(turn(u, 4 - step(lax.div(t, 2)), 4), turn(w, 3 - 2 * lax.rem(t, 2), 4))
            gather_wait(buf, n, k)
            halo_start(buf, halo, n, k)

        if n == 0:
            m_start()

        @pl.loop(0, PIECES)
        def _(t):
            if during is not None:
                pl.when(t == 10)(during)

            @pl.when(jnp.logical_and(t >= 4, t < 8))
            def _():
                k = pid(turn(u, 4 - step(t - 4), 4), turn(w, 2, 4))
                gather_wait(buf, n, k)
                halo_start(buf, halo, n, k)

            k = piece_order(t)
            for side in range(2):
                halo_copy(buf, halo, n, k, side).wait_recv()
            project_piece(buf, halo, k)

    def halo_mask(v):
        return jnp.where(exist, v.reshape(ROWS // 8, 8, LANES), 0.0).reshape(ROWS, LANES)

    def make_diff():
        last = lanes_of((ROWS, LANES)) == LANES - 1
        for a in range(ANGLES):
            v0 = wide[a, 0]
            v1 = wide[a, 1]
            s0 = pltpu.roll(v0, LANES - 1, 1)
            s1 = pltpu.roll(v1, LANES - 1, 1)
            diff[a, 0] = jnp.where(last, s1, s0) - v0
            diff[a, 1] = jnp.where(last, s0, s1) - v1

    def back_piece(dst, k):
        for s in range(SLICES):
            at = SLICES * k + s
            acc = None
            for a in range(ANGLES):
                rs = rts[a // 2, a % 2, at]
                cs = cts[a // 2, a % 2, at]
                f = fts[a // 2, a % 2, at]
                other = jnp.logical_or(lane < cs, lane >= LANES + cs)

                def rows_at(ref, t):
                    return ref[a, t, pl.ds(rs, LINES), :].reshape(tiles3)

                v = jnp.where(other, rows_at(wide, 1), rows_at(wide, 0))
                e = jnp.where(other, rows_at(diff, 1), rows_at(diff, 0))
                term = pltpu.roll(v + f * e, lax.rem(LANES - cs, LANES), 2)
                acc = term if acc is None else acc + term
            dst[k, s] = acc.reshape(LINES, LANES)

    def scatter_copy1(src, land, n, d, a):
        return rcopy(src.at[pid(a, turn(w, d, 4))], land.at[d - 1, a], rs_send.at[n, 4 * (d - 1) + a],
                     rs_recv.at[n, 4 * (d - 1) + a], plane_dev(pid(u, turn(w, d, 4))))

    def scatter_copy2(src, dst, n, d):
        a = turn(u, d, 4)
        return rcopy(src.at[a], dst.at[d - 1], rt_send.at[n, d - 1], rt_recv.at[n, d - 1], plane_dev(pid(a, w)))

    def back_scatter(dst, land, n, first):
        @pl.loop(0, PIECES)
        def _(t):
            i = lax.rem(t, 3)
            d = jnp.where(t >= 12, 0, jnp.where(i == 0, 2, 2 * i - 1))
            a = turn(first, jnp.where(t >= 12, t - 12, lax.div(t, 3)), 4)
            back_piece(dst, pid(a, turn(w, d, 4)))

            @pl.when(t < 12)
            def _():
                scatter_copy1(dst, land, n, d, a).start()

    def line_sum(dst, land, n, a):
        total = dst[pid(a, w)]
        for d in (1, 3, 2):
            scatter_copy1(dst, land, n, d, a).wait_recv()
            total = total + land[d - 1, a]
        return total

    def plane_sum(dst, land, total1, land2, n):
        for da in (1, 2, 3, 0):
            a = turn(u, da, 4)
            total1[a] = line_sum(dst, land, n, a)
            if da:
                scatter_copy2(total1, land2, n, da).start()
        total = total1[u]
        for d in (1, 3, 2):
            scatter_copy2(total1, land2, n, d).wait_recv()
            total = total + land2[d - 1]
        return total

    def owner_copy(a, total1, land):
        return rcopy(total1.at[a], land.at[u], own_send.at[a], own_recv.at[u], owner_dev(*xy(a, w)))

    def owner_start(dst, land1, total1, land, n):
        for a in range(4):
            total1[a] = line_sum(dst, land1, n, a)
            copy = owner_copy(a, total1, land)
            local = pltpu.make_async_copy(total1.at[a], land.at[u], own_recv.at[u])
            apart(owner_dev(*xy(a, w)), lambda: copy.start(), lambda: local.start())

    def owner_sum(total1, land):
        total = None
        for a in range(4):
            rcopy(total1.at[0], land.at[a], own_send.at[0], own_recv.at[a], partner).wait_recv()
            total = land[a] if total is None else total + land[a]
        return total

    def owner_finish(total1, land):
        for a in range(4):
            copy = owner_copy(a, total1, land)
            pl.when(jnp.logical_not(is_me(owner_dev(*xy(a, w)))))(lambda: copy.wait_send())

    def slab_at(buf, h, block):
        return buf.at[pl.ds(3 * h, SLICES), :, pl.ds(pl.multiple_of(LANES * block, LANES), LANES)]

    def slab_piece(buf, xx, yy, lo):
        return slab_at(buf, lax.rem(yy, 2), 4 * xx + 2 * lo + lax.div(yy, 2))

    def slab_copy(buf, n, a, b, lo, slot, dev):
        xx, yy = xy(a, b)
        ref = slab_piece(buf, xx, yy, lo)
        return rcopy(ref, ref, sl_send.at[n, slot], sl_recv.at[n, 2 * (4 * xx + yy) + lo], dev)

    def second_dev(d):
        return plane_dev(pid(u, turn(w, d, 4)))

    def slab_wait(buf, n, a, b, lo):
        slab_copy(buf, n, a, b, lo, 0, partner).wait_recv()

    def swap_copy(src, buf, n):
        return rcopy(src, slab_at(buf, ylo, c), sl_send.at[n, 31],
                     sl_recv.at[n, 2 * (4 * zhi + 2 * core + ylo) + zlo], owner_dev(px, py))

    def swap_start(src, buf, n):
        local = pltpu.make_async_copy(src, slab_at(buf, ylo, c), sl_recv.at[n, 2 * (4 * zhi + 2 * core + ylo) + zlo])
        apart(owner_dev(px, py), lambda: swap_copy(src, buf, n).start(), lambda: local.start())

    def slab_near(buf, n, a, lo, slot):
        slab_copy(buf, n, a, w, lo, slot, second_dev(1)).start()
        slab_copy(buf, n, a, w, lo, slot + 1, second_dev(3)).start()

    def slab_first(buf, n):
        for i, d in enumerate((2, 1, 3)):
            slab_copy(buf, n, u, w, zlo, i, plane_dev(pid(turn(u, d, 4), w))).start()
        slab_near(buf, n, u, zlo, 7)
        for i, d in enumerate((2, 1, 3, 0)):
            slab_copy(buf, n, u, w, zlo, 3 + i, (2 * pid(turn(u, d, 4), w) + 1 - zlo, slab)).start()

    def slab_second(buf, n):
        for i, d in enumerate((1, 3, 2)):
            a = turn(u, d, 4)
            slab_wait(buf, n, a, w, zlo)
            slab_near(buf, n, a, zlo, 9 + 2 * i)
        for i, d in enumerate((0, 1, 3, 2)):
            a = turn(u, d, 4)
            slab_wait(buf, n, a, w, 1 - zlo)
            slab_near(buf, n, a, 1 - zlo, 15 + 2 * i)

    def slab_third(buf, n):
        for i, d in enumerate((0, 1, 3, 2)):
            a = turn(u, d, 4)
            slab_wait(buf, n, a, turn(w, 3, 4), 0)
            slab_copy(buf, n, a, turn(w, 3, 4), 0, 23 + 2 * i, second_dev(1)).start()
            slab_wait(buf, n, a, turn(w, 1, 4), 1)
            slab_copy(buf, n, a, turn(w, 1, 4), 1, 24 + 2 * i, second_dev(3)).start()

    def slab_rest(buf, n):
        for lo in range(2):
            for d in (3 if lo else 1, 2):
                @pl.loop(0, 4)
                def _(a):
                    slab_wait(buf, n, a, turn(w, d, 4), lo)

    def slab_finish(buf, n):
        @pl.loop(0, 31)
        def _(t):
            slab_copy(buf, n, u, w, zlo, t, partner).wait_send()

    def blk_copy(src, dst, n, d):
        k = turn(c, d, PIECES)
        return rcopy(src.at[k], dst.at[:, :, pl.ds(pl.multiple_of(LANES * c, LANES), LANES)], blk_send.at[n, d],
                     blk_recv.at[n, c], col_dev(k))

    def blk_send_all(src, dst, n):
        @pl.loop(1, PIECES)
        def _(d):
            blk_copy(src, dst, n, d).start()

        dst[:, :, pl.ds(pl.multiple_of(LANES * c, LANES), LANES)] = src[c]

    def blk_finish(src, dst, n):
        @pl.loop(1, PIECES)
        def _(d):
            k = turn(c, d, PIECES)
            rcopy(src.at[0], dst.at[:, :, pl.ds(pl.multiple_of(LANES * k, LANES), LANES)], blk_send.at[n, d],
                  blk_recv.at[n, k], partner).wait_recv()
            blk_copy(src, dst, n, d).wait_send()

    def gather_finish(buf, halo, n):
        if n:
            for d in range(1, 4):
                rcopy(buf.at[0], buf.at[0], ag_send.at[n, d - 1], ag_recv.at[n, 0], partner).wait_send()
        for da in range(4):
            for d in (1, 2, 3):
                gather_copy2(buf, n, da, d).wait_send()

        @pl.loop(0, PIECES)
        def _(t):
            for side in range(2):
                halo_copy(buf, halo, n, t, side).wait_send()

    def scatter_finish(src, land1, n):
        @pl.loop(0, 12)
        def _(t):
            rcopy(src.at[0], land1.at[0, 0], rs_send.at[n, t], rs_recv.at[n, 0], partner).wait_send()

    def smem_copy(n):
        return pltpu.make_async_copy(tables[n][1], tables[n][2], loc_sem.at[4 + n])

    for n in range(3):
        table_copy(n).wait()
        tabs[n].wait()
        smem_copy(n).start()
    for n in range(3):
        smem_copy(n).wait()

    def place_measured():
        @pl.loop(1, PIECES)
        def _(d):
            k = turn(c, d, PIECES)
            rcopy(msh.at[0], mbuf.at[k], m_send.at[d], m_recv.at[k], partner).wait_recv()

        for k in range(PIECES):
            rows = pl.ds(6 * (2 * (k // 4) + k % 2), 6)
            for e in range(2):
                for t in range(2):
                    wide[2 * ((k // 2) % 2) + e, t, rows, :] = mbuf[k, e, :, LANES * t:LANES * (t + 1)]

    def rows_of(blk):
        for k in range(PIECES):
            rows = pl.ds(6 * (2 * (k // 4) + k % 2), 6)
            for e in range(2):
                blk[k, e] = wide[2 * ((k // 2) % 2) + e, 0, rows, :]

    gather_project(xbuf, xhalo, 0, place_measured)
    for a in range(ANGLES):
        wide[a, 0] = wide[a, 0] - img[a, 0]
        wide[a, 1] = halo_mask(wide[a, 1] - img[a, 1])
    make_diff()

    back_scatter(part, rs1, 0, turn(u, 1, 4))
    rows_of(rblk)
    blk_send_all(rblk, rres, 0)
    own[...] = plane_sum(part, rs1, sum1, rs2, 0)
    gbuf[p] = own[...]
    gather_send1(gbuf, 1)
    swap_start(own, gslab, 0)
    img[...] = jnp.zeros_like(img)
    gather_project(gbuf, ghalo, 1, None)
    slab_wait(gslab, 0, u, w, zlo)
    slab_first(gslab, 0)

    norm = jnp.zeros((ROWS, LANES), F32)
    for a in range(ANGLES):
        mine = img[a, 0]
        wide[a, 0] = mine
        wide[a, 1] = halo_mask(img[a, 1])
        norm = norm + mine * mine
    make_diff()
    back_scatter(qpart, qrs1, 1, 0)

    tiles[...] = jnp.zeros_like(tiles)

    def down(v):
        return jnp.sum(v, axis=0, keepdims=True)

    def sum_copy(set_, n, d):
        at, dev, land = (
            (c, col_dev(turn(c, d, PIECES)), sc1),
            (px, plane_dev(4 * turn(px, d, 4) + py), sc2),
            (py, plane_dev(4 * px + turn(py, d, 4)), sc3),
        )[n]
        return rcopy(tiles.at[set_, n], land.at[set_, at], sc_send.at[set_, n, d], sc_recv.at[set_, n, at], dev)

    def sum_start(set_, n):
        @pl.loop(1, PIECES if n == 0 else 4)
        def _(d):
            sum_copy(set_, n, d).start()

        (sc1, sc2, sc3)[n][set_, (c, px, py)[n]] = tiles[set_, n]

    def sum_finish(set_, n):
        count = PIECES if n == 0 else 4
        land = (sc1, sc2, sc3)[n]

        @pl.loop(1, count)
        def _(d):
            k = turn((c, px, py)[n], d, count)
            rcopy(tiles.at[set_, n], land.at[set_, k], sc_send.at[set_, n, d], sc_recv.at[set_, n, k], partner).wait_recv()
            sum_copy(set_, n, d).wait_send()

        total = land[set_, 0]
        for k in range(1, count):
            total = total + land[set_, k]
        return total

    def sum_step(set_, n):
        tiles[set_, n + 1] = sum_finish(set_, n)
        sum_start(set_, n + 1)

    g = gbuf[p]
    tiles[0, 0, 0:1, :] = down(jnp.sum(g * g, axis=0))
    tiles[0, 0, 1:2, :] = down(norm)
    sum_start(0, 0)
    slab_second(gslab, 0)
    owner_start(qpart, qrs1, qsum1, qland, 1)
    sum_step(0, 0)
    rows_of(iblk)

    @pl.loop(1, PIECES)
    def _(d):
        m_copy(d).wait_send()

    gather_finish(xbuf, xhalo, 0)
    gather_finish(gbuf, ghalo, 1)
    scatter_finish(part, rs1, 0)
    for d in range(1, 4):
        scatter_copy2(sum1, rs2, 0, d).wait_send()
    x_each(lambda copy: copy.wait_send(), lambda copy: None)
    q = owner_sum(qsum1, qland)
    qslab[pl.ds(3 * ylo, SLICES), :, pl.ds(pl.multiple_of(LANES * (4 * px + 2 * zlo + yhi), LANES), LANES)] = q
    slab_first(qslab, 1)
    tiles[1, 0, 0:1, :] = down(jnp.sum(q * q, axis=0))
    sum_start(1, 0)
    blk_send_all(iblk, ires, 1)
    sum_step(0, 1)
    slab_third(gslab, 0)
    slab_second(qslab, 1)
    sum_step(1, 0)
    scatter_finish(qpart, qrs1, 1)
    owner_finish(qsum1, qland)
    sums = jnp.sum(sum_finish(0, 2), axis=1, keepdims=True)
    gamma = sums[0:1]
    alpha = gamma / sums[1:2]
    slab_third(qslab, 1)
    sum_step(1, 1)

    blk_finish(rblk, rres, 0)
    blk_finish(iblk, ires, 1)
    for e in range(2):
        res_out[:, e, :] = rres[e] - alpha * ires[e]

    def out_copy(src, dst, n, i):
        return pltpu.make_async_copy(src.at[i], dst.at[i], out_sem.at[n, i])

    slab_rest(gslab, 0)
    for i in range(6):
        volv[i] = xv[i] + alpha * gslab[i]
        out_copy(volv, vol_out, 0, i).start()
    scale = alpha * alpha * (jnp.sum(sum_finish(1, 2), axis=1, keepdims=True)[0:1] / gamma)
    slab_rest(qslab, 1)
    for i in range(6):
        dirv[i] = scale * gslab[i] - alpha * qslab[i]
        out_copy(dirv, dir_out, 1, i).start()

    slab_finish(gslab, 0)
    slab_finish(qslab, 1)
    pl.when(jnp.logical_not(is_me(owner_dev(px, py))))(lambda: swap_copy(own, gslab, 0).wait_send())
    for i in range(6):
        out_copy(volv, vol_out, 0, i).wait()
        out_copy(dirv, dir_out, 1, i).wait()


def per_device(start_volume, measured, row_shift, col_shift, col_frac):
    piece = (SLICES, LINES, LANES)
    vmem = pltpu.VMEM
    dma = pltpu.SemaphoreType.DMA
    scratch = [
        vmem(start_volume.shape, F32), vmem(start_volume.shape, F32), vmem(start_volume.shape, F32),
        vmem(start_volume.shape, F32), vmem(start_volume.shape, F32),
        vmem((6, 2, X), F32),
        vmem((PIECES, 2, 6, 2 * LANES), F32),
        vmem((PIECES, 2, 6, 2 * LANES), F32),
        vmem((2, 2, 48), jnp.int32), vmem((2, 2, 48), jnp.int32), vmem((2, 2, 48), F32),
        pltpu.SMEM((2, 2, 48), jnp.int32), pltpu.SMEM((2, 2, 48), jnp.int32), pltpu.SMEM((2, 2, 48), F32),
        vmem((PIECES,) + piece, F32), vmem((PIECES, 2) + piece, F32),
        vmem((PIECES,) + piece, F32), vmem((PIECES, 2) + piece, F32),
        vmem((ANGLES * SLICES, 2, 3 * LINES, LANES), F32),
        vmem((ANGLES, 2, ROWS, LANES), F32),
        vmem((ANGLES, 2, ROWS, LANES), F32),
        vmem((ANGLES, 2, ROWS, LANES), F32),
        vmem((PIECES,) + piece, F32), vmem((3, 4) + piece, F32), vmem((4,) + piece, F32), vmem((3,) + piece, F32), vmem(piece, F32),
        vmem((PIECES,) + piece, F32), vmem((3, 4) + piece, F32), vmem((4,) + piece, F32), vmem((4,) + piece, F32),
        vmem((PIECES, 2, 6, LANES), F32), vmem((PIECES, 2, 6, LANES), F32),
        vmem(measured.shape, F32), vmem(measured.shape, F32),
        vmem((2, 3, 8, LANES), F32), vmem((2, PIECES, 8, LANES), F32), vmem((2, 4, 8, LANES), F32), vmem((2, 4, 8, LANES), F32),
        dma((8,)), dma((3,)), dma((3,)), dma((PIECES,)), dma((PIECES,)), dma((4, 3)),
        dma((2, 15)), dma((2, PIECES)), dma((2, 2, PIECES)), dma((2, 2, PIECES)),
        dma((2, 12)), dma((2, 12)), dma((1, 3)), dma((1, 3)), dma((4,)), dma((4,)),
        dma((2, 32)), dma((2, 32)), dma((2, PIECES)), dma((2, PIECES)), dma((2, 3, PIECES)), dma((2, 3, PIECES)), dma((2, 6)),
    ]
    whole = pl.BlockSpec(memory_space=pltpu.VMEM)
    far = pl.BlockSpec(memory_space=pltpu.HBM)
    rows = jnp.transpose(measured, (1, 0, 2))
    volume, residual, direction = pl.pallas_call(
        kernel,
        out_shape=(
            jax.ShapeDtypeStruct(start_volume.shape, F32),
            jax.ShapeDtypeStruct(rows.shape, F32),
            jax.ShapeDtypeStruct(start_volume.shape, F32),
        ),
        in_specs=[far] * 5,
        out_specs=(far, whole, far),
        scratch_shapes=scratch,
        compiler_params=pltpu.CompilerParams(
            collective_id=0, has_side_effects=True, vmem_limit_bytes=60 * 2**20
        ),
    )(start_volume, rows, row_shift, col_shift, col_frac)
    return volume, jnp.transpose(residual, (1, 0, 2)), direction


def solution(mesh):
    return jax.shard_map(
        per_device,
        mesh=mesh,
        in_specs=(
            P("slab", None, None),
            P("ang", "slab", None),
            P("ang", None),
            P("ang", None),
            P("ang", None),
        ),
        out_specs=(P("slab", None, None), P("ang", "slab", None), P("slab", None, None)),
        check_vma=False,
    )
```

```python
import jax
import jax.numpy as jnp
from jax import lax
from jax.experimental import pallas as pl
from jax.experimental.pallas import tpu as pltpu
from jax.sharding import PartitionSpec as P

MESH = pl.DeviceIdType.MESH
F32 = jnp.float32
PIECES = 16
SLICES = 3
LINES = 24
ROWS = 48
ANGLES = 4
LANES = 128
X = 2048


def rcopy(src, dst, send, recv, dev):
    return pltpu.make_async_remote_copy(
        src_ref=src, dst_ref=dst, send_sem=send, recv_sem=recv, device_id=dev, device_id_type=MESH
    )


def lanes_of(shape):
    return lax.broadcasted_iota(jnp.int32, shape, len(shape) - 1)


def kernel(
    x_hbm, m_hbm, rt_ref, ct_ref, ft_ref,
    vol_out, res_out, dir_out,
    xv, volv, dirv, gslab, qslab, m_ref, msh, mbuf, rtv, ctv, ftv, rts, cts, fts,
    xbuf, xhalo, gbuf, ghalo, pad, img, wide, diff,
    part, rs1, sum1, rs2, own, qpart, qrs1, qsum1, qland,
    rblk, iblk, rres, ires, tiles, sc1, sc2, sc3,
    loc_sem, tab_send, tab_recv, m_send, m_recv, x_send,
    ag_send, ag_recv, hl_send, hl_recv,
    rs_send, rs_recv, rt_send, rt_recv, own_send, own_recv,
    sl_send, sl_recv, blk_send, blk_recv, sc_send, sc_recv, out_sem,
):
    ang = lax.axis_index("ang")
    slab = lax.axis_index("slab")
    p = lax.div(ang, 2)
    zlo = lax.rem(ang, 2)
    px = lax.div(p, 4)
    py = lax.rem(p, 4)
    zhi = lax.div(slab, 2)
    core = lax.rem(slab, 2)
    z = 2 * zhi + zlo
    c = 2 * z + core
    even = core == 0
    u = jnp.where(even, px, py)
    w = jnp.where(even, py, px)

    def pid(a, b):
        return jnp.where(even, 4 * a + b, 4 * b + a)

    def plane_dev(q):
        return (2 * q + zlo, slab)

    def col_dev(k):
        zz = lax.div(k, 2)
        return (2 * p + lax.rem(zz, 2), 2 * lax.div(zz, 2) + lax.rem(k, 2))

    def turn(v, d, n):
        return lax.rem(v + d, n)

    lane = lanes_of((8, LANES))
    exist = jnp.where(lane < 64, jnp.where(c < PIECES - 1, 1, 0), jnp.where(c > 0, 1, 0)) > 0
    me_dev = (ang, slab)

    def xy(a, b):
        return jnp.where(even, a, b), jnp.where(even, b, a)

    def is_me(dev):
        return jnp.logical_and(dev[0] == ang, dev[1] == slab)

    def apart(dev, then, here):
        pl.when(jnp.logical_not(is_me(dev)))(then)
        pl.when(is_me(dev))(here)

    def owner_dev(xx, yy):
        return (2 * (4 * zhi + 2 * core + lax.rem(yy, 2)) + zlo, 2 * xx + lax.div(yy, 2))

    partner = (2 * p + (1 - zlo), slab)
    yhi = lax.div(py, 2)
    ylo = lax.rem(py, 2)

    mload = pltpu.make_async_copy(m_hbm, m_ref, loc_sem.at[0])
    mload.start()
    tables = ((rt_ref, rtv, rts), (ct_ref, ctv, cts), (ft_ref, ftv, fts))

    def table_copy(n):
        return pltpu.make_async_copy(tables[n][0], tables[n][1].at[zlo], loc_sem.at[4 + n])

    for n in range(3):
        table_copy(n).start()
    xload = pltpu.make_async_copy(x_hbm, xv, loc_sem.at[1])
    xload.start()

    barrier = pltpu.get_barrier_semaphore()

    def greet(dev):
        pl.semaphore_signal(barrier, inc=1, device_id=dev, device_id_type=MESH)

    @pl.loop(1, PIECES)
    def _(d):
        greet(col_dev(turn(c, d, PIECES)))

    for d in range(1, 4):
        greet(plane_dev(pid(turn(u, d, 4), w)))
        greet(plane_dev(pid(u, turn(w, d, 4))))
    for a in range(4):
        greet((2 * pid(a, w) + 1 - zlo, slab))
    mine = 0
    for a in range(4):
        to = owner_dev(*xy(a, w))
        pl.when(jnp.logical_not(is_me(to)))(lambda to=to: greet(to))
        mine = mine + jnp.where(is_me(to), 1, 0)
        at_x, at_y = zhi, 2 * core + ylo
        come = (2 * jnp.where(yhi == 0, 4 * a + at_y, 4 * at_x + a) + zlo, 2 * px + yhi)
        pl.when(jnp.logical_not(is_me(come)))(lambda come=come: greet(come))

    lane6 = lanes_of((6, LANES))
    mload.wait()
    for a in range(2):
        for t in range(PIECES):
            here = m_ref[:, a, pl.ds(LANES * t, LANES)]
            right = m_ref[:, a, pl.ds(LANES * min(t + 1, 15), LANES)]
            left = m_ref[:, a, pl.ds(LANES * max(t - 1, 0), LANES)]
            msh[t, a, :, :LANES] = here
            msh[t, a, :, LANES:] = jnp.where(lane6 < 64, right, left)

    pad[...] = jnp.zeros_like(pad)
    img[...] = jnp.zeros_like(img)
    xload.wait()
    pl.semaphore_wait(barrier, 15 + 6 + 4 + 8 - 2 * mine)

    near = turn(zhi, 3 + 2 * zlo, 4)
    served = ((zhi, zlo), (near, 0), (near, 1), (turn(zhi, 2, 4), 1 - zlo))

    def x_each(act_far, act_here):
        for to, (to_hi, to_lo) in enumerate(served):
            for h in range(3):
                cc = 4 * to_hi + 2 * to_lo + (1 if h < 2 else 0)
                half = h if h < 2 else ylo
                k = 4 * zhi + 2 * core + half
                src = xv.at[pl.ds(3 * half, SLICES), :, pl.ds(pl.multiple_of(LANES * cc, LANES), LANES)]
                copy = rcopy(src, xbuf.at[k], x_send.at[to, h], ag_recv.at[0, k], col_dev(cc))
                local = pltpu.make_async_copy(src, xbuf.at[k], ag_recv.at[0, k])

                def act(copy=copy, local=local, cc=cc):
                    apart(col_dev(cc), lambda: act_far(copy), lambda: act_here(local))

                pl.when(zhi == px if h < 2 else core == yhi)(act)

    x_each(lambda copy: copy.start(), lambda copy: copy.start())

    tabs = []
    for n, (src, dst, _) in enumerate(tables):
        t = rcopy(src, dst.at[zlo], tab_send.at[n], tab_recv.at[n], partner)
        t.start()
        tabs.append(t)

    def m_copy(d):
        k = turn(c, d, PIECES)
        return rcopy(msh.at[k], mbuf.at[c], m_send.at[d], m_recv.at[c], col_dev(k))

    def m_start():
        @pl.loop(1, PIECES)
        def _(d):
            m_copy(d).start()

    mbuf[c] = msh[c]

    def step(q):
        return jnp.where(q < 2, q, 5 - q)

    def piece_order(t):
        late = t - 9
        dx = jnp.where(t < 9, step(lax.rem(t, 3)), jnp.where(late < 4, 2, step(late - 4)))
        dy = jnp.where(t < 9, step(lax.div(t, 3)), jnp.where(late < 4, step(late), 2))
        return 4 * turn(px, 4 - dx, 4) + turn(py, 4 - dy, 4)

    def gather_send1(buf, n):
        for d in range(1, 4):
            rcopy(buf.at[p], buf.at[p], ag_send.at[n, d - 1], ag_recv.at[n, p],
                  plane_dev(pid(turn(u, d, 4), w))).start()

    def gather_copy2(buf, n, da, d):
        k = pid(turn(u, 4 - da, 4), w)
        return rcopy(buf.at[k], buf.at[k], ag_send.at[n, 3 + 3 * da + d - 1], ag_recv.at[n, k],
                     plane_dev(pid(u, turn(w, d, 4))))

    def halo_copy(buf, halo, n, k, side):
        to = turn(c, 1 if side == 0 else PIECES - 1, PIECES)
        return rcopy(buf.at[k], halo.at[k, side], hl_send.at[n, side, k], hl_recv.at[n, side, k], col_dev(to))

    def halo_start(buf, halo, n, k):
        for side in range(2):
            halo_copy(buf, halo, n, k, side).start()

    def gather_wait(buf, n, k):
        rcopy(buf.at[k], buf.at[k], ag_send.at[n, 0], ag_recv.at[n, k], partner).wait_recv()

    tiles3 = (SLICES, 8, LANES)

    def project_piece(buf, halo, k):
        for s in range(SLICES):
            w0 = buf[k, s].reshape(tiles3)
            left = halo[k, 0, s].reshape(tiles3)
            right = halo[k, 1, s].reshape(tiles3)
            w1 = jnp.where(exist, jnp.where(lane < 64, right, left), 0.0)
            s0 = pltpu.roll(w0, 1, 2)
            s1 = pltpu.roll(w1, 1, 2)
            d0 = jnp.where(lane < 1, s1, s0) - w0
            d1 = jnp.where(lane < 1, s0, s1) - w1
            at = SLICES * k + s
            for a in range(ANGLES):
                f = fts[a // 2, a % 2, at]
                cs = cts[a // 2, a % 2, at]
                v0 = w0 + f * d0
                v1 = w1 + f * d1
                other = jnp.logical_or(lane >= LANES - cs, lane < -cs)
                sh = lax.rem(cs + LANES, LANES)
                full = (LINES, LANES)
                pad[SLICES * a + s, 0, pl.ds(LINES, LINES), :] = pltpu.roll(jnp.where(other, v1, v0), sh, 2).reshape(full)
                pad[SLICES * a + s, 1, pl.ds(LINES, LINES), :] = pltpu.roll(jnp.where(other, v0, v1), sh, 2).reshape(full)
        for a in range(ANGLES):
            for t in range(2):
                acc = img[a, t]
                for s in range(SLICES):
                    rs = rts[a // 2, a % 2, SLICES * k + s]
                    acc = acc + pad[SLICES * a + s, t, pl.ds(LINES - rs, ROWS), :]
                img[a, t] = acc

    def gather_project(buf, halo, n, during):
        for da in (0, 1, 3, 2):
            k = pid(turn(u, 4 - da, 4), w)
            if n == 0 or da:
                gather_wait(buf, n, k)
            for d in (1, 3, 2):
                gather_copy2(buf, n, da, d).start()
            halo_start(buf, halo, n, k)

        @pl.loop(0, 8)
        def _(t):
            k = pid(turn(u, 4 - step(lax.div(t, 2)), 4), turn(w, 3 - 2 * lax.rem(t, 2), 4))
            gather_wait(buf, n, k)
            halo_start(buf, halo, n, k)

        if n == 0:
            m_start()

        @pl.loop(0, PIECES)
        def _(t):
            if during is not None:
                pl.when(t == 10)(during)

            @pl.when(jnp.logical_and(t >= 4, t < 8))
            def _():
                k = pid(turn(u, 4 - step(t - 4), 4), turn(w, 2, 4))
                gather_wait(buf, n, k)
                halo_start(buf, halo, n, k)

            k = piece_order(t)
            for side in range(2):
                halo_copy(buf, halo, n, k, side).wait_recv()
            project_piece(buf, halo, k)

    def halo_mask(v):
        return jnp.where(exist, v.reshape(ROWS // 8, 8, LANES), 0.0).reshape(ROWS, LANES)

    def make_diff():
        last = lanes_of((ROWS, LANES)) == LANES - 1
        for a in range(ANGLES):
            v0 = wide[a, 0]
            v1 = wide[a, 1]
            s0 = pltpu.roll(v0, LANES - 1, 1)
            s1 = pltpu.roll(v1, LANES - 1, 1)
            diff[a, 0] = jnp.where(last, s1, s0) - v0
            diff[a, 1] = jnp.where(last, s0, s1) - v1

    def back_piece(dst, k):
        for s in range(SLICES):
            at = SLICES * k + s
            acc = None
            for a in range(ANGLES):
                rs = rts[a // 2, a % 2, at]
                cs = cts[a // 2, a % 2, at]
                f = fts[a // 2, a % 2, at]
                other = jnp.logical_or(lane < cs, lane >= LANES + cs)

                def rows_at(ref, t):
                    return ref[a, t, pl.ds(rs, LINES), :].reshape(tiles3)

                v = jnp.where(other, rows_at(wide, 1), rows_at(wide, 0))
                e = jnp.where(other, rows_at(diff, 1), rows_at(diff, 0))
                term = pltpu.roll(v + f * e, lax.rem(LANES - cs, LANES), 2)
                acc = term if acc is None else acc + term
            dst[k, s] = acc.reshape(LINES, LANES)

    def scatter_copy1(src, land, n, d, a):
        return rcopy(src.at[pid(a, turn(w, d, 4))], land.at[d - 1, a], rs_send.at[n, 4 * (d - 1) + a],
                     rs_recv.at[n, 4 * (d - 1) + a], plane_dev(pid(u, turn(w, d, 4))))

    def scatter_copy2(src, dst, n, d):
        a = turn(u, d, 4)
        return rcopy(src.at[a], dst.at[d - 1], rt_send.at[n, d - 1], rt_recv.at[n, d - 1], plane_dev(pid(a, w)))

    def back_scatter(dst, land, n, first):
        @pl.loop(0, PIECES)
        def _(t):
            i = lax.rem(t, 3)
            d = jnp.where(t >= 12, 0, jnp.where(i == 0, 2, 2 * i - 1))
            a = turn(first, jnp.where(t >= 12, t - 12, lax.div(t, 3)), 4)
            back_piece(dst, pid(a, turn(w, d, 4)))

            @pl.when(t < 12)
            def _():
                scatter_copy1(dst, land, n, d, a).start()

    def line_sum(dst, land, n, a):
        total = dst[pid(a, w)]
        for d in (1, 3, 2):
            scatter_copy1(dst, land, n, d, a).wait_recv()
            total = total + land[d - 1, a]
        return total

    def plane_sum(dst, land, total1, land2, n):
        for da in (1, 2, 3, 0):
            a = turn(u, da, 4)
            total1[a] = line_sum(dst, land, n, a)
            if da:
                scatter_copy2(total1, land2, n, da).start()
        total = total1[u]
        for d in (1, 3, 2):
            scatter_copy2(total1, land2, n, d).wait_recv()
            total = total + land2[d - 1]
        return total

    def owner_copy(a, total1, land):
        return rcopy(total1.at[a], land.at[u], own_send.at[a], own_recv.at[u], owner_dev(*xy(a, w)))

    def owner_start(dst, land1, total1, land, n):
        for a in range(4):
            total1[a] = line_sum(dst, land1, n, a)
            copy = owner_copy(a, total1, land)
            local = pltpu.make_async_copy(total1.at[a], land.at[u], own_recv.at[u])
            apart(owner_dev(*xy(a, w)), lambda: copy.start(), lambda: local.start())

    def owner_sum(total1, land):
        total = None
        for a in range(4):
            rcopy(total1.at[0], land.at[a], own_send.at[0], own_recv.at[a], partner).wait_recv()
            total = land[a] if total is None else total + land[a]
        return total

    def owner_finish(total1, land):
        for a in range(4):
            copy = owner_copy(a, total1, land)
            pl.when(jnp.logical_not(is_me(owner_dev(*xy(a, w)))))(lambda: copy.wait_send())

    def slab_at(buf, h, block):
        return buf.at[pl.ds(3 * h, SLICES), :, pl.ds(pl.multiple_of(LANES * block, LANES), LANES)]

    def slab_piece(buf, xx, yy, lo):
        return slab_at(buf, lax.rem(yy, 2), 4 * xx + 2 * lo + lax.div(yy, 2))

    def slab_copy(buf, n, a, b, lo, slot, dev):
        xx, yy = xy(a, b)
        ref = slab_piece(buf, xx, yy, lo)
        return rcopy(ref, ref, sl_send.at[n, slot], sl_recv.at[n, 2 * (4 * xx + yy) + lo], dev)

    def second_dev(d):
        return plane_dev(pid(u, turn(w, d, 4)))

    def slab_wait(buf, n, a, b, lo):
        slab_copy(buf, n, a, b, lo, 0, partner).wait_recv()

    def swap_copy(src, buf, n):
        return rcopy(src, slab_at(buf, ylo, c), sl_send.at[n, 31],
                     sl_recv.at[n, 2 * (4 * zhi + 2 * core + ylo) + zlo], owner_dev(px, py))

    def swap_start(src, buf, n):
        local = pltpu.make_async_copy(src, slab_at(buf, ylo, c), sl_recv.at[n, 2 * (4 * zhi + 2 * core + ylo) + zlo])
        apart(owner_dev(px, py), lambda: swap_copy(src, buf, n).start(), lambda: local.start())

    def slab_near(buf, n, a, lo, slot):
        slab_copy(buf, n, a, w, lo, slot, second_dev(1)).start()
        slab_copy(buf, n, a, w, lo, slot + 1, second_dev(3)).start()

    def slab_first(buf, n):
        for i, d in enumerate((1, 3, 2)):
            slab_copy(buf, n, u, w, zlo, i, plane_dev(pid(turn(u, d, 4), w))).start()
        slab_near(buf, n, u, zlo, 7)
        for i, d in enumerate((0, 1, 3, 2)):
            slab_copy(buf, n, u, w, zlo, 3 + i, (2 * pid(turn(u, d, 4), w) + 1 - zlo, slab)).start()

    def slab_second(buf, n):
        for i, d in enumerate((1, 3, 2)):
            a = turn(u, d, 4)
            slab_wait(buf, n, a, w, zlo)
            slab_near(buf, n, a, zlo, 9 + 2 * i)
        for i, d in enumerate((0, 1, 3, 2)):
            a = turn(u, d, 4)
            slab_wait(buf, n, a, w, 1 - zlo)
            slab_near(buf, n, a, 1 - zlo, 15 + 2 * i)

    def slab_third(buf, n):
        for i, d in enumerate((0, 1, 3, 2)):
            a = turn(u, d, 4)
            slab_wait(buf, n, a, turn(w, 3, 4), 0)
            slab_copy(buf, n, a, turn(w, 3, 4), 0, 23 + 2 * i, second_dev(1)).start()
            slab_wait(buf, n, a, turn(w, 1, 4), 1)
            slab_copy(buf, n, a, turn(w, 1, 4), 1, 24 + 2 * i, second_dev(3)).start()

    def slab_rest(buf, n):
        for lo in range(2):
            for d in (3 if lo else 1, 2):
                @pl.loop(0, 4)
                def _(a):
                    slab_wait(buf, n, a, turn(w, d, 4), lo)

    def slab_finish(buf, n):
        @pl.loop(0, 31)
        def _(t):
            slab_copy(buf, n, u, w, zlo, t, partner).wait_send()

    def blk_copy(src, dst, n, d):
        k = turn(c, d, PIECES)
        return rcopy(src.at[k], dst.at[:, :, pl.ds(pl.multiple_of(LANES * c, LANES), LANES)], blk_send.at[n, d],
                     blk_recv.at[n, c], col_dev(k))

    def blk_send_all(src, dst, n):
        @pl.loop(1, PIECES)
        def _(d):
            blk_copy(src, dst, n, d).start()

        dst[:, :, pl.ds(pl.multiple_of(LANES * c, LANES), LANES)] = src[c]

    def blk_finish(src, dst, n):
        @pl.loop(1, PIECES)
        def _(d):
            k = turn(c, d, PIECES)
            rcopy(src.at[0], dst.at[:, :, pl.ds(pl.multiple_of(LANES * k, LANES), LANES)], blk_send.at[n, d],
                  blk_recv.at[n, k], partner).wait_recv()
            blk_copy(src, dst, n, d).wait_send()

    def gather_finish(buf, halo, n):
        if n:
            for d in range(1, 4):
                rcopy(buf.at[0], buf.at[0], ag_send.at[n, d - 1], ag_recv.at[n, 0], partner).wait_send()
        for da in range(4):
            for d in (1, 2, 3):
                gather_copy2(buf, n, da, d).wait_send()

        @pl.loop(0, PIECES)
        def _(t):
            for side in range(2):
                halo_copy(buf, halo, n, t, side).wait_send()

    def scatter_finish(src, land1, n):
        @pl.loop(0, 12)
        def _(t):
            rcopy(src.at[0], land1.at[0, 0], rs_send.at[n, t], rs_recv.at[n, 0], partner).wait_send()

    def smem_copy(n):
        return pltpu.make_async_copy(tables[n][1], tables[n][2], loc_sem.at[4 + n])

    for n in range(3):
        table_copy(n).wait()
        tabs[n].wait()
        smem_copy(n).start()
    for n in range(3):
        smem_copy(n).wait()

    def place_measured():
        @pl.loop(1, PIECES)
        def _(d):
            k = turn(c, d, PIECES)
            rcopy(msh.at[0], mbuf.at[k], m_send.at[d], m_recv.at[k], partner).wait_recv()

        for k in range(PIECES):
            rows = pl.ds(6 * (2 * (k // 4) + k % 2), 6)
            for e in range(2):
                for t in range(2):
                    wide[2 * ((k // 2) % 2) + e, t, rows, :] = mbuf[k, e, :, LANES * t:LANES * (t + 1)]

    def rows_of(blk):
        for k in range(PIECES):
            rows = pl.ds(6 * (2 * (k // 4) + k % 2), 6)
            for e in range(2):
                blk[k, e] = wide[2 * ((k // 2) % 2) + e, 0, rows, :]

    gather_project(xbuf, xhalo, 0, place_measured)
    for a in range(ANGLES):
        wide[a, 0] = wide[a, 0] - img[a, 0]
        wide[a, 1] = halo_mask(wide[a, 1] - img[a, 1])
    make_diff()

    back_scatter(part, rs1, 0, turn(u, 1, 4))
    rows_of(rblk)
    blk_send_all(rblk, rres, 0)
    own[...] = plane_sum(part, rs1, sum1, rs2, 0)
    gbuf[p] = own[...]
    gather_send1(gbuf, 1)
    swap_start(own, gslab, 0)
    img[...] = jnp.zeros_like(img)
    gather_project(gbuf, ghalo, 1, None)
    slab_wait(gslab, 0, u, w, zlo)
    slab_first(gslab, 0)

    norm = jnp.zeros((ROWS, LANES), F32)
    for a in range(ANGLES):
        mine = img[a, 0]
        wide[a, 0] = mine
        wide[a, 1] = halo_mask(img[a, 1])
        norm = norm + mine * mine
    make_diff()
    back_scatter(qpart, qrs1, 1, 0)

    tiles[...] = jnp.zeros_like(tiles)

    def down(v):
        return jnp.sum(v, axis=0, keepdims=True)

    def sum_copy(set_, n, d):
        at, dev, land = (
            (c, col_dev(turn(c, d, PIECES)), sc1),
            (px, plane_dev(4 * turn(px, d, 4) + py), sc2),
            (py, plane_dev(4 * px + turn(py, d, 4)), sc3),
        )[n]
        return rcopy(tiles.at[set_, n], land.at[set_, at], sc_send.at[set_, n, d], sc_recv.at[set_, n, at], dev)

    def sum_start(set_, n):
        @pl.loop(1, PIECES if n == 0 else 4)
        def _(d):
            sum_copy(set_, n, d).start()

        (sc1, sc2, sc3)[n][set_, (c, px, py)[n]] = tiles[set_, n]

    def sum_finish(set_, n):
        count = PIECES if n == 0 else 4
        land = (sc1, sc2, sc3)[n]

        @pl.loop(1, count)
        def _(d):
            k = turn((c, px, py)[n], d, count)
            rcopy(tiles.at[set_, n], land.at[set_, k], sc_send.at[set_, n, d], sc_recv.at[set_, n, k], partner).wait_recv()
            sum_copy(set_, n, d).wait_send()

        total = land[set_, 0]
        for k in range(1, count):
            total = total + land[set_, k]
        return total

    def sum_step(set_, n):
        tiles[set_, n + 1] = sum_finish(set_, n)
        sum_start(set_, n + 1)

    g = gbuf[p]
    tiles[0, 0, 0:1, :] = down(jnp.sum(g * g, axis=0))
    tiles[0, 0, 1:2, :] = down(norm)
    sum_start(0, 0)
    owner_start(qpart, qrs1, qsum1, qland, 1)
    slab_second(gslab, 0)
    sum_step(0, 0)
    rows_of(iblk)

    @pl.loop(1, PIECES)
    def _(d):
        m_copy(d).wait_send()

    gather_finish(xbuf, xhalo, 0)
    gather_finish(gbuf, ghalo, 1)
    scatter_finish(part, rs1, 0)
    for d in range(1, 4):
        scatter_copy2(sum1, rs2, 0, d).wait_send()
    x_each(lambda copy: copy.wait_send(), lambda copy: None)
    q = owner_sum(qsum1, qland)
    qslab[pl.ds(3 * ylo, SLICES), :, pl.ds(pl.multiple_of(LANES * (4 * px + 2 * zlo + yhi), LANES), LANES)] = q
    slab_first(qslab, 1)
    tiles[1, 0, 0:1, :] = down(jnp.sum(q * q, axis=0))
    sum_start(1, 0)
    blk_send_all(iblk, ires, 1)
    sum_step(0, 1)
    slab_third(gslab, 0)
    slab_second(qslab, 1)
    sum_step(1, 0)
    scatter_finish(qpart, qrs1, 1)
    owner_finish(qsum1, qland)
    sums = jnp.sum(sum_finish(0, 2), axis=1, keepdims=True)
    gamma = sums[0:1]
    alpha = gamma / sums[1:2]
    slab_third(qslab, 1)
    sum_step(1, 1)

    blk_finish(rblk, rres, 0)
    blk_finish(iblk, ires, 1)
    for e in range(2):
        res_out[:, e, :] = rres[e] - alpha * ires[e]

    def out_copy(src, dst, n, i):
        return pltpu.make_async_copy(src.at[i], dst.at[i], out_sem.at[n, i])

    slab_rest(gslab, 0)
    for i in range(6):
        volv[i] = xv[i] + alpha * gslab[i]
        out_copy(volv, vol_out, 0, i).start()
    scale = alpha * alpha * (jnp.sum(sum_finish(1, 2), axis=1, keepdims=True)[0:1] / gamma)
    slab_rest(qslab, 1)
    for i in range(6):
        dirv[i] = scale * gslab[i] - alpha * qslab[i]
        out_copy(dirv, dir_out, 1, i).start()

    slab_finish(gslab, 0)
    slab_finish(qslab, 1)
    pl.when(jnp.logical_not(is_me(owner_dev(px, py))))(lambda: swap_copy(own, gslab, 0).wait_send())
    for i in range(6):
        out_copy(volv, vol_out, 0, i).wait()
        out_copy(dirv, dir_out, 1, i).wait()


def per_device(start_volume, measured, row_shift, col_shift, col_frac):
    piece = (SLICES, LINES, LANES)
    vmem = pltpu.VMEM
    dma = pltpu.SemaphoreType.DMA
    scratch = [
        vmem(start_volume.shape, F32), vmem(start_volume.shape, F32), vmem(start_volume.shape, F32),
        vmem(start_volume.shape, F32), vmem(start_volume.shape, F32),
        vmem((6, 2, X), F32),
        vmem((PIECES, 2, 6, 2 * LANES), F32),
        vmem((PIECES, 2, 6, 2 * LANES), F32),
        vmem((2, 2, 48), jnp.int32), vmem((2, 2, 48), jnp.int32), vmem((2, 2, 48), F32),
        pltpu.SMEM((2, 2, 48), jnp.int32), pltpu.SMEM((2, 2, 48), jnp.int32), pltpu.SMEM((2, 2, 48), F32),
        vmem((PIECES,) + piece, F32), vmem((PIECES, 2) + piece, F32),
        vmem((PIECES,) + piece, F32), vmem((PIECES, 2) + piece, F32),
        vmem((ANGLES * SLICES, 2, 3 * LINES, LANES), F32),
        vmem((ANGLES, 2, ROWS, LANES), F32),
        vmem((ANGLES, 2, ROWS, LANES), F32),
        vmem((ANGLES, 2, ROWS, LANES), F32),
        vmem((PIECES,) + piece, F32), vmem((3, 4) + piece, F32), vmem((4,) + piece, F32), vmem((3,) + piece, F32), vmem(piece, F32),
        vmem((PIECES,) + piece, F32), vmem((3, 4) + piece, F32), vmem((4,) + piece, F32), vmem((4,) + piece, F32),
        vmem((PIECES, 2, 6, LANES), F32), vmem((PIECES, 2, 6, LANES), F32),
        vmem(measured.shape, F32), vmem(measured.shape, F32),
        vmem((2, 3, 8, LANES), F32), vmem((2, PIECES, 8, LANES), F32), vmem((2, 4, 8, LANES), F32), vmem((2, 4, 8, LANES), F32),
        dma((8,)), dma((3,)), dma((3,)), dma((PIECES,)), dma((PIECES,)), dma((4, 3)),
        dma((2, 15)), dma((2, PIECES)), dma((2, 2, PIECES)), dma((2, 2, PIECES)),
        dma((2, 12)), dma((2, 12)), dma((1, 3)), dma((1, 3)), dma((4,)), dma((4,)),
        dma((2, 32)), dma((2, 32)), dma((2, PIECES)), dma((2, PIECES)), dma((2, 3, PIECES)), dma((2, 3, PIECES)), dma((2, 6)),
    ]
    whole = pl.BlockSpec(memory_space=pltpu.VMEM)
    far = pl.BlockSpec(memory_space=pltpu.HBM)
    rows = jnp.transpose(measured, (1, 0, 2))
    volume, residual, direction = pl.pallas_call(
        kernel,
        out_shape=(
            jax.ShapeDtypeStruct(start_volume.shape, F32),
            jax.ShapeDtypeStruct(rows.shape, F32),
            jax.ShapeDtypeStruct(start_volume.shape, F32),
        ),
        in_specs=[far] * 5,
        out_specs=(far, whole, far),
        scratch_shapes=scratch,
        compiler_params=pltpu.CompilerParams(
            collective_id=0, has_side_effects=True, vmem_limit_bytes=60 * 2**20
        ),
    )(start_volume, rows, row_shift, col_shift, col_frac)
    return volume, jnp.transpose(residual, (1, 0, 2)), direction


def solution(mesh):
    return jax.shard_map(
        per_device,
        mesh=mesh,
        in_specs=(
            P("slab", None, None),
            P("ang", "slab", None),
            P("ang", None),
            P("ang", None),
            P("ang", None),
        ),
        out_specs=(P("slab", None, None), P("ang", "slab", None), P("slab", None, None)),
        check_vma=False,
    )
```
